32 devices in a mesh: groups: 2 (over y), rows: 4 (over z), cols: 4 (over x, core).
Axes of the slice: x: 2, y: 2, z: 4, core: 2. Of those that a mesh axis runs over, the one named last changes fastest.
Arguments:
- doubles: bfloat16 [1024, 4096], P(('groups', 'rows'), 'cols'), parts along dimension 0, may hold values from -6 to 6
- doubles_kept: int32 [8, 32], P('groups', 'cols'), parts along dimension 0, may hold values from 0 to 1, as said below
- integrals: bfloat16 [8192, 1024], P(('groups', 'cols'), 'rows'), parts along dimension 0, may hold values from -0.1875 to 0.1875
- integral_kept: int32 [64, 8], P(('groups', 'cols'), 'rows'), parts along dimension 0, may hold values 0 or 1
- residual: float32 [1024, 1024], P(('groups', 'cols'), 'rows'), parts along dimension 0, may hold values from -6 to 6
Outputs:
- updated: float32 [1024, 1024], P(('groups', 'cols'), 'rows'), parts along dimension 0
The draws below stay inside these ranges and needn't reach their ends.
There are 2 independent parts, one for each index of `groups`. The reference program is written for one: setup_inputs(seed, part) draws one part's arguments, and reference() takes and returns one part's arrays. A program takes and returns all parts, laid end to end along the dimension named above; each array names one. Nothing has to cross between parts.
Inputs may be any that keep to these rules, and one draw needn't show every extreme that they name: `doubles_kept`: in each row, each aligned group of 8 contracted tiles holds exactly 4 ones.
All inputs are finite; a program needn't handle non-finite values. No bound on the sum of `integral_kept` on one device may be relied on, other than what follows from the above.
Results may differ from the reference program's by a relative error of at most 0.0003.
Values may be sent and summed in bfloat16 or wider, within the bound.
No kernel may reach another device: no remote copies, remote signals or barrier semaphores. Data moves between devices by JAX's collectives and lax.ppermute only.
A program may use at most 64 MiB of HBM per device.

```python
import jax
import jax.numpy as jnp

TILE = 128
CT_DEV = 8
KEEP = 4
PAIR_DEV = 128
PBLK = 4
PAIRS = 512
CT = 32
CD = 4096
AT = 8
AB = 1024


def draw_doubles_kept(key, part):
    key = jax.random.fold_in(key, 11)
    scores = jax.random.randint(key, (PBLK, CT // CT_DEV, CT_DEV), 0, 1 << 20)
    scores = scores * CT_DEV + jnp.arange(CT_DEV, dtype=jnp.int32)
    ranks = jnp.argsort(jnp.argsort(scores, axis=-1), axis=-1)
    return (ranks < KEEP).astype(jnp.int32).reshape(PBLK, CT)


def touch_ends(drawn, key, low, high):
    longest = drawn.shape.index(max(drawn.shape))
    spots = []
    for shift in (0, 1):
        where = [jax.random.randint(jax.random.fold_in(key, axis), (), 0, length) for axis, length in enumerate(drawn.shape)]
        where[longest] = (where[longest] + shift) % drawn.shape[longest]
        spots.append(tuple(where))
    return drawn.at[spots[0]].set(low).at[spots[1]].set(high)


def block_scale(own_key, shape, shards, low, largest):
    loudness = 1.0
    for dim, parts in shards:
        steps = jax.random.uniform(jax.random.fold_in(jax.random.fold_in(own_key, 6), dim), (parts,), jnp.float32, low / len(shards), largest / len(shards))
        loudness = loudness * jnp.repeat(jnp.exp(steps), shape[dim] // parts).reshape((-1,) + (1,) * (len(shape) - 1 - dim))
    return loudness


def noise(rng, shape, deviation, bound, cuts=(), held_as=jnp.bfloat16):
    result = jax.random.normal(rng, shape, jnp.float32) * deviation
    if len(cuts) > 0:
        result = block_scale(rng, shape, cuts, -0.22, 0.18) * result
    return jnp.clip(result, min=-bound, max=bound).astype(held_as)


def setup_inputs(seed: int = 0, part: int = 0) -> dict:
    arg_keys = jax.random.split(jax.random.key(seed), 6)
    part_splits = jax.random.split(jax.random.fold_in(arg_keys[5], part), 6)
    doubles = noise(part_splits[0], (PAIRS, CD), 1.0, 6.0, ((0, 4), (1, 4)))
    doubles_kept = draw_doubles_kept(jax.random.fold_in(jax.random.fold_in(arg_keys[5], part), 71), part)
    integrals = noise(part_splits[2], (CD, AB), (CD // 4) ** -0.5, 0.1875, ((0, 4), (1, 4)))
    integral_kept = touch_ends((jax.random.randint(part_splits[3], (CT, AT), 0, 2) < 1).astype(jnp.int32), jax.random.fold_in(part_splits[3], 1), 0, 1)
    residual = noise(part_splits[4], (PAIRS, AB), 1.0, 6.0, ((0, 4), (1, 4)), jnp.float32)
    return {"doubles": doubles, "doubles_kept": doubles_kept, "integrals": integrals, "integral_kept": integral_kept, "residual": residual}


def reference(doubles, doubles_kept, integrals, integral_kept, residual):
    amp_mask = doubles_kept.astype(jnp.bfloat16)
    screened_doubles = (doubles.reshape(PBLK, PAIR_DEV, CT, TILE) * amp_mask[:, None, :, None]).reshape(PAIRS, CD)
    int_mask = integral_kept.astype(jnp.bfloat16)
    screened_integrals = (integrals.reshape(CT, TILE, AT, TILE) * int_mask[:, None, :, None]).reshape(CD, AB)
    ladder = jnp.dot(screened_doubles.astype(jnp.float32), screened_integrals.astype(jnp.float32), preferred_element_type=jnp.float32)
    return residual + ladder
```

```python
import functools

import jax
import jax.numpy as jnp
from jax import lax
from jax.experimental import pallas as pl
from jax.experimental.pallas import tpu as pltpu
from jax.sharding import PartitionSpec as P

TILE = 128
GROUP = 8
KEEP = 4

VMEM = pl.BlockSpec(memory_space=pltpu.VMEM)
SMEM = pl.BlockSpec(memory_space=pltpu.SMEM)


def list_kept(kept, row, tiles, places):
    at = jnp.int32(0)
    for tile in range(tiles):
        places[at] = jnp.int32(tile)
        at = at + kept[row, tile]


def pack_kernel(tiles, slots, me_ref, kept, doubles, packed, places):
    list_kept(kept, me_ref[0], tiles, places)
    for slot in range(slots):
        start = pl.multiple_of(places[slot] * TILE, TILE)
        packed[:, slot * TILE : (slot + 1) * TILE] = doubles[:, pl.ds(start, TILE)]


def pack(doubles, doubles_kept, me):
    pairs, width = doubles.shape
    tiles = width // TILE
    slots = tiles // GROUP * KEEP
    return pl.pallas_call(
        functools.partial(pack_kernel, tiles, slots),
        out_shape=jax.ShapeDtypeStruct((pairs, slots * TILE), doubles.dtype),
        in_specs=[SMEM, SMEM, VMEM],
        out_specs=VMEM,
        scratch_shapes=[pltpu.SMEM((tiles + 1,), jnp.int32)],
        name="pack",
    )(me, doubles_kept, doubles)


def ladder_kernel(count, tiles, slots, where, kept, int_kept, integrals, *rest):
    blocks, outs = rest[:count], rest[count : 2 * count]
    held, masked, places = rest[2 * count :]
    for i, block in enumerate(blocks):
        held[i] = block[...]
    tiles_ab = integrals.shape[1] // TILE
    for n in range(count):
        list_kept(kept, where[1, n], tiles, places)
        for slot in range(slots):
            tile = places[slot]
            start = pl.multiple_of(tile * TILE, TILE)
            for ab in range(tiles_ab):
                part = integrals[pl.ds(start, TILE), ab * TILE : (ab + 1) * TILE]
                on = (int_kept[tile, ab] != 0).astype(jnp.float32).astype(part.dtype)
                masked[slot * TILE : (slot + 1) * TILE, ab * TILE : (ab + 1) * TILE] = part * on
        outs[n][...] = jnp.dot(held[where[0, n]], masked[...], preferred_element_type=jnp.float32).astype(outs[n].dtype)


def ladder(where, doubles_kept, integral_kept, integrals, blocks, dtype):
    count = len(blocks)
    pairs, packed_width = blocks[0].shape
    tiles = integrals.shape[0] // TILE
    slots = packed_width // TILE
    width = integrals.shape[1]
    return pl.pallas_call(
        functools.partial(ladder_kernel, count, tiles, slots),
        out_shape=[jax.ShapeDtypeStruct((pairs, width), dtype)] * count,
        in_specs=[SMEM, SMEM, SMEM, VMEM] + [VMEM] * count,
        out_specs=[VMEM] * count,
        scratch_shapes=[
            pltpu.VMEM((count, pairs, packed_width), integrals.dtype),
            pltpu.VMEM((packed_width, width), integrals.dtype),
            pltpu.SMEM((tiles + 1,), jnp.int32),
        ],
        name="ladder",
    )(where, doubles_kept, integral_kept, integrals, *blocks)


def swap(x, axis, size, step):
    return lax.ppermute(x, axis, [(i, i ^ step) for i in range(size)])


def local_few(doubles, doubles_kept, integrals, integral_kept, residual):
    count = lax.axis_size("rows")
    row, col = lax.axis_index("rows"), lax.axis_index("cols")
    packed = pack(doubles, doubles_kept, row.astype(jnp.int32).reshape(1))
    blocks = [packed] + [swap(packed, "rows", count, step) for step in range(1, count)]
    steps = jnp.arange(count, dtype=jnp.int32)
    block = jnp.bitwise_xor(col, steps)
    where = jnp.stack([jnp.bitwise_xor(row, block), block]).astype(jnp.int32)
    sums = ladder(where, doubles_kept, integral_kept, integrals, blocks, jnp.float32)
    total = residual + sums[0]
    for step in range(1, count):
        total = total + swap(sums[step], "cols", count, step)
    return total


def local_many(doubles, doubles_kept, integrals, integral_kept, residual):
    row = lax.axis_index("rows")
    packed = pack(doubles, doubles_kept, row.astype(jnp.int32).reshape(1))
    gathered = lax.all_gather(packed, "rows", axis=0)
    number = jnp.arange(1, dtype=jnp.int32)

    def one(block, carry):
        where = jnp.stack([number, number + block])
        (out,) = ladder(where, doubles_kept, integral_kept, integrals, [gathered[block]], jnp.float32)
        return lax.dynamic_update_index_in_dim(carry, out, block, 0)

    shape = (gathered.shape[0], doubles.shape[0], integrals.shape[1])
    sums = lax.fori_loop(0, gathered.shape[0], one, jnp.zeros(shape, jnp.float32))
    sums = sums.reshape(-1, integrals.shape[1])
    return residual + lax.psum_scatter(sums, "cols", scatter_dimension=0, tiled=True)


def solution(mesh):
    rows, cols = mesh.shape["rows"], mesh.shape["cols"]
    few = rows == cols and rows <= 8 and rows & (rows - 1) == 0
    in_specs = (
        P(("groups", "rows"), "cols"),
        P("groups", "cols"),
        P(("groups", "cols"), "rows"),
        P(("groups", "cols"), "rows"),
        P(("groups", "cols"), "rows"),
    )
    out_specs = P(("groups", "cols"), "rows")
    return jax.shard_map(
        local_few if few else local_many, mesh=mesh, in_specs=in_specs, out_specs=out_specs, check_vma=False
    )
```

```python
import functools

import jax
import jax.numpy as jnp
from jax import lax
from jax.experimental import pallas as pl
from jax.experimental.pallas import tpu as pltpu
from jax.sharding import PartitionSpec as P

TILE = 128
GROUP = 8
KEEP = 4
HEAD = 16
STEPS = 8

VMEM = pl.BlockSpec(memory_space=pltpu.VMEM)
SMEM = pl.BlockSpec(memory_space=pltpu.SMEM)
PARAMS = pltpu.CompilerParams(vmem_limit_bytes=8 * 1024 * 1024)


def list_kept(kept, row, tiles, places):
    at = jnp.int32(0)
    for tile in range(tiles):
        places[at] = jnp.int32(tile)
        at = at + kept[row, tile]


def pack_kernel(count, tiles, slots, me, kept, doubles, packed, places):
    list_kept(kept, me[0] // count, tiles, places)
    for slot in range(slots):
        start = pl.multiple_of(places[slot] * TILE, TILE)
        packed[:, slot * TILE : (slot + 1) * TILE] = doubles[:, pl.ds(start, TILE)]


def prepare_kernel(count, tiles, slots, me, kept, int_kept, integrals, own, gathered, product, places):
    row, col = me[0] // count, me[0] % count
    tiles_ab = integrals.shape[1] // TILE
    for n in range(count):
        list_kept(kept, col ^ n, tiles, places)
        for slot in range(slots):
            tile = places[slot]
            start = pl.multiple_of(tile * TILE, TILE)
            for ab in range(tiles_ab):
                part = integrals[pl.ds(start, TILE), ab * TILE : (ab + 1) * TILE]
                on = (int_kept[tile, ab] != 0).astype(jnp.float32).astype(part.dtype)
                gathered[n, slot * TILE : (slot + 1) * TILE, ab * TILE : (ab + 1) * TILE] = part * on
    product[...] = jnp.dot(own[...], gathered[row ^ col], preferred_element_type=jnp.float32)


def encode(x, out):
    pairs, width = x.shape
    largest = jnp.max(jnp.abs(x), axis=0, keepdims=True)
    exponent = jnp.floor((14.95 - jnp.log2(jnp.maximum(largest, 1e-30))) * STEPS)
    scale = jnp.exp2(exponent * (1.0 / STEPS))
    out[:pairs, :] = jnp.round(x * scale).astype(jnp.int32).astype(jnp.int16)
    out[pairs:, :] = jnp.broadcast_to(exponent.astype(jnp.int32), (HEAD, width)).astype(jnp.int16)


def decode(message, pairs):
    code = message[:pairs, :].astype(jnp.int32).astype(jnp.float32)
    exponent = message[pairs:, :].astype(jnp.int32).astype(jnp.float32)[:1, :]
    return code * jnp.exp2(exponent * (-1.0 / STEPS))


def ladder_kernel(count, me, product, gathered, *rest):
    blocks, kept_sums, outs, sums = rest[: count - 1], rest[count - 1], rest[count : 2 * count - 1], rest[-1]
    mine = me[0] // count ^ me[0] % count
    sums[mine] = product[...]
    for step, block in enumerate(blocks, 1):
        sums[mine ^ step] = jnp.dot(block[...], gathered[mine ^ step], preferred_element_type=jnp.float32)
    kept_sums[...] = sums[0]
    for n, out in enumerate(outs, 1):
        encode(sums[n], out)


def finish_kernel(residual, kept_sums, *rest):
    messages, out = rest[:-1], rest[-1]
    total = residual[...] + kept_sums[...]
    for message in messages:
        total = total + decode(message, total.shape[0])
    out[...] = total


def swap(x, axis, size, step):
    return lax.ppermute(x, axis, [(i, i ^ step) for i in range(size)])


def local_few(doubles, doubles_kept, integrals, integral_kept, residual):
    count = lax.axis_size("rows")
    me = (lax.axis_index("rows") * count + lax.axis_index("cols")).astype(jnp.int32).reshape(1)
    pairs, cd_local = doubles.shape
    width = integrals.shape[1]
    tiles = cd_local // TILE
    slots = tiles // GROUP * KEEP
    places = pltpu.SMEM((tiles + 1,), jnp.int32)
    sums_shape = jax.ShapeDtypeStruct((pairs, width), jnp.float32)
    packed = pl.pallas_call(
        functools.partial(pack_kernel, count, tiles, slots),
        out_shape=jax.ShapeDtypeStruct((pairs, slots * TILE), doubles.dtype),
        in_specs=[SMEM, SMEM, VMEM],
        out_specs=VMEM,
        scratch_shapes=[places],
        compiler_params=PARAMS,
        name="pack",
    )(me, doubles_kept, doubles)
    blocks = [swap(packed, "rows", count, step) for step in range(1, count)]
    gathered, product = pl.pallas_call(
        functools.partial(prepare_kernel, count, tiles, slots),
        out_shape=[jax.ShapeDtypeStruct((count, slots * TILE, width), integrals.dtype), sums_shape],
        in_specs=[SMEM, SMEM, SMEM, VMEM, VMEM],
        out_specs=[VMEM] * 2,
        scratch_shapes=[places],
        compiler_params=PARAMS,
        cost_estimate=pl.CostEstimate(flops=2 * pairs * slots * TILE * width, bytes_accessed=4 << 20, transcendentals=0),
        name="prepare",
    )(me, doubles_kept, integral_kept, integrals, packed)
    message = jax.ShapeDtypeStruct((pairs + HEAD, width), jnp.int16)
    kept_sums, *messages = pl.pallas_call(
        functools.partial(ladder_kernel, count),
        out_shape=[sums_shape] + [message] * (count - 1),
        in_specs=[SMEM] + [VMEM] * (count + 1),
        out_specs=[VMEM] * count,
        scratch_shapes=[pltpu.VMEM((count, pairs, width), jnp.float32)],
        compiler_params=PARAMS,
        name="ladder",
    )(me, product, gathered, *blocks)
    messages = [swap(x, "cols", count, step) for step, x in reversed(list(enumerate(messages, 1)))]
    return pl.pallas_call(
        finish_kernel,
        out_shape=sums_shape,
        in_specs=[VMEM] * (count + 1),
        out_specs=VMEM,
        compiler_params=PARAMS,
        name="finish",
    )(residual, kept_sums, *messages)


def local_many(doubles, doubles_kept, integrals, integral_kept, residual):
    pairs, cd_local = doubles.shape
    tiles = cd_local // TILE
    blocks = lax.all_gather(doubles, "rows", axis=0).reshape(-1, pairs, tiles, TILE)
    blocks = blocks * doubles_kept.astype(doubles.dtype)[:, None, :, None]
    tiles_ab = integrals.shape[1] // TILE
    masked = integrals.reshape(tiles, TILE, tiles_ab, TILE) * integral_kept.astype(integrals.dtype)[:, None, :, None]
    sums = jnp.dot(
        blocks.reshape(-1, cd_local), masked.reshape(integrals.shape), preferred_element_type=jnp.float32
    )
    return residual + lax.psum_scatter(sums, "cols", scatter_dimension=0, tiled=True)


def solution(mesh):
    rows, cols = mesh.shape["rows"], mesh.shape["cols"]
    few = rows == cols and rows <= 8 and rows & (rows - 1) == 0
    in_specs = (
        P(("groups", "rows"), "cols"),
        P("groups", "cols"),
        P(("groups", "cols"), "rows"),
        P(("groups", "cols"), "rows"),
        P(("groups", "cols"), "rows"),
    )
    out_specs = P(("groups", "cols"), "rows")
    return jax.shard_map(
        local_few if few else local_many, mesh=mesh, in_specs=in_specs, out_specs=out_specs, check_vma=False
    )
```

```python
import functools

import jax
import jax.numpy as jnp
from jax import lax
from jax.experimental import pallas as pl
from jax.experimental.pallas import tpu as pltpu
from jax.sharding import PartitionSpec as P

TILE = 128
GROUP = 8
KEEP = 4
HEAD = 16
STEPS = 8

VMEM = pl.BlockSpec(memory_space=pltpu.VMEM)
SMEM = pl.BlockSpec(memory_space=pltpu.SMEM)
HBM = pl.BlockSpec(memory_space=pltpu.HBM)
PARAMS = pltpu.CompilerParams(vmem_limit_bytes=8 * 1024 * 1024)
ROWS = 4


def list_kept(kept, row, tiles, places):
    at = jnp.int32(0)
    for tile in range(tiles):
        places[at] = jnp.int32(tile)
        at = at + kept[row, tile]


def half_of(ref, half):
    size = ref.shape[0] // 2
    return ref.at[pl.ds(pl.multiple_of(half * size, size), size)]


def pack_kernel(tiles, slots, me, kept, doubles, packed, near_half, far_half, table, block, places, sems):
    row = me[0] // ROWS
    table_copy = pltpu.make_async_copy(kept, table, sems.at[0])
    block_copy = pltpu.make_async_copy(doubles, block, sems.at[1])
    table_copy.start()
    block_copy.start()
    table_copy.wait()
    list_kept(table, row, tiles, places)
    block_copy.wait()
    for slot in range(slots):
        tile = pl.ds(pl.multiple_of(places[slot] * TILE, TILE), TILE)
        to = slice(slot * TILE, (slot + 1) * TILE)
        packed[:, to] = block[:, tile]
        near_half[:, to] = half_of(block, row % 2)[:, tile]
        far_half[:, to] = half_of(block, 1 - row % 2)[:, tile]


def prepare_kernel(tiles, slots, me, kept, int_kept, integrals, own, gathered, product, places):
    row, col = me[0] // ROWS, me[0] % ROWS
    tiles_ab = integrals.shape[1] // TILE
    for n in range(ROWS):
        list_kept(kept, col ^ n, tiles, places)
        for slot in range(slots):
            tile = places[slot]
            start = pl.multiple_of(tile * TILE, TILE)
            for ab in range(tiles_ab):
                part = integrals[pl.ds(start, TILE), ab * TILE : (ab + 1) * TILE]
                on = (int_kept[tile, ab] != 0).astype(jnp.float32).astype(part.dtype)
                gathered[n, slot * TILE : (slot + 1) * TILE, ab * TILE : (ab + 1) * TILE] = part * on
    product[...] = jnp.dot(own[...], gathered[row ^ col], preferred_element_type=jnp.float32)


def encode(x, out):
    pairs, width = x.shape
    largest = jnp.max(jnp.abs(x), axis=0, keepdims=True)
    exponent = jnp.floor((14.95 - jnp.log2(jnp.maximum(largest, 1e-30))) * STEPS)
    code = jnp.round(x * jnp.exp2(exponent * (1.0 / STEPS))).astype(jnp.int32)
    bands = width // TILE
    each = HEAD // bands
    exponent = jnp.broadcast_to(exponent.astype(jnp.int32), (each, width))
    for band in range(bands):
        out[band * pairs : (band + 1) * pairs, :] = code[:, band * TILE : (band + 1) * TILE].astype(jnp.int16)
    head = jnp.concatenate([exponent[:, band * TILE : (band + 1) * TILE] for band in range(bands)], axis=0)
    out[bands * pairs :, :] = head.astype(jnp.int16)


def decode(message, pairs):
    bands = (message.shape[0] - HEAD) // pairs
    each = HEAD // bands
    head = message[bands * pairs :, :].astype(jnp.int32).astype(jnp.float32)
    parts = []
    for band in range(bands):
        scale = jnp.exp2(head[band * each : band * each + 1, :] * (-1.0 / STEPS))
        parts.append(message[band * pairs : (band + 1) * pairs, :].astype(jnp.int32).astype(jnp.float32) * scale)
    return jnp.concatenate(parts, axis=1)


def ladder_kernel(phase, me, product, gathered, pair, near, far, kept_sums, *rest):
    outs, sums = rest[:-1], rest[-1]
    row = me[0] // ROWS
    mine = row ^ me[0] % ROWS
    half = row % 2 if phase == 0 else 1 - row % 2
    sums[mine] = half_of(product, half)[...]
    for step, block in enumerate((half_of(pair, half), near, far), 1):
        sums[mine ^ step] = jnp.dot(block[...], gathered[mine ^ step], preferred_element_type=jnp.float32)
    kept_sums[...] = sums[0]
    for n, out in enumerate(outs, 1):
        encode(sums[n], out)


def total_of(start, kept_sums, messages):
    total = start + kept_sums[...]
    for message in messages:
        total = total + decode(message, total.shape[0])
    return total


def first_kernel(me, residual, kept_sums, *rest):
    messages, out = rest[:-1], rest[-1]
    half = me[0] // ROWS % 2
    half_of(out, 1 - half)[...] = half_of(residual, 1 - half)[...]
    half_of(out, half)[...] = total_of(half_of(residual, half)[...], kept_sums, messages)


def second_kernel(me, base, kept_sums, *rest):
    messages, out = rest[:-1], rest[-1]
    half = me[0] // ROWS % 2
    half_of(out, half)[...] = half_of(base, half)[...]
    half_of(out, 1 - half)[...] = total_of(half_of(base, 1 - half)[...], kept_sums, messages)


def swap(x, axis, step):
    return lax.ppermute(x, axis, [(i, i ^ step) for i in range(ROWS)])


def local_few(doubles, doubles_kept, integrals, integral_kept, residual):
    me = (lax.axis_index("rows") * ROWS + lax.axis_index("cols")).astype(jnp.int32).reshape(1)
    pairs, cd_local = doubles.shape
    width = integrals.shape[1]
    tiles = cd_local // TILE
    slots = tiles // GROUP * KEEP
    places = pltpu.SMEM((tiles + 1,), jnp.int32)
    sums_shape = jax.ShapeDtypeStruct((pairs, width), jnp.float32)
    half_sums = jax.ShapeDtypeStruct((pairs // 2, width), jnp.float32)
    half_block = jax.ShapeDtypeStruct((pairs // 2, slots * TILE), doubles.dtype)
    message = jax.ShapeDtypeStruct((pairs // 2 * width // TILE + HEAD, TILE), jnp.int16)
    packed, near_half, far_half = pl.pallas_call(
        functools.partial(pack_kernel, tiles, slots),
        out_shape=[jax.ShapeDtypeStruct((pairs, slots * TILE), doubles.dtype), half_block, half_block],
        in_specs=[SMEM, HBM, HBM],
        out_specs=[VMEM] * 3,
        scratch_shapes=[
            pltpu.SMEM(doubles_kept.shape, jnp.int32),
            pltpu.VMEM(doubles.shape, doubles.dtype),
            places,
            pltpu.SemaphoreType.DMA((2,)),
        ],
        compiler_params=PARAMS,
        name="pack",
    )(me, pltpu.with_memory_space_constraint(doubles_kept, pltpu.HBM), pltpu.with_memory_space_constraint(doubles, pltpu.HBM))
    near = swap(near_half, "rows", 2)
    far = swap(far_half, "rows", 3)
    pair = swap(packed, "rows", 1)
    gathered, product = pl.pallas_call(
        functools.partial(prepare_kernel, tiles, slots),
        out_shape=[jax.ShapeDtypeStruct((ROWS, slots * TILE, width), integrals.dtype), sums_shape],
        in_specs=[SMEM, SMEM, SMEM, VMEM, VMEM],
        out_specs=[VMEM] * 2,
        scratch_shapes=[places],
        compiler_params=PARAMS,
        cost_estimate=pl.CostEstimate(flops=2 * pairs * slots * TILE * width, bytes_accessed=4 << 20, transcendentals=0),
        name="prepare",
    )(me, doubles_kept, integral_kept, integrals, packed)
    far_late = swap(near, "rows", 1)
    near_late = swap(far, "rows", 1)

    def ladder(phase, near, far):
        kept_sums, *messages = pl.pallas_call(
            functools.partial(ladder_kernel, phase),
            out_shape=[half_sums] + [message] * (ROWS - 1),
            in_specs=[SMEM] + [VMEM] * 5,
            out_specs=[VMEM] * ROWS,
            scratch_shapes=[pltpu.VMEM((ROWS,) + half_sums.shape, jnp.float32)],
            compiler_params=PARAMS,
            name="ladder",
        )(me, product, gathered, pair, near, far)
        return [kept_sums] + [swap(x, "cols", step) for step, x in reversed(list(enumerate(messages, 1)))]

    def finish(kernel, start, sums):
        return pl.pallas_call(
            kernel,
            out_shape=sums_shape,
            in_specs=[SMEM] + [VMEM] * (ROWS + 1),
            out_specs=VMEM,
            compiler_params=PARAMS,
            name="finish",
        )(me, start, *sums)

    first = ladder(0, near, far)
    second = ladder(1, near_late, far_late)
    return finish(second_kernel, finish(first_kernel, residual, first), second)


def local_many(doubles, doubles_kept, integrals, integral_kept, residual):
    pairs, cd_local = doubles.shape
    tiles = cd_local // TILE
    blocks = lax.all_gather(doubles, "rows", axis=0).reshape(-1, pairs, tiles, TILE)
    blocks = blocks * doubles_kept.astype(doubles.dtype)[:, None, :, None]
    tiles_ab = integrals.shape[1] // TILE
    masked = integrals.reshape(tiles, TILE, tiles_ab, TILE) * integral_kept.astype(integrals.dtype)[:, None, :, None]
    sums = jnp.dot(
        blocks.reshape(-1, cd_local), masked.reshape(integrals.shape), preferred_element_type=jnp.float32
    )
    return residual + lax.psum_scatter(sums, "cols", scatter_dimension=0, tiled=True)


def solution(mesh):
    few = mesh.shape["rows"] == mesh.shape["cols"] == ROWS
    in_specs = (
        P(("groups", "rows"), "cols"),
        P("groups", "cols"),
        P(("groups", "cols"), "rows"),
        P(("groups", "cols"), "rows"),
        P(("groups", "cols"), "rows"),
    )
    out_specs = P(("groups", "cols"), "rows")
    return jax.shard_map(
        local_few if few else local_many, mesh=mesh, in_specs=in_specs, out_specs=out_specs, check_vma=False
    )
```

```python
import functools

import jax
import jax.numpy as jnp
from jax import lax
from jax.experimental import pallas as pl
from jax.experimental.pallas import tpu as pltpu
from jax.sharding import PartitionSpec as P

TILE = 128
GROUP = 8
KEEP = 4
HEAD = 16
STEPS = 8

VMEM = pl.BlockSpec(memory_space=pltpu.VMEM)
SMEM = pl.BlockSpec(memory_space=pltpu.SMEM)
HBM = pl.BlockSpec(memory_space=pltpu.HBM)
PARAMS = pltpu.CompilerParams(vmem_limit_bytes=8 * 1024 * 1024)
ROWS = 4


def list_kept(kept, row, tiles, places):
    at = jnp.int32(0)
    for tile in range(tiles):
        places[at] = jnp.int32(tile)
        at = at + kept[row, tile]


def half_of(ref, half):
    size = ref.shape[0] // 2
    return ref.at[pl.ds(pl.multiple_of(half * size, size), size)]


def pack_kernel(tiles, slots, me, kept, doubles, packed, near_half, far_half, table, block, places, sems):
    row = me[0] // ROWS
    table_copy = pltpu.make_async_copy(kept, table, sems.at[0])
    block_copy = pltpu.make_async_copy(doubles, block, sems.at[1])
    table_copy.start()
    block_copy.start()
    table_copy.wait()
    list_kept(table, row, tiles, places)
    block_copy.wait()
    for slot in range(slots):
        tile = pl.ds(pl.multiple_of(places[slot] * TILE, TILE), TILE)
        to = slice(slot * TILE, (slot + 1) * TILE)
        packed[:, to] = block[:, tile]
        near_half[:, to] = half_of(block, row % 2)[:, tile]
        far_half[:, to] = half_of(block, 1 - row % 2)[:, tile]


def prepare_kernel(tiles, slots, me, kept, int_kept, integrals, own, gathered, product, token, places):
    row, col = me[0] // ROWS, me[0] % ROWS
    tiles_ab = integrals.shape[1] // TILE
    for n in range(ROWS):
        list_kept(kept, col ^ n, tiles, places)
        for slot in range(slots):
            tile = places[slot]
            start = pl.multiple_of(tile * TILE, TILE)
            for ab in range(tiles_ab):
                part = integrals[pl.ds(start, TILE), ab * TILE : (ab + 1) * TILE]
                on = (int_kept[tile, ab] != 0).astype(jnp.float32).astype(part.dtype)
                gathered[n, slot * TILE : (slot + 1) * TILE, ab * TILE : (ab + 1) * TILE] = part * on
    product[...] = jnp.dot(own[...], gathered[row ^ col], preferred_element_type=jnp.float32)
    token[0] = row


def after_kernel(token, x, out):
    pass


def encode(x, out):
    pairs, width = x.shape
    largest = jnp.max(jnp.abs(x), axis=0, keepdims=True)
    exponent = jnp.floor((14.95 - jnp.log2(jnp.maximum(largest, 1e-30))) * STEPS)
    code = jnp.round(x * jnp.exp2(exponent * (1.0 / STEPS))).astype(jnp.int32)
    bands = width // TILE
    each = HEAD // bands
    exponent = jnp.broadcast_to(exponent.astype(jnp.int32), (each, width))
    for band in range(bands):
        out[band * pairs : (band + 1) * pairs, :] = code[:, band * TILE : (band + 1) * TILE].astype(jnp.int16)
    head = jnp.concatenate([exponent[:, band * TILE : (band + 1) * TILE] for band in range(bands)], axis=0)
    out[bands * pairs :, :] = head.astype(jnp.int16)


def decode(message, pairs):
    bands = (message.shape[0] - HEAD) // pairs
    each = HEAD // bands
    head = message[bands * pairs :, :].astype(jnp.int32).astype(jnp.float32)
    parts = []
    for band in range(bands):
        scale = jnp.exp2(head[band * each : band * each + 1, :] * (-1.0 / STEPS))
        parts.append(message[band * pairs : (band + 1) * pairs, :].astype(jnp.int32).astype(jnp.float32) * scale)
    return jnp.concatenate(parts, axis=1)


def ladder_kernel(phase, me, product, gathered, pair, near, far, kept_sums, *rest):
    outs, sums = rest[:-1], rest[-1]
    row = me[0] // ROWS
    mine = row ^ me[0] % ROWS
    half = row % 2 if phase == 0 else 1 - row % 2
    sums[mine] = half_of(product, half)[...]
    for step, block in enumerate((half_of(pair, half), near, far), 1):
        sums[mine ^ step] = jnp.dot(block[...], gathered[mine ^ step], preferred_element_type=jnp.float32)
    kept_sums[...] = sums[0]
    for n, out in enumerate(outs, 1):
        encode(sums[n], out)


def total_of(start, kept_sums, messages):
    total = start + kept_sums[...]
    for message in messages:
        total = total + decode(message, total.shape[0])
    return total


def first_kernel(me, residual, kept_sums, *rest):
    messages, out = rest[:-1], rest[-1]
    half = me[0] // ROWS % 2
    half_of(out, 1 - half)[...] = half_of(residual, 1 - half)[...]
    half_of(out, half)[...] = total_of(half_of(residual, half)[...], kept_sums, messages)


def second_kernel(me, base, kept_sums, *rest):
    messages, out = rest[:-1], rest[-1]
    half = me[0] // ROWS % 2
    half_of(out, half)[...] = half_of(base, half)[...]
    half_of(out, 1 - half)[...] = total_of(half_of(base, 1 - half)[...], kept_sums, messages)


def swap(x, axis, step):
    return lax.ppermute(x, axis, [(i, i ^ step) for i in range(ROWS)])


def local_few(doubles, doubles_kept, integrals, integral_kept, residual):
    me = (lax.axis_index("rows") * ROWS + lax.axis_index("cols")).astype(jnp.int32).reshape(1)
    pairs, cd_local = doubles.shape
    width = integrals.shape[1]
    tiles = cd_local // TILE
    slots = tiles // GROUP * KEEP
    places = pltpu.SMEM((tiles + 1,), jnp.int32)
    sums_shape = jax.ShapeDtypeStruct((pairs, width), jnp.float32)
    half_sums = jax.ShapeDtypeStruct((pairs // 2, width), jnp.float32)
    half_block = jax.ShapeDtypeStruct((pairs // 2, slots * TILE), doubles.dtype)
    message = jax.ShapeDtypeStruct((pairs // 2 * width // TILE + HEAD, TILE), jnp.int16)
    packed, near_half, far_half = pl.pallas_call(
        functools.partial(pack_kernel, tiles, slots),
        out_shape=[jax.ShapeDtypeStruct((pairs, slots * TILE), doubles.dtype), half_block, half_block],
        in_specs=[SMEM, HBM, HBM],
        out_specs=[VMEM] * 3,
        scratch_shapes=[
            pltpu.SMEM(doubles_kept.shape, jnp.int32),
            pltpu.VMEM(doubles.shape, doubles.dtype),
            places,
            pltpu.SemaphoreType.DMA((2,)),
        ],
        compiler_params=PARAMS,
        name="pack",
    )(me, pltpu.with_memory_space_constraint(doubles_kept, pltpu.HBM), pltpu.with_memory_space_constraint(doubles, pltpu.HBM))
    near = swap(near_half, "rows", 2)
    far = swap(far_half, "rows", 3)
    pair = swap(packed, "rows", 1)
    gathered, product, token = pl.pallas_call(
        functools.partial(prepare_kernel, tiles, slots),
        out_shape=[jax.ShapeDtypeStruct((ROWS, slots * TILE, width), integrals.dtype), sums_shape, jax.ShapeDtypeStruct((1,), jnp.int32)],
        in_specs=[SMEM, SMEM, SMEM, VMEM, VMEM],
        out_specs=[VMEM, VMEM, SMEM],
        scratch_shapes=[places],
        compiler_params=PARAMS,
        cost_estimate=pl.CostEstimate(flops=2 * pairs * slots * TILE * width, bytes_accessed=4 << 20, transcendentals=0),
        name="prepare",
    )(me, doubles_kept, integral_kept, integrals, packed)
    after = pl.pallas_call(
        after_kernel,
        out_shape=half_block,
        in_specs=[SMEM, pl.BlockSpec(memory_space=pl.ANY)],
        out_specs=pl.BlockSpec(memory_space=pl.ANY),
        input_output_aliases={1: 0},
        compiler_params=PARAMS,
        name="after",
    )
    near, far = after(token, near), after(token, far)
    far_late = swap(near, "rows", 1)
    near_late = swap(far, "rows", 1)

    def ladder(phase, near, far):
        kept_sums, *messages = pl.pallas_call(
            functools.partial(ladder_kernel, phase),
            out_shape=[half_sums] + [message] * (ROWS - 1),
            in_specs=[SMEM] + [VMEM] * 5,
            out_specs=[VMEM] * ROWS,
            scratch_shapes=[pltpu.VMEM((ROWS,) + half_sums.shape, jnp.float32)],
            compiler_params=PARAMS,
            name="ladder",
        )(me, product, gathered, pair, near, far)
        return [kept_sums] + [swap(x, "cols", step) for step, x in reversed(list(enumerate(messages, 1)))]

    def finish(kernel, start, sums):
        return pl.pallas_call(
            kernel,
            out_shape=sums_shape,
            in_specs=[SMEM] + [VMEM] * (ROWS + 1),
            out_specs=VMEM,
            compiler_params=PARAMS,
            name="finish",
        )(me, start, *sums)

    first = ladder(0, near, far)
    second = ladder(1, near_late, far_late)
    return finish(second_kernel, finish(first_kernel, residual, first), second)


def local_many(doubles, doubles_kept, integrals, integral_kept, residual):
    pairs, cd_local = doubles.shape
    tiles = cd_local // TILE
    blocks = lax.all_gather(doubles, "rows", axis=0).reshape(-1, pairs, tiles, TILE)
    blocks = blocks * doubles_kept.astype(doubles.dtype)[:, None, :, None]
    tiles_ab = integrals.shape[1] // TILE
    masked = integrals.reshape(tiles, TILE, tiles_ab, TILE) * integral_kept.astype(integrals.dtype)[:, None, :, None]
    sums = jnp.dot(
        blocks.reshape(-1, cd_local), masked.reshape(integrals.shape), preferred_element_type=jnp.float32
    )
    return residual + lax.psum_scatter(sums, "cols", scatter_dimension=0, tiled=True)


def solution(mesh):
    few = mesh.shape["rows"] == mesh.shape["cols"] == ROWS
    in_specs = (
        P(("groups", "rows"), "cols"),
        P("groups", "cols"),
        P(("groups", "cols"), "rows"),
        P(("groups", "cols"), "rows"),
        P(("groups", "cols"), "rows"),
    )
    out_specs = P(("groups", "cols"), "rows")
    return jax.shard_map(
        local_few if few else local_many, mesh=mesh, in_specs=in_specs, out_specs=out_specs, check_vma=False
    )
```

```python
import functools

import jax
import jax.numpy as jnp
from jax import lax
from jax.experimental import pallas as pl
from jax.experimental.pallas import tpu as pltpu
from jax.sharding import PartitionSpec as P

TILE = 128
GROUP = 8
KEEP = 4
HEAD = 16
STEPS = 8

VMEM = pl.BlockSpec(memory_space=pltpu.VMEM)
SMEM = pl.BlockSpec(memory_space=pltpu.SMEM)
HBM = pl.BlockSpec(memory_space=pltpu.HBM)
PARAMS = pltpu.CompilerParams(vmem_limit_bytes=8 * 1024 * 1024)


def list_kept(kept, row, tiles, places):
    at = jnp.int32(0)
    for tile in range(tiles):
        places[at] = jnp.int32(tile)
        at = at + kept[row, tile]


def pack_kernel(count, tiles, slots, me, kept, doubles, packed, table, block, places, sems):
    table_copy = pltpu.make_async_copy(kept, table, sems.at[0])
    block_copy = pltpu.make_async_copy(doubles, block, sems.at[1])
    table_copy.start()
    block_copy.start()
    table_copy.wait()
    list_kept(table, me[0] // count, tiles, places)
    block_copy.wait()
    for slot in range(slots):
        tile = block[:, pl.ds(pl.multiple_of(places[slot] * TILE, TILE), TILE)]
        for n in range(count):
            packed[n, :, slot * TILE : (slot + 1) * TILE] = tile


def prepare_kernel(count, tiles, slots, me, kept, int_kept, integrals, own, gathered, product, places):
    row, col = me[0] // count, me[0] % count
    tiles_ab = integrals.shape[1] // TILE
    for n in range(count):
        list_kept(kept, col ^ n, tiles, places)
        for slot in range(slots):
            tile = places[slot]
            start = pl.multiple_of(tile * TILE, TILE)
            for ab in range(tiles_ab):
                part = integrals[pl.ds(start, TILE), ab * TILE : (ab + 1) * TILE]
                on = (int_kept[tile, ab] != 0).astype(jnp.float32).astype(part.dtype)
                gathered[n, slot * TILE : (slot + 1) * TILE, ab * TILE : (ab + 1) * TILE] = part * on
    product[...] = jnp.dot(own[0], gathered[row ^ col], preferred_element_type=jnp.float32)


def encode(x, out):
    pairs, width = x.shape
    largest = jnp.max(jnp.abs(x), axis=0, keepdims=True)
    exponent = jnp.floor((14.95 - jnp.log2(jnp.maximum(largest, 1e-30))) * STEPS)
    scale = jnp.exp2(exponent * (1.0 / STEPS))
    out[:pairs, :] = jnp.round(x * scale).astype(jnp.int32).astype(jnp.int16)
    out[pairs:, :] = jnp.broadcast_to(exponent.astype(jnp.int32), (HEAD, width)).astype(jnp.int16)


def decode(message, pairs):
    code = message[:pairs, :].astype(jnp.int32).astype(jnp.float32)
    exponent = message[pairs:, :].astype(jnp.int32).astype(jnp.float32)[:1, :]
    return code * jnp.exp2(exponent * (-1.0 / STEPS))


def ladder_kernel(count, me, product, gathered, blocks, kept_sums, messages, sums):
    row, col = me[0] // count, me[0] % count
    mine = row ^ col
    sums[mine] = product[...]
    for step in range(1, count):
        sums[mine ^ step] = jnp.dot(blocks[row ^ step], gathered[mine ^ step], preferred_element_type=jnp.float32)
    kept_sums[...] = sums[0]
    for n in range(1, count):
        encode(sums[n], messages.at[col ^ n])


def finish_kernel(count, me, residual, kept_sums, messages, out):
    col = me[0] % count
    total = residual[...] + kept_sums[...]
    for n in range(1, count):
        total = total + decode(messages.at[col ^ n], total.shape[0])
    out[...] = total


def local_few(doubles, doubles_kept, integrals, integral_kept, residual):
    count = lax.axis_size("rows")
    me = (lax.axis_index("rows") * count + lax.axis_index("cols")).astype(jnp.int32).reshape(1)
    pairs, cd_local = doubles.shape
    width = integrals.shape[1]
    tiles = cd_local // TILE
    slots = tiles // GROUP * KEEP
    places = pltpu.SMEM((tiles + 1,), jnp.int32)
    sums_shape = jax.ShapeDtypeStruct((pairs, width), jnp.float32)
    packed = pl.pallas_call(
        functools.partial(pack_kernel, count, tiles, slots),
        out_shape=jax.ShapeDtypeStruct((count, pairs, slots * TILE), doubles.dtype),
        in_specs=[SMEM, HBM, HBM],
        out_specs=VMEM,
        scratch_shapes=[
            pltpu.SMEM(doubles_kept.shape, jnp.int32),
            pltpu.VMEM(doubles.shape, doubles.dtype),
            places,
            pltpu.SemaphoreType.DMA((2,)),
        ],
        compiler_params=PARAMS,
        name="pack",
    )(
        me,
        pltpu.with_memory_space_constraint(doubles_kept, pltpu.HBM),
        pltpu.with_memory_space_constraint(doubles, pltpu.HBM),
    )
    blocks = lax.all_to_all(packed, "rows", split_axis=0, concat_axis=0)
    gathered, product = pl.pallas_call(
        functools.partial(prepare_kernel, count, tiles, slots),
        out_shape=[jax.ShapeDtypeStruct((count, slots * TILE, width), integrals.dtype), sums_shape],
        in_specs=[SMEM, SMEM, SMEM, VMEM, VMEM],
        out_specs=[VMEM] * 2,
        scratch_shapes=[places],
        compiler_params=PARAMS,
        cost_estimate=pl.CostEstimate(flops=2 * pairs * slots * TILE * width, bytes_accessed=4 << 20, transcendentals=0),
        name="prepare",
    )(me, doubles_kept, integral_kept, integrals, packed)
    message = jax.ShapeDtypeStruct((count, pairs + HEAD, width), jnp.int16)
    kept_sums, messages = pl.pallas_call(
        functools.partial(ladder_kernel, count),
        out_shape=[sums_shape] + [message],
        in_specs=[SMEM] + [VMEM] * 3,
        out_specs=[VMEM] * 2,
        scratch_shapes=[pltpu.VMEM((count, pairs, width), jnp.float32)],
        compiler_params=PARAMS,
        name="ladder",
    )(me, product, gathered, blocks)
    messages = lax.all_to_all(messages, "cols", split_axis=0, concat_axis=0)
    return pl.pallas_call(
        functools.partial(finish_kernel, count),
        out_shape=sums_shape,
        in_specs=[SMEM] + [VMEM] * 3,
        out_specs=VMEM,
        compiler_params=PARAMS,
        name="finish",
    )(me, residual, kept_sums, messages)


def local_many(doubles, doubles_kept, integrals, integral_kept, residual):
    pairs, cd_local = doubles.shape
    tiles = cd_local // TILE
    blocks = lax.all_gather(doubles, "rows", axis=0).reshape(-1, pairs, tiles, TILE)
    blocks = blocks * doubles_kept.astype(doubles.dtype)[:, None, :, None]
    tiles_ab = integrals.shape[1] // TILE
    masked = integrals.reshape(tiles, TILE, tiles_ab, TILE) * integral_kept.astype(integrals.dtype)[:, None, :, None]
    sums = jnp.dot(
        blocks.reshape(-1, cd_local), masked.reshape(integrals.shape), preferred_element_type=jnp.float32
    )
    return residual + lax.psum_scatter(sums, "cols", scatter_dimension=0, tiled=True)


def solution(mesh):
    rows, cols = mesh.shape["rows"], mesh.shape["cols"]
    few = rows == cols and rows <= 8 and rows & (rows - 1) == 0
    in_specs = (
        P(("groups", "rows"), "cols"),
        P("groups", "cols"),
        P(("groups", "cols"), "rows"),
        P(("groups", "cols"), "rows"),
        P(("groups", "cols"), "rows"),
    )
    out_specs = P(("groups", "cols"), "rows")
    return jax.shard_map(
        local_few if few else local_many, mesh=mesh, in_specs=in_specs, out_specs=out_specs, check_vma=False
    )
```

```python
import functools

import jax
import jax.numpy as jnp
from jax import lax
from jax.experimental import pallas as pl
from jax.experimental.pallas import tpu as pltpu
from jax.sharding import PartitionSpec as P

TILE = 128
GROUP = 8
KEEP = 4
HEAD = 16
STEPS = 8

VMEM = pl.BlockSpec(memory_space=pltpu.VMEM)
SMEM = pl.BlockSpec(memory_space=pltpu.SMEM)
HBM = pl.BlockSpec(memory_space=pltpu.HBM)
PARAMS = pltpu.CompilerParams(vmem_limit_bytes=8 * 1024 * 1024)
ROWS = 4


def cost(flops):
    return pl.CostEstimate(flops=flops, bytes_accessed=1024, transcendentals=0)


def list_kept(kept, row, tiles, places):
    at = jnp.int32(0)
    for tile in range(tiles):
        places[at] = jnp.int32(tile)
        at = at + kept[row, tile]


def part_of(ref, part, size):
    return ref.at[pl.ds(pl.multiple_of(part * size, size), size)]


def pack_kernel(tiles, slots, me, kept, doubles, packed, direct, near, far, table, block, places, sems):
    row = me[0] // ROWS
    table_copy = pltpu.make_async_copy(kept, table, sems.at[0])
    block_copy = pltpu.make_async_copy(doubles, block, sems.at[1])
    table_copy.start()
    block_copy.start()
    table_copy.wait()
    list_kept(table, row, tiles, places)
    block_copy.wait()
    half, quarter = direct.shape[0], near.shape[0]
    for slot in range(slots):
        tile = pl.ds(pl.multiple_of(places[slot] * TILE, TILE), TILE)
        to = slice(slot * TILE, (slot + 1) * TILE)
        packed[:, to] = block[:, tile]
        direct[:, to] = block[:half, tile]
        near[:, to] = part_of(block, 2 + row % 2, quarter)[:, tile]
        far[:, to] = part_of(block, 3 - row % 2, quarter)[:, tile]


def prepare_kernel(tiles, slots, me, kept, int_kept, integrals, own, gathered, product, places):
    row, col = me[0] // ROWS, me[0] % ROWS
    tiles_ab = integrals.shape[1] // TILE
    for n in range(ROWS):
        list_kept(kept, col ^ n, tiles, places)
        for slot in range(slots):
            tile = places[slot]
            start = pl.multiple_of(tile * TILE, TILE)
            for ab in range(tiles_ab):
                part = integrals[pl.ds(start, TILE), ab * TILE : (ab + 1) * TILE]
                on = (int_kept[tile, ab] != 0).astype(jnp.float32).astype(part.dtype)
                gathered[n, slot * TILE : (slot + 1) * TILE, ab * TILE : (ab + 1) * TILE] = part * on
    product[...] = jnp.dot(own[...], gathered[row ^ col], preferred_element_type=jnp.float32)


def after_kernel(token, x, out):
    pass


def encode(x, out):
    pairs, width = x.shape
    largest = jnp.max(jnp.abs(x), axis=0, keepdims=True)
    exponent = jnp.floor((14.95 - jnp.log2(jnp.maximum(largest, 1e-30))) * STEPS)
    code = jnp.round(x * jnp.exp2(exponent * (1.0 / STEPS))).astype(jnp.int32)
    bands = width // TILE
    each = HEAD // bands
    exponent = jnp.broadcast_to(exponent.astype(jnp.int32), (each, width))
    for band in range(bands):
        out[band * pairs : (band + 1) * pairs, :] = code[:, band * TILE : (band + 1) * TILE].astype(jnp.int16)
    head = jnp.concatenate([exponent[:, band * TILE : (band + 1) * TILE] for band in range(bands)], axis=0)
    out[bands * pairs :, :] = head.astype(jnp.int16)


def decode(message, pairs):
    bands = (message.shape[0] - HEAD) // pairs
    each = HEAD // bands
    head = message[bands * pairs :, :].astype(jnp.int32).astype(jnp.float32)
    parts = []
    for band in range(bands):
        scale = jnp.exp2(head[band * each : band * each + 1, :] * (-1.0 / STEPS))
        parts.append(message[band * pairs : (band + 1) * pairs, :].astype(jnp.int32).astype(jnp.float32) * scale)
    return jnp.concatenate(parts, axis=1)


def send_sums(sums, kept_sums, outs):
    kept_sums[...] = sums[0]
    for n, out in enumerate(outs, 1):
        encode(sums[n], out)


def direct_kernel(me, product, gathered, pair, near, far, kept_sums, *rest):
    outs, sums = rest[:-1], rest[-1]
    mine = me[0] // ROWS ^ me[0] % ROWS
    half = near.shape[0]
    sums[mine] = product[:half, :]
    for step, block in enumerate((pair[:half, :], near[...], far[...]), 1):
        sums[mine ^ step] = jnp.dot(block, gathered[mine ^ step], preferred_element_type=jnp.float32)
    send_sums(sums, kept_sums, outs)


def swapped_kernel(me, product, gathered, pair, near, far, near_late, far_late, kept_sums, *rest):
    outs, sums = rest[:-1], rest[-1]
    row = me[0] // ROWS
    mine = row ^ me[0] % ROWS
    quarter = near.shape[0]
    sums[mine] = product[2 * quarter :, :]
    sums[mine ^ 1] = jnp.dot(pair[2 * quarter :, :], gathered[mine ^ 1], preferred_element_type=jnp.float32)
    for step, block, late in ((2, near, near_late), (3, far, far_late)):
        for part, x in ((row % 2, block), (1 - row % 2, late)):
            part_of(sums.at[mine ^ step], part, quarter)[...] = jnp.dot(
                x[...], gathered[mine ^ step], preferred_element_type=jnp.float32
            )
    send_sums(sums, kept_sums, outs)


def total_of(start, kept_sums, messages):
    total = start + kept_sums[...]
    for message in messages:
        total = total + decode(message, total.shape[0])
    return total


def first_kernel(residual, kept_sums, *rest):
    messages, out = rest[:-1], rest[-1]
    half = kept_sums.shape[0]
    out[:half, :] = total_of(residual[:half, :], kept_sums, messages)
    out[half:, :] = residual[half:, :]


def second_kernel(base, kept_sums, *rest):
    messages, out = rest[:-1], rest[-1]
    half = kept_sums.shape[0]
    out[:half, :] = base[:half, :]
    out[half:, :] = total_of(base[half:, :], kept_sums, messages)


def after(token, x, flops):
    return pl.pallas_call(
        after_kernel,
        out_shape=jax.ShapeDtypeStruct(x.shape, x.dtype),
        in_specs=[pl.BlockSpec(memory_space=pl.ANY)] * 2,
        out_specs=pl.BlockSpec(memory_space=pl.ANY),
        input_output_aliases={1: 0},
        compiler_params=PARAMS,
        cost_estimate=cost(flops),
        name="after",
    )(token, x)


def swap(x, axis, step):
    return lax.ppermute(x, axis, [(i, i ^ step) for i in range(ROWS)])


def local_few(doubles, doubles_kept, integrals, integral_kept, residual):
    me = (lax.axis_index("rows") * ROWS + lax.axis_index("cols")).astype(jnp.int32).reshape(1)
    pairs, cd_local = doubles.shape
    width = integrals.shape[1]
    tiles = cd_local // TILE
    slots = tiles // GROUP * KEEP
    places = pltpu.SMEM((tiles + 1,), jnp.int32)
    sums_shape = jax.ShapeDtypeStruct((pairs, width), jnp.float32)
    half_sums = jax.ShapeDtypeStruct((pairs // 2, width), jnp.float32)
    half_block = jax.ShapeDtypeStruct((pairs // 2, slots * TILE), doubles.dtype)
    quarter_block = jax.ShapeDtypeStruct((pairs // 4, slots * TILE), doubles.dtype)
    message = jax.ShapeDtypeStruct((pairs // 2 * width // TILE + HEAD, TILE), jnp.int16)
    packed, direct, near, far = pl.pallas_call(
        functools.partial(pack_kernel, tiles, slots),
        out_shape=[jax.ShapeDtypeStruct((pairs, slots * TILE), doubles.dtype), half_block, quarter_block, quarter_block],
        in_specs=[SMEM, HBM, HBM],
        out_specs=[VMEM] * 4,
        scratch_shapes=[
            pltpu.SMEM(doubles_kept.shape, jnp.int32),
            pltpu.VMEM(doubles.shape, doubles.dtype),
            places,
            pltpu.SemaphoreType.DMA((2,)),
        ],
        compiler_params=PARAMS,
        name="pack",
    )(me, pltpu.with_memory_space_constraint(doubles_kept, pltpu.HBM), pltpu.with_memory_space_constraint(doubles, pltpu.HBM))
    pair = swap(packed, "rows", 1)
    far_direct = swap(direct, "rows", 3)
    near_direct = swap(direct, "rows", 2)
    far = swap(far, "rows", 3)
    near = swap(near, "rows", 2)
    gathered, product = pl.pallas_call(
        functools.partial(prepare_kernel, tiles, slots),
        out_shape=[jax.ShapeDtypeStruct((ROWS, slots * TILE, width), integrals.dtype), sums_shape],
        in_specs=[SMEM, SMEM, SMEM, VMEM, VMEM],
        out_specs=[VMEM] * 2,
        scratch_shapes=[places],
        compiler_params=PARAMS,
        cost_estimate=cost(0),
        name="prepare",
    )(me, doubles_kept, integral_kept, integrals, packed)
    near, far = after(product, near, 10**10), after(product, far, 0)
    far_late = swap(near, "rows", 1)
    near_late = swap(far, "rows", 1)

    def ladder(kernel, *blocks):
        kept_sums, *messages = pl.pallas_call(
            kernel,
            out_shape=[half_sums] + [message] * (ROWS - 1),
            in_specs=[SMEM] + [VMEM] * (3 + len(blocks)),
            out_specs=[VMEM] * ROWS,
            scratch_shapes=[pltpu.VMEM((ROWS,) + half_sums.shape, jnp.float32)],
            compiler_params=PARAMS,
            cost_estimate=cost(10**11),
            name="ladder",
        )(me, product, gathered, pair, *blocks)
        return [kept_sums] + [swap(x, "cols", step) for step, x in reversed(list(enumerate(messages, 1)))]

    def finish(kernel, start, sums):
        return pl.pallas_call(
            kernel,
            out_shape=sums_shape,
            in_specs=[VMEM] * (ROWS + 1),
            out_specs=VMEM,
            compiler_params=PARAMS,
            name="finish",
        )(start, *sums)

    first = ladder(direct_kernel, near_direct, far_direct)
    second = ladder(swapped_kernel, near, far, near_late, far_late)
    return finish(second_kernel, finish(first_kernel, residual, first), second)


def local_many(doubles, doubles_kept, integrals, integral_kept, residual):
    pairs, cd_local = doubles.shape
    tiles = cd_local // TILE
    blocks = lax.all_gather(doubles, "rows", axis=0).reshape(-1, pairs, tiles, TILE)
    blocks = blocks * doubles_kept.astype(doubles.dtype)[:, None, :, None]
    tiles_ab = integrals.shape[1] // TILE
    masked = integrals.reshape(tiles, TILE, tiles_ab, TILE) * integral_kept.astype(integrals.dtype)[:, None, :, None]
    sums = jnp.dot(
        blocks.reshape(-1, cd_local), masked.reshape(integrals.shape), preferred_element_type=jnp.float32
    )
    return residual + lax.psum_scatter(sums, "cols", scatter_dimension=0, tiled=True)


def solution(mesh):
    few = mesh.shape["rows"] == mesh.shape["cols"] == ROWS
    in_specs = (
        P(("groups", "rows"), "cols"),
        P("groups", "cols"),
        P(("groups", "cols"), "rows"),
        P(("groups", "cols"), "rows"),
        P(("groups", "cols"), "rows"),
    )
    out_specs = P(("groups", "cols"), "rows")
    return jax.shard_map(
        local_few if few else local_many, mesh=mesh, in_specs=in_specs, out_specs=out_specs, check_vma=False
    )
```

```python
import functools

import jax
import jax.numpy as jnp
from jax import lax
from jax.experimental import pallas as pl
from jax.experimental.pallas import tpu as pltpu
from jax.sharding import PartitionSpec as P

TILE = 128
GROUP = 8
KEEP = 4
HEAD = 16
STEPS = 8

VMEM = pl.BlockSpec(memory_space=pltpu.VMEM)
SMEM = pl.BlockSpec(memory_space=pltpu.SMEM)
HBM = pl.BlockSpec(memory_space=pltpu.HBM)
PARAMS = pltpu.CompilerParams(vmem_limit_bytes=8 * 1024 * 1024)
ROWS = 4


def cost(flops):
    return pl.CostEstimate(flops=flops, bytes_accessed=1024, transcendentals=0)


def list_kept(kept, row, tiles, places):
    at = jnp.int32(0)
    for tile in range(tiles):
        places[at] = jnp.int32(tile)
        at = at + kept[row, tile]


def pack_kernel(tiles, slots, me, kept, doubles, packed, first, second, table, block, places, sems):
    table_copy = pltpu.make_async_copy(kept, table, sems.at[0])
    block_copy = pltpu.make_async_copy(doubles, block, sems.at[1])
    table_copy.start()
    block_copy.start()
    table_copy.wait()
    list_kept(table, me[0] // ROWS, tiles, places)
    block_copy.wait()
    half = first.shape[0]
    for slot in range(slots):
        tile = block[:, pl.ds(pl.multiple_of(places[slot] * TILE, TILE), TILE)]
        to = slice(slot * TILE, (slot + 1) * TILE)
        packed[:, to] = tile
        first[:, to] = tile[:half]
        second[:, to] = tile[half:]


def prepare_kernel(tiles, slots, me, kept, int_kept, integrals, own, gathered, product, places):
    row, col = me[0] // ROWS, me[0] % ROWS
    tiles_ab = integrals.shape[1] // TILE
    for n in range(ROWS):
        list_kept(kept, col ^ n, tiles, places)
        for slot in range(slots):
            tile = places[slot]
            start = pl.multiple_of(tile * TILE, TILE)
            for ab in range(tiles_ab):
                part = integrals[pl.ds(start, TILE), ab * TILE : (ab + 1) * TILE]
                on = (int_kept[tile, ab] != 0).astype(jnp.float32).astype(part.dtype)
                gathered[n, slot * TILE : (slot + 1) * TILE, ab * TILE : (ab + 1) * TILE] = part * on
    product[...] = jnp.dot(own[...], gathered[row ^ col], preferred_element_type=jnp.float32)


def encode(x, out):
    pairs, width = x.shape
    largest = jnp.max(jnp.abs(x), axis=0, keepdims=True)
    exponent = jnp.floor((14.95 - jnp.log2(jnp.maximum(largest, 1e-30))) * STEPS)
    code = jnp.round(x * jnp.exp2(exponent * (1.0 / STEPS))).astype(jnp.int32)
    bands = width // TILE
    each = HEAD // bands
    exponent = jnp.broadcast_to(exponent.astype(jnp.int32), (each, width))
    for band in range(bands):
        out[band * pairs : (band + 1) * pairs, :] = code[:, band * TILE : (band + 1) * TILE].astype(jnp.int16)
    head = jnp.concatenate([exponent[:, band * TILE : (band + 1) * TILE] for band in range(bands)], axis=0)
    out[bands * pairs :, :] = head.astype(jnp.int16)


def decode(message, pairs):
    bands = (message.shape[0] - HEAD) // pairs
    each = HEAD // bands
    head = message[bands * pairs :, :].astype(jnp.int32).astype(jnp.float32)
    parts = []
    for band in range(bands):
        scale = jnp.exp2(head[band * each : band * each + 1, :] * (-1.0 / STEPS))
        parts.append(message[band * pairs : (band + 1) * pairs, :].astype(jnp.int32).astype(jnp.float32) * scale)
    return jnp.concatenate(parts, axis=1)


def ladder_kernel(start, me, product, gathered, *rest):
    blocks, kept_sums, outs, sums = rest[: ROWS - 1], rest[ROWS - 1], rest[ROWS:-1], rest[-1]
    mine = me[0] // ROWS ^ me[0] % ROWS
    sums[mine] = product[start : start + sums.shape[1], :]
    for step, block in zip(range(ROWS - 1, 0, -1), blocks):
        sums[mine ^ step] = jnp.dot(block[...], gathered[mine ^ step], preferred_element_type=jnp.float32)
    kept_sums[...] = sums[0]
    for n, out in enumerate(outs, 1):
        encode(sums[n], out)


def total_of(start, kept_sums, messages):
    total = start + kept_sums[...]
    for message in messages:
        total = total + decode(message, total.shape[0])
    return total


def first_kernel(residual, kept_sums, *rest):
    messages, out = rest[:-1], rest[-1]
    half = kept_sums.shape[0]
    out[:half, :] = total_of(residual[:half, :], kept_sums, messages)
    out[half:, :] = residual[half:, :]


def second_kernel(base, kept_sums, *rest):
    messages, out = rest[:-1], rest[-1]
    half = kept_sums.shape[0]
    out[:half, :] = base[:half, :]
    out[half:, :] = total_of(base[half:, :], kept_sums, messages)


def swap(x, axis, step):
    return lax.ppermute(x, axis, [(i, i ^ step) for i in range(ROWS)])


def local_few(doubles, doubles_kept, integrals, integral_kept, residual):
    me = (lax.axis_index("rows") * ROWS + lax.axis_index("cols")).astype(jnp.int32).reshape(1)
    pairs, cd_local = doubles.shape
    width = integrals.shape[1]
    tiles = cd_local // TILE
    slots = tiles // GROUP * KEEP
    places = pltpu.SMEM((tiles + 1,), jnp.int32)
    sums_shape = jax.ShapeDtypeStruct((pairs, width), jnp.float32)
    half_sums = jax.ShapeDtypeStruct((pairs // 2, width), jnp.float32)
    half_block = jax.ShapeDtypeStruct((pairs // 2, slots * TILE), doubles.dtype)
    message = jax.ShapeDtypeStruct((pairs // 2 * width // TILE + HEAD, TILE), jnp.int16)
    packed, first, second = pl.pallas_call(
        functools.partial(pack_kernel, tiles, slots),
        out_shape=[jax.ShapeDtypeStruct((pairs, slots * TILE), doubles.dtype), half_block, half_block],
        in_specs=[SMEM, HBM, HBM],
        out_specs=[VMEM] * 3,
        scratch_shapes=[
            pltpu.SMEM(doubles_kept.shape, jnp.int32),
            pltpu.VMEM(doubles.shape, doubles.dtype),
            places,
            pltpu.SemaphoreType.DMA((2,)),
        ],
        compiler_params=PARAMS,
        name="pack",
    )(me, pltpu.with_memory_space_constraint(doubles_kept, pltpu.HBM), pltpu.with_memory_space_constraint(doubles, pltpu.HBM))
    first, second = ([swap(x, "rows", step) for step in range(ROWS - 1, 0, -1)] for x in (first, second))
    gathered, product = pl.pallas_call(
        functools.partial(prepare_kernel, tiles, slots),
        out_shape=[jax.ShapeDtypeStruct((ROWS, slots * TILE, width), integrals.dtype), sums_shape],
        in_specs=[SMEM, SMEM, SMEM, VMEM, VMEM],
        out_specs=[VMEM] * 2,
        scratch_shapes=[places],
        compiler_params=PARAMS,
        cost_estimate=cost(0),
        name="prepare",
    )(me, doubles_kept, integral_kept, integrals, packed)
    def ladder(start, blocks):
        kept_sums, *messages = pl.pallas_call(
            functools.partial(ladder_kernel, start),
            out_shape=[half_sums] + [message] * (ROWS - 1),
            in_specs=[SMEM] + [VMEM] * 5,
            out_specs=[VMEM] * ROWS,
            scratch_shapes=[pltpu.VMEM((ROWS,) + half_sums.shape, jnp.float32)],
            compiler_params=PARAMS,
            cost_estimate=cost(10**11),
            name="ladder",
        )(me, product, gathered, *blocks)
        return [kept_sums] + [swap(x, "cols", step) for step, x in reversed(list(enumerate(messages, 1)))]

    def finish(kernel, start, sums):
        return pl.pallas_call(
            kernel,
            out_shape=sums_shape,
            in_specs=[VMEM] * (ROWS + 1),
            out_specs=VMEM,
            compiler_params=PARAMS,
            name="finish",
        )(start, *sums)

    sums = finish(first_kernel, residual, ladder(0, first))
    return finish(second_kernel, sums, ladder(pairs // 2, second))


def local_many(doubles, doubles_kept, integrals, integral_kept, residual):
    pairs, cd_local = doubles.shape
    tiles = cd_local // TILE
    blocks = lax.all_gather(doubles, "rows", axis=0).reshape(-1, pairs, tiles, TILE)
    blocks = blocks * doubles_kept.astype(doubles.dtype)[:, None, :, None]
    tiles_ab = integrals.shape[1] // TILE
    masked = integrals.reshape(tiles, TILE, tiles_ab, TILE) * integral_kept.astype(integrals.dtype)[:, None, :, None]
    sums = jnp.dot(
        blocks.reshape(-1, cd_local), masked.reshape(integrals.shape), preferred_element_type=jnp.float32
    )
    return residual + lax.psum_scatter(sums, "cols", scatter_dimension=0, tiled=True)


def solution(mesh):
    few = mesh.shape["rows"] == mesh.shape["cols"] == ROWS
    in_specs = (
        P(("groups", "rows"), "cols"),
        P("groups", "cols"),
        P(("groups", "cols"), "rows"),
        P(("groups", "cols"), "rows"),
        P(("groups", "cols"), "rows"),
    )
    out_specs = P(("groups", "cols"), "rows")
    return jax.shard_map(
        local_few if few else local_many, mesh=mesh, in_specs=in_specs, out_specs=out_specs, check_vma=False
    )
```

```python
import functools

import jax
import jax.numpy as jnp
from jax import lax
from jax.experimental import pallas as pl
from jax.experimental.pallas import tpu as pltpu
from jax.sharding import PartitionSpec as P

TILE = 128
GROUP = 8
KEEP = 4
HEAD = 16
STEPS = 8

VMEM = pl.BlockSpec(memory_space=pltpu.VMEM)
SMEM = pl.BlockSpec(memory_space=pltpu.SMEM)
HBM = pl.BlockSpec(memory_space=pltpu.HBM)
PARAMS = pltpu.CompilerParams(vmem_limit_bytes=8 * 1024 * 1024)
ROWS = 4


def cost(flops):
    return pl.CostEstimate(flops=flops, bytes_accessed=1024, transcendentals=0)


def list_kept(kept, row, tiles, places):
    at = jnp.int32(0)
    for tile in range(tiles):
        places[at] = jnp.int32(tile)
        at = at + kept[row, tile]


def pack_kernel(tiles, slots, me, kept, doubles, packed, first, second, table, block, places, sems):
    table_copy = pltpu.make_async_copy(kept, table, sems.at[0])
    block_copy = pltpu.make_async_copy(doubles, block, sems.at[1])
    table_copy.start()
    block_copy.start()
    table_copy.wait()
    list_kept(table, me[0] // ROWS, tiles, places)
    block_copy.wait()
    half = first.shape[0]
    for slot in range(slots):
        tile = block[:, pl.ds(pl.multiple_of(places[slot] * TILE, TILE), TILE)]
        to = slice(slot * TILE, (slot + 1) * TILE)
        packed[:, to] = tile
        first[:, to] = tile[:half]
        second[:, to] = tile[half:]


def prepare_kernel(tiles, slots, me, kept, int_kept, integrals, own, gathered, product, table, int_table, held, places, sems):
    copies = [
        pltpu.make_async_copy(*pair, sems.at[i])
        for i, pair in enumerate(((kept, table), (int_kept, int_table), (integrals, held)))
    ]
    for copy in copies:
        copy.start()
    for copy in copies:
        copy.wait()
    row, col = me[0] // ROWS, me[0] % ROWS
    tiles_ab = integrals.shape[1] // TILE
    for n in range(ROWS):
        list_kept(table, col ^ n, tiles, places)
        for slot in range(slots):
            tile = places[slot]
            start = pl.multiple_of(tile * TILE, TILE)
            for ab in range(tiles_ab):
                part = held[pl.ds(start, TILE), ab * TILE : (ab + 1) * TILE]
                on = (int_table[tile, ab] != 0).astype(jnp.float32).astype(part.dtype)
                gathered[n, slot * TILE : (slot + 1) * TILE, ab * TILE : (ab + 1) * TILE] = part * on
    product[...] = jnp.dot(own[...], gathered[row ^ col], preferred_element_type=jnp.float32)


def encode(x, out):
    pairs, width = x.shape
    largest = jnp.max(jnp.abs(x), axis=0, keepdims=True)
    exponent = jnp.floor((14.95 - jnp.log2(jnp.maximum(largest, 1e-30))) * STEPS)
    code = jnp.round(x * jnp.exp2(exponent * (1.0 / STEPS))).astype(jnp.int32)
    bands = width // TILE
    each = HEAD // bands
    exponent = jnp.broadcast_to(exponent.astype(jnp.int32), (each, width))
    for band in range(bands):
        out[band * pairs : (band + 1) * pairs, :] = code[:, band * TILE : (band + 1) * TILE].astype(jnp.int16)
    head = jnp.concatenate([exponent[:, band * TILE : (band + 1) * TILE] for band in range(bands)], axis=0)
    out[bands * pairs :, :] = head.astype(jnp.int16)


def decode(message, pairs):
    bands = (message.shape[0] - HEAD) // pairs
    each = HEAD // bands
    head = message[bands * pairs :, :].astype(jnp.int32).astype(jnp.float32)
    parts = []
    for band in range(bands):
        scale = jnp.exp2(head[band * each : band * each + 1, :] * (-1.0 / STEPS))
        parts.append(message[band * pairs : (band + 1) * pairs, :].astype(jnp.int32).astype(jnp.float32) * scale)
    return jnp.concatenate(parts, axis=1)


def far_kernel(me, gathered, near, far, near_sums, far_sums):
    mine = me[0] // ROWS ^ me[0] % ROWS
    near_sums[...] = jnp.dot(near[...], gathered[mine ^ 2], preferred_element_type=jnp.float32)
    far_sums[...] = jnp.dot(far[...], gathered[mine ^ 3], preferred_element_type=jnp.float32)


def ladder_kernel(me, product, gathered, pair, near, far, kept_sums, *rest):
    outs, sums = rest[:-1], rest[-1]
    mine = me[0] // ROWS ^ me[0] % ROWS
    half = near.shape[0]
    multiplied = near.dtype == jnp.float32
    part = slice(0, half) if multiplied else slice(half, 2 * half)
    sums[mine] = product[part, :]
    sums[mine ^ 1] = jnp.dot(pair[part, :], gathered[mine ^ 1], preferred_element_type=jnp.float32)
    for step, x in ((2, near), (3, far)):
        if multiplied:
            sums[mine ^ step] = x[...]
        else:
            sums[mine ^ step] = jnp.dot(x[...], gathered[mine ^ step], preferred_element_type=jnp.float32)
    kept_sums[...] = sums[0]
    for n, out in enumerate(outs, 1):
        encode(sums[n], out)


def total_of(start, kept_sums, messages):
    total = start + kept_sums[...]
    for message in messages:
        total = total + decode(message, total.shape[0])
    return total


def first_kernel(residual, kept_sums, *rest):
    messages, out = rest[:-1], rest[-1]
    half = kept_sums.shape[0]
    out[:half, :] = total_of(residual[:half, :], kept_sums, messages)
    out[half:, :] = residual[half:, :]


def second_kernel(base, kept_sums, *rest):
    messages, out = rest[:-1], rest[-1]
    half = kept_sums.shape[0]
    out[:half, :] = base[:half, :]
    out[half:, :] = total_of(base[half:, :], kept_sums, messages)


def swap(x, axis, step):
    return lax.ppermute(x, axis, [(i, i ^ step) for i in range(ROWS)])


def local_few(doubles, doubles_kept, integrals, integral_kept, residual):
    me = (lax.axis_index("rows") * ROWS + lax.axis_index("cols")).astype(jnp.int32).reshape(1)
    pairs, cd_local = doubles.shape
    width = integrals.shape[1]
    tiles = cd_local // TILE
    slots = tiles // GROUP * KEEP
    places = pltpu.SMEM((tiles + 1,), jnp.int32)
    sums_shape = jax.ShapeDtypeStruct((pairs, width), jnp.float32)
    half_sums = jax.ShapeDtypeStruct((pairs // 2, width), jnp.float32)
    half_block = jax.ShapeDtypeStruct((pairs // 2, slots * TILE), doubles.dtype)
    message = jax.ShapeDtypeStruct((pairs // 2 * width // TILE + HEAD, TILE), jnp.int16)
    doubles, doubles_kept, integrals, integral_kept = (
        pltpu.with_memory_space_constraint(x, pltpu.HBM) for x in (doubles, doubles_kept, integrals, integral_kept)
    )
    packed, first, second = pl.pallas_call(
        functools.partial(pack_kernel, tiles, slots),
        out_shape=[jax.ShapeDtypeStruct((pairs, slots * TILE), doubles.dtype), half_block, half_block],
        in_specs=[SMEM, HBM, HBM],
        out_specs=[VMEM] * 3,
        scratch_shapes=[
            pltpu.SMEM(doubles_kept.shape, jnp.int32),
            pltpu.VMEM(doubles.shape, doubles.dtype),
            places,
            pltpu.SemaphoreType.DMA((2,)),
        ],
        compiler_params=PARAMS,
        name="pack",
    )(me, doubles_kept, doubles)
    pair = swap(packed, "rows", 1)
    first, second = ([swap(x, "rows", step) for step in (2, 3)] for x in (first, second))
    gathered, product = pl.pallas_call(
        functools.partial(prepare_kernel, tiles, slots),
        out_shape=[jax.ShapeDtypeStruct((ROWS, slots * TILE, width), integrals.dtype), sums_shape],
        in_specs=[SMEM, HBM, HBM, HBM, VMEM],
        out_specs=[VMEM] * 2,
        scratch_shapes=[
            pltpu.SMEM(doubles_kept.shape, jnp.int32),
            pltpu.SMEM(integral_kept.shape, jnp.int32),
            pltpu.VMEM(integrals.shape, integrals.dtype),
            places,
            pltpu.SemaphoreType.DMA((3,)),
        ],
        compiler_params=PARAMS,
        cost_estimate=cost(0),
        name="prepare",
    )(me, doubles_kept, integral_kept, integrals, packed)
    first = pl.pallas_call(
        far_kernel,
        out_shape=[half_sums] * 2,
        in_specs=[SMEM] + [VMEM] * 3,
        out_specs=[VMEM] * 2,
        compiler_params=PARAMS,
        cost_estimate=cost(10**9),
        name="far",
    )(me, gathered, *first)

    def ladder(near, far):
        kept_sums, *messages = pl.pallas_call(
            ladder_kernel,
            out_shape=[half_sums] + [message] * (ROWS - 1),
            in_specs=[SMEM] + [VMEM] * 5,
            out_specs=[VMEM] * ROWS,
            scratch_shapes=[pltpu.VMEM((ROWS,) + half_sums.shape, jnp.float32)],
            compiler_params=PARAMS,
            cost_estimate=cost(10**11),
            name="ladder",
        )(me, product, gathered, pair, near, far)
        return [kept_sums] + [swap(x, "cols", step) for step, x in reversed(list(enumerate(messages, 1)))]

    def finish(kernel, start, sums):
        return pl.pallas_call(
            kernel,
            out_shape=sums_shape,
            in_specs=[VMEM] * (ROWS + 1),
            out_specs=VMEM,
            compiler_params=PARAMS,
            name="finish",
        )(start, *sums)

    sums = finish(first_kernel, residual, ladder(*first))
    return finish(second_kernel, sums, ladder(*second))


def local_many(doubles, doubles_kept, integrals, integral_kept, residual):
    pairs, cd_local = doubles.shape
    tiles = cd_local // TILE
    blocks = lax.all_gather(doubles, "rows", axis=0).reshape(-1, pairs, tiles, TILE)
    blocks = blocks * doubles_kept.astype(doubles.dtype)[:, None, :, None]
    tiles_ab = integrals.shape[1] // TILE
    masked = integrals.reshape(tiles, TILE, tiles_ab, TILE) * integral_kept.astype(integrals.dtype)[:, None, :, None]
    sums = jnp.dot(
        blocks.reshape(-1, cd_local), masked.reshape(integrals.shape), preferred_element_type=jnp.float32
    )
    return residual + lax.psum_scatter(sums, "cols", scatter_dimension=0, tiled=True)


def solution(mesh):
    few = mesh.shape["rows"] == mesh.shape["cols"] == ROWS
    in_specs = (
        P(("groups", "rows"), "cols"),
        P("groups", "cols"),
        P(("groups", "cols"), "rows"),
        P(("groups", "cols"), "rows"),
        P(("groups", "cols"), "rows"),
    )
    out_specs = P(("groups", "cols"), "rows")
    return jax.shard_map(
        local_few if few else local_many, mesh=mesh, in_specs=in_specs, out_specs=out_specs, check_vma=False
    )
```

```python
import functools

import jax
import jax.numpy as jnp
from jax import lax
from jax.experimental import pallas as pl
from jax.experimental.pallas import tpu as pltpu
from jax.sharding import PartitionSpec as P

TILE = 128
GROUP = 8
KEEP = 4
HEAD = 16
STEPS = 8

VMEM = pl.BlockSpec(memory_space=pltpu.VMEM)
SMEM = pl.BlockSpec(memory_space=pltpu.SMEM)
HBM = pl.BlockSpec(memory_space=pltpu.HBM)
PARAMS = pltpu.CompilerParams(vmem_limit_bytes=8 * 1024 * 1024)
ROWS = 4


def cost(flops):
    return pl.CostEstimate(flops=flops, bytes_accessed=1024, transcendentals=0)


def list_kept(kept, row, tiles, places):
    at = jnp.int32(0)
    for tile in range(tiles):
        places[at] = jnp.int32(tile)
        at = at + kept[row, tile]


def pack_kernel(tiles, slots, me, kept, doubles, packed, first, second, table, block, places, sems):
    table_copy = pltpu.make_async_copy(kept, table, sems.at[0])
    block_copy = pltpu.make_async_copy(doubles, block, sems.at[1])
    table_copy.start()
    block_copy.start()
    table_copy.wait()
    list_kept(table, me[0] // ROWS, tiles, places)
    block_copy.wait()
    half = first.shape[0]
    for slot in range(slots):
        tile = block[:, pl.ds(pl.multiple_of(places[slot] * TILE, TILE), TILE)]
        to = slice(slot * TILE, (slot + 1) * TILE)
        packed[:, to] = tile
        first[:, to] = tile[:half]
        second[:, to] = tile[half:]


def prepare_kernel(tiles, slots, me, kept, int_kept, integrals, own, gathered, product, table, int_table, held, places, sems):
    copies = [
        pltpu.make_async_copy(*pair, sems.at[i])
        for i, pair in enumerate(((kept, table), (int_kept, int_table), (integrals, held)))
    ]
    for copy in copies:
        copy.start()
    for copy in copies:
        copy.wait()
    row, col = me[0] // ROWS, me[0] % ROWS
    tiles_ab = integrals.shape[1] // TILE
    for n in range(ROWS):
        list_kept(table, col ^ n, tiles, places)
        for slot in range(slots):
            tile = places[slot]
            start = pl.multiple_of(tile * TILE, TILE)
            for ab in range(tiles_ab):
                part = held[pl.ds(start, TILE), ab * TILE : (ab + 1) * TILE]
                on = (int_table[tile, ab] != 0).astype(jnp.float32).astype(part.dtype)
                gathered[n, slot * TILE : (slot + 1) * TILE, ab * TILE : (ab + 1) * TILE] = part * on
    product[...] = jnp.dot(own[...], gathered[row ^ col], preferred_element_type=jnp.float32)


def encode(x, out):
    pairs, width = x.shape
    largest = jnp.max(jnp.abs(x), axis=0, keepdims=True)
    exponent = jnp.floor((14.95 - jnp.log2(jnp.maximum(largest, 1e-30))) * STEPS)
    code = jnp.round(x * jnp.exp2(exponent * (1.0 / STEPS))).astype(jnp.int32)
    bands = width // TILE
    each = HEAD // bands
    exponent = jnp.broadcast_to(exponent.astype(jnp.int32), (each, width))
    for band in range(bands):
        out[band * pairs : (band + 1) * pairs, :] = code[:, band * TILE : (band + 1) * TILE].astype(jnp.int16)
    head = jnp.concatenate([exponent[:, band * TILE : (band + 1) * TILE] for band in range(bands)], axis=0)
    out[bands * pairs :, :] = head.astype(jnp.int16)


def decode(message, pairs):
    bands = (message.shape[0] - HEAD) // pairs
    each = HEAD // bands
    head = message[bands * pairs :, :].astype(jnp.int32).astype(jnp.float32)
    parts = []
    for band in range(bands):
        scale = jnp.exp2(head[band * each : band * each + 1, :] * (-1.0 / STEPS))
        parts.append(message[band * pairs : (band + 1) * pairs, :].astype(jnp.int32).astype(jnp.float32) * scale)
    return jnp.concatenate(parts, axis=1)


def ladder_kernel(me, product, gathered, pair, near_first, near_second, far_first, far_second, kept_sums, *rest):
    outs, sums = rest[:-1], rest[-1]
    mine = me[0] // ROWS ^ me[0] % ROWS
    half = near_first.shape[0]
    sums[mine] = product[...]
    sums[mine ^ 1] = jnp.dot(pair[...], gathered[mine ^ 1], preferred_element_type=jnp.float32)
    for step, start, block in ((2, 0, near_first), (3, 0, far_first), (2, half, near_second), (3, half, far_second)):
        sums[mine ^ step, start : start + half, :] = jnp.dot(
            block[...], gathered[mine ^ step], preferred_element_type=jnp.float32
        )
    kept_sums[...] = sums[0]
    for n, out in enumerate(outs, 1):
        encode(sums[n], out)


def finish_kernel(residual, kept_sums, *rest):
    messages, out = rest[:-1], rest[-1]
    total = residual[...] + kept_sums[...]
    for message in messages:
        total = total + decode(message, total.shape[0])
    out[...] = total


def swap(x, axis, step):
    return lax.ppermute(x, axis, [(i, i ^ step) for i in range(ROWS)])


def local_few(doubles, doubles_kept, integrals, integral_kept, residual):
    me = (lax.axis_index("rows") * ROWS + lax.axis_index("cols")).astype(jnp.int32).reshape(1)
    pairs, cd_local = doubles.shape
    width = integrals.shape[1]
    tiles = cd_local // TILE
    slots = tiles // GROUP * KEEP
    places = pltpu.SMEM((tiles + 1,), jnp.int32)
    sums_shape = jax.ShapeDtypeStruct((pairs, width), jnp.float32)
    half_block = jax.ShapeDtypeStruct((pairs // 2, slots * TILE), doubles.dtype)
    message = jax.ShapeDtypeStruct((pairs * width // TILE + HEAD, TILE), jnp.int16)
    doubles, doubles_kept, integrals, integral_kept = (
        pltpu.with_memory_space_constraint(x, pltpu.HBM) for x in (doubles, doubles_kept, integrals, integral_kept)
    )
    packed, first, second = pl.pallas_call(
        functools.partial(pack_kernel, tiles, slots),
        out_shape=[jax.ShapeDtypeStruct((pairs, slots * TILE), doubles.dtype), half_block, half_block],
        in_specs=[SMEM, HBM, HBM],
        out_specs=[VMEM] * 3,
        scratch_shapes=[
            pltpu.SMEM(doubles_kept.shape, jnp.int32),
            pltpu.VMEM(doubles.shape, doubles.dtype),
            places,
            pltpu.SemaphoreType.DMA((2,)),
        ],
        compiler_params=PARAMS,
        name="pack",
    )(me, doubles_kept, doubles)
    near_second = swap(second, "rows", 2)
    pair = swap(packed, "rows", 1)
    far_first = swap(first, "rows", 3)
    near_first = swap(first, "rows", 2)
    far_second = swap(near_second, "rows", 1)
    gathered, product = pl.pallas_call(
        functools.partial(prepare_kernel, tiles, slots),
        out_shape=[jax.ShapeDtypeStruct((ROWS, slots * TILE, width), integrals.dtype), sums_shape],
        in_specs=[SMEM, HBM, HBM, HBM, VMEM],
        out_specs=[VMEM] * 2,
        scratch_shapes=[
            pltpu.SMEM(doubles_kept.shape, jnp.int32),
            pltpu.SMEM(integral_kept.shape, jnp.int32),
            pltpu.VMEM(integrals.shape, integrals.dtype),
            places,
            pltpu.SemaphoreType.DMA((3,)),
        ],
        compiler_params=PARAMS,
        cost_estimate=cost(0),
        name="prepare",
    )(me, doubles_kept, integral_kept, integrals, packed)
    kept_sums, *messages = pl.pallas_call(
        ladder_kernel,
        out_shape=[sums_shape] + [message] * (ROWS - 1),
        in_specs=[SMEM] + [VMEM] * 7,
        out_specs=[VMEM] * ROWS,
        scratch_shapes=[pltpu.VMEM((ROWS, pairs, width), jnp.float32)],
        compiler_params=PARAMS,
        cost_estimate=cost(10**11),
        name="ladder",
    )(me, product, gathered, pair, near_first, near_second, far_first, far_second)
    messages = [swap(x, "cols", step) for step, x in reversed(list(enumerate(messages, 1)))]
    return pl.pallas_call(
        finish_kernel,
        out_shape=sums_shape,
        in_specs=[VMEM] * (ROWS + 1),
        out_specs=VMEM,
        compiler_params=PARAMS,
        name="finish",
    )(residual, kept_sums, *messages)


def local_many(doubles, doubles_kept, integrals, integral_kept, residual):
    pairs, cd_local = doubles.shape
    tiles = cd_local // TILE
    blocks = lax.all_gather(doubles, "rows", axis=0).reshape(-1, pairs, tiles, TILE)
    blocks = blocks * doubles_kept.astype(doubles.dtype)[:, None, :, None]
    tiles_ab = integrals.shape[1] // TILE
    masked = integrals.reshape(tiles, TILE, tiles_ab, TILE) * integral_kept.astype(integrals.dtype)[:, None, :, None]
    sums = jnp.dot(
        blocks.reshape(-1, cd_local), masked.reshape(integrals.shape), preferred_element_type=jnp.float32
    )
    return residual + lax.psum_scatter(sums, "cols", scatter_dimension=0, tiled=True)


def solution(mesh):
    few = mesh.shape["rows"] == mesh.shape["cols"] == ROWS
    in_specs = (
        P(("groups", "rows"), "cols"),
        P("groups", "cols"),
        P(("groups", "cols"), "rows"),
        P(("groups", "cols"), "rows"),
        P(("groups", "cols"), "rows"),
    )
    out_specs = P(("groups", "cols"), "rows")
    return jax.shard_map(
        local_few if few else local_many, mesh=mesh, in_specs=in_specs, out_specs=out_specs, check_vma=False
    )
```

```python
import functools

import jax
import jax.numpy as jnp
from jax import lax
from jax.experimental import pallas as pl
from jax.experimental.pallas import tpu as pltpu
from jax.sharding import PartitionSpec as P

TILE = 128
GROUP = 8
KEEP = 4
HEAD = 16
STEPS = 8

VMEM = pl.BlockSpec(memory_space=pltpu.VMEM)
SMEM = pl.BlockSpec(memory_space=pltpu.SMEM)
HBM = pl.BlockSpec(memory_space=pltpu.HBM)
PARAMS = pltpu.CompilerParams(vmem_limit_bytes=8 * 1024 * 1024)
ROWS = 4


def cost(flops):
    return pl.CostEstimate(flops=flops, bytes_accessed=1024, transcendentals=0)


def list_kept(kept, row, tiles, places):
    at = jnp.int32(0)
    for tile in range(tiles):
        places[at] = jnp.int32(tile)
        at = at + kept[row, tile]


def pack_kernel(tiles, slots, me, kept, doubles, packed, first, second, table, block, places, sems):
    table_copy = pltpu.make_async_copy(kept, table, sems.at[0])
    block_copy = pltpu.make_async_copy(doubles, block, sems.at[1])
    table_copy.start()
    block_copy.start()
    table_copy.wait()
    list_kept(table, me[0] // ROWS, tiles, places)
    block_copy.wait()
    half = first.shape[0]
    for slot in range(slots):
        tile = block[:, pl.ds(pl.multiple_of(places[slot] * TILE, TILE), TILE)]
        to = slice(slot * TILE, (slot + 1) * TILE)
        packed[:, to] = tile
        first[:, to] = tile[:half]
        second[:, to] = tile[half:]


def prepare_kernel(tiles, slots, me, kept, int_kept, integrals, own, gathered, product, table, int_table, held, places, sems):
    copies = [
        pltpu.make_async_copy(*pair, sems.at[i])
        for i, pair in enumerate(((kept, table), (int_kept, int_table), (integrals, held)))
    ]
    for copy in copies:
        copy.start()
    for copy in copies:
        copy.wait()
    row, col = me[0] // ROWS, me[0] % ROWS
    tiles_ab = integrals.shape[1] // TILE
    for n in range(ROWS):
        list_kept(table, col ^ n, tiles, places)
        for slot in range(slots):
            tile = places[slot]
            start = pl.multiple_of(tile * TILE, TILE)
            for ab in range(tiles_ab):
                part = held[pl.ds(start, TILE), ab * TILE : (ab + 1) * TILE]
                on = (int_table[ab, tile] != 0).astype(jnp.float32).astype(part.dtype)
                gathered[n, slot * TILE : (slot + 1) * TILE, ab * TILE : (ab + 1) * TILE] = part * on
    product[...] = jnp.dot(own[...], gathered[row ^ col], preferred_element_type=jnp.float32)


def after_kernel(token, x, out):
    pass


def encode(x, out):
    pairs, width = x.shape
    largest = jnp.max(jnp.abs(x), axis=0, keepdims=True)
    exponent = jnp.floor((14.95 - jnp.log2(jnp.maximum(largest, 1e-30))) * STEPS)
    code = jnp.round(x * jnp.exp2(exponent * (1.0 / STEPS))).astype(jnp.int32)
    bands = width // TILE
    each = HEAD // bands
    exponent = jnp.broadcast_to(exponent.astype(jnp.int32), (each, width))
    for band in range(bands):
        out[band * pairs : (band + 1) * pairs, :] = code[:, band * TILE : (band + 1) * TILE].astype(jnp.int16)
    head = jnp.concatenate([exponent[:, band * TILE : (band + 1) * TILE] for band in range(bands)], axis=0)
    out[bands * pairs :, :] = head.astype(jnp.int16)


def decode(message, pairs):
    bands = (message.shape[0] - HEAD) // pairs
    each = HEAD // bands
    head = message[bands * pairs :, :].astype(jnp.int32).astype(jnp.float32)
    parts = []
    for band in range(bands):
        scale = jnp.exp2(head[band * each : band * each + 1, :] * (-1.0 / STEPS))
        parts.append(message[band * pairs : (band + 1) * pairs, :].astype(jnp.int32).astype(jnp.float32) * scale)
    return jnp.concatenate(parts, axis=1)


def ladder_kernel(me, product, gathered, pair, near_first, near_second, far_first, far_second, kept_sums, *rest):
    outs, sums = rest[:-1], rest[-1]
    mine = me[0] // ROWS ^ me[0] % ROWS
    half = near_first.shape[0]
    sums[mine] = product[...]
    sums[mine ^ 1] = jnp.dot(pair[...], gathered[mine ^ 1], preferred_element_type=jnp.float32)
    for step, start, block in ((2, 0, near_first), (3, 0, far_first), (2, half, near_second), (3, half, far_second)):
        sums[mine ^ step, start : start + half, :] = jnp.dot(
            block[...], gathered[mine ^ step], preferred_element_type=jnp.float32
        )
    kept_sums[...] = sums[0]
    for n, out in enumerate(outs, 1):
        encode(sums[n], out)


def finish_kernel(residual, kept_sums, *rest):
    messages, out = rest[:-1], rest[-1]
    total = residual[...] + kept_sums[...]
    for message in messages:
        total = total + decode(message, total.shape[0])
    out[...] = total


def after(token, x):
    return pl.pallas_call(
        after_kernel,
        out_shape=jax.ShapeDtypeStruct(x.shape, x.dtype),
        in_specs=[pl.BlockSpec(memory_space=pl.ANY)] * 2,
        out_specs=pl.BlockSpec(memory_space=pl.ANY),
        input_output_aliases={1: 0},
        compiler_params=PARAMS,
        cost_estimate=cost(0),
        name="after",
    )(token, x)


def swap(x, axis, step):
    return lax.ppermute(x, axis, [(i, i ^ step) for i in range(ROWS)])


def local_few(doubles, doubles_kept, integrals, integral_kept, residual):
    me = (lax.axis_index("rows") * ROWS + lax.axis_index("cols")).astype(jnp.int32).reshape(1)
    pairs, cd_local = doubles.shape
    width = integrals.shape[1]
    tiles = cd_local // TILE
    slots = tiles // GROUP * KEEP
    places = pltpu.SMEM((tiles + 1,), jnp.int32)
    sums_shape = jax.ShapeDtypeStruct((pairs, width), jnp.float32)
    half_block = jax.ShapeDtypeStruct((pairs // 2, slots * TILE), doubles.dtype)
    message = jax.ShapeDtypeStruct((pairs * width // TILE + HEAD, TILE), jnp.int16)
    doubles, doubles_kept, integrals, integral_kept = (
        pltpu.with_memory_space_constraint(x, pltpu.HBM) for x in (doubles, doubles_kept, integrals, integral_kept.T)
    )
    packed, first, second = pl.pallas_call(
        functools.partial(pack_kernel, tiles, slots),
        out_shape=[jax.ShapeDtypeStruct((pairs, slots * TILE), doubles.dtype), half_block, half_block],
        in_specs=[SMEM, HBM, HBM],
        out_specs=[VMEM] * 3,
        scratch_shapes=[
            pltpu.SMEM(doubles_kept.shape, jnp.int32),
            pltpu.VMEM(doubles.shape, doubles.dtype),
            places,
            pltpu.SemaphoreType.DMA((2,)),
        ],
        compiler_params=PARAMS,
        name="pack",
    )(me, doubles_kept, doubles)
    near_second = swap(second, "rows", 2)
    pair = swap(packed, "rows", 1)
    far_first = swap(first, "rows", 3)
    near_first = swap(first, "rows", 2)
    near_second = after(pair, near_second)
    far_second = swap(near_second, "rows", 1)
    gathered, product = pl.pallas_call(
        functools.partial(prepare_kernel, tiles, slots),
        out_shape=[jax.ShapeDtypeStruct((ROWS, slots * TILE, width), integrals.dtype), sums_shape],
        in_specs=[SMEM, HBM, HBM, HBM, VMEM],
        out_specs=[VMEM] * 2,
        scratch_shapes=[
            pltpu.SMEM(doubles_kept.shape, jnp.int32),
            pltpu.SMEM(integral_kept.shape, jnp.int32),
            pltpu.VMEM(integrals.shape, integrals.dtype),
            places,
            pltpu.SemaphoreType.DMA((3,)),
        ],
        compiler_params=PARAMS,
        cost_estimate=cost(0),
        name="prepare",
    )(me, doubles_kept, integral_kept, integrals, packed)
    kept_sums, *messages = pl.pallas_call(
        ladder_kernel,
        out_shape=[sums_shape] + [message] * (ROWS - 1),
        in_specs=[SMEM] + [VMEM] * 7,
        out_specs=[VMEM] * ROWS,
        scratch_shapes=[pltpu.VMEM((ROWS, pairs, width), jnp.float32)],
        compiler_params=PARAMS,
        cost_estimate=cost(10**11),
        name="ladder",
    )(me, product, gathered, pair, near_first, near_second, far_first, far_second)
    messages = [swap(x, "cols", step) for step, x in reversed(list(enumerate(messages, 1)))]
    return pl.pallas_call(
        finish_kernel,
        out_shape=sums_shape,
        in_specs=[VMEM] * (ROWS + 1),
        out_specs=VMEM,
        compiler_params=PARAMS,
        name="finish",
    )(residual, kept_sums, *messages)


def local_many(doubles, doubles_kept, integrals, integral_kept, residual):
    pairs, cd_local = doubles.shape
    tiles = cd_local // TILE
    blocks = lax.all_gather(doubles, "rows", axis=0).reshape(-1, pairs, tiles, TILE)
    blocks = blocks * doubles_kept.astype(doubles.dtype)[:, None, :, None]
    tiles_ab = integrals.shape[1] // TILE
    masked = integrals.reshape(tiles, TILE, tiles_ab, TILE) * integral_kept.astype(integrals.dtype)[:, None, :, None]
    sums = jnp.dot(
        blocks.reshape(-1, cd_local), masked.reshape(integrals.shape), preferred_element_type=jnp.float32
    )
    return residual + lax.psum_scatter(sums, "cols", scatter_dimension=0, tiled=True)


def solution(mesh):
    few = mesh.shape["rows"] == mesh.shape["cols"] == ROWS
    in_specs = (
        P(("groups", "rows"), "cols"),
        P("groups", "cols"),
        P(("groups", "cols"), "rows"),
        P(("groups", "cols"), "rows"),
        P(("groups", "cols"), "rows"),
    )
    out_specs = P(("groups", "cols"), "rows")
    return jax.shard_map(
        local_few if few else local_many, mesh=mesh, in_specs=in_specs, out_specs=out_specs, check_vma=False
    )
```

```python
import functools

import jax
import jax.numpy as jnp
from jax import lax
from jax.experimental import pallas as pl
from jax.experimental.pallas import tpu as pltpu
from jax.sharding import PartitionSpec as P

TILE = 128
GROUP = 8
KEEP = 4
HEAD = 16
STEPS = 8

VMEM = pl.BlockSpec(memory_space=pltpu.VMEM)
SMEM = pl.BlockSpec(memory_space=pltpu.SMEM)
HBM = pl.BlockSpec(memory_space=pltpu.HBM)
PARAMS = pltpu.CompilerParams(vmem_limit_bytes=8 * 1024 * 1024)
ROWS = 4


def cost(flops):
    return pl.CostEstimate(flops=flops, bytes_accessed=1024, transcendentals=0)


def list_kept(kept, row, tiles, places):
    at = jnp.int32(0)
    for tile in range(tiles):
        places[at] = jnp.int32(tile)
        at = at + kept[row, tile]


def pack_kernel(tiles, slots, me, kept, doubles, packed, first, second, table, block, places, sems):
    table_copy = pltpu.make_async_copy(kept, table, sems.at[0])
    block_copy = pltpu.make_async_copy(doubles, block, sems.at[1])
    table_copy.start()
    block_copy.start()
    table_copy.wait()
    list_kept(table, me[0] // ROWS, tiles, places)
    block_copy.wait()
    half = first.shape[0]
    for slot in range(slots):
        tile = block[:, pl.ds(pl.multiple_of(places[slot] * TILE, TILE), TILE)]
        to = slice(slot * TILE, (slot + 1) * TILE)
        packed[:, to] = tile
        first[:, to] = tile[:half]
        second[:, to] = tile[half:]


def prepare_kernel(tiles, slots, me, kept, int_kept, integrals, own, gathered, product, table, int_table, held, places, sems):
    copies = [
        pltpu.make_async_copy(*pair, sems.at[i])
        for i, pair in enumerate(((kept, table), (int_kept, int_table), (integrals, held)))
    ]
    for copy in copies:
        copy.start()
    for copy in copies:
        copy.wait()
    row, col = me[0] // ROWS, me[0] % ROWS
    tiles_ab = integrals.shape[1] // TILE
    for n in range(ROWS):
        list_kept(table, col ^ n, tiles, places)
        for slot in range(slots):
            tile = places[slot]
            start = pl.multiple_of(tile * TILE, TILE)
            for ab in range(tiles_ab):
                part = held[pl.ds(start, TILE), ab * TILE : (ab + 1) * TILE]
                on = (int_table[ab, tile] != 0).astype(jnp.float32).astype(part.dtype)
                gathered[n, slot * TILE : (slot + 1) * TILE, ab * TILE : (ab + 1) * TILE] = part * on
    product[...] = jnp.dot(own[...], gathered[row ^ col], preferred_element_type=jnp.float32)


def after_kernel(token, x, out):
    pass


def encode(x, out):
    pairs, width = x.shape
    largest = jnp.max(jnp.abs(x), axis=0, keepdims=True)
    exponent = jnp.floor((14.95 - jnp.log2(jnp.maximum(largest, 1e-30))) * STEPS)
    code = jnp.round(x * jnp.exp2(exponent * (1.0 / STEPS))).astype(jnp.int32)
    bands = width // TILE
    each = HEAD // bands
    exponent = jnp.broadcast_to(exponent.astype(jnp.int32), (each, width))
    for band in range(bands):
        out[band * pairs : (band + 1) * pairs, :] = code[:, band * TILE : (band + 1) * TILE].astype(jnp.int16)
    head = jnp.concatenate([exponent[:, band * TILE : (band + 1) * TILE] for band in range(bands)], axis=0)
    out[bands * pairs :, :] = head.astype(jnp.int16)


def decode(message, pairs):
    bands = (message.shape[0] - HEAD) // pairs
    each = HEAD // bands
    head = message[bands * pairs :, :].astype(jnp.int32).astype(jnp.float32)
    parts = []
    for band in range(bands):
        scale = jnp.exp2(head[band * each : band * each + 1, :] * (-1.0 / STEPS))
        parts.append(message[band * pairs : (band + 1) * pairs, :].astype(jnp.int32).astype(jnp.float32) * scale)
    return jnp.concatenate(parts, axis=1)


def ladder_kernel(start, me, product, gathered, pair, far, near, kept_sums, *rest):
    outs, sums = rest[:-1], rest[-1]
    mine = me[0] // ROWS ^ me[0] % ROWS
    part = slice(start, start + near.shape[0])
    sums[mine] = product[part, :]
    for step, block in enumerate((pair[part, :], near[...], far[...]), 1):
        sums[mine ^ step] = jnp.dot(block, gathered[mine ^ step], preferred_element_type=jnp.float32)
    kept_sums[...] = sums[0]
    for n, out in enumerate(outs, 1):
        encode(sums[n], out)


def finish_kernel(start, base, kept_sums, *rest):
    messages, out = rest[:-1], rest[-1]
    half = kept_sums.shape[0]
    part, other = slice(start, start + half), slice(half - start, 2 * half - start)
    total = base[part, :] + kept_sums[...]
    for message in messages:
        total = total + decode(message, half)
    out[part, :] = total
    out[other, :] = base[other, :]


def after(token, x):
    return pl.pallas_call(
        after_kernel,
        out_shape=jax.ShapeDtypeStruct(x.shape, x.dtype),
        in_specs=[pl.BlockSpec(memory_space=pl.ANY)] * 2,
        out_specs=pl.BlockSpec(memory_space=pl.ANY),
        input_output_aliases={1: 0},
        compiler_params=PARAMS,
        cost_estimate=cost(4 * 10**8),
        name="after",
    )(token, x)


def swap(x, axis, step):
    return lax.ppermute(x, axis, [(i, i ^ step) for i in range(ROWS)])


def local_few(doubles, doubles_kept, integrals, integral_kept, residual):
    me = (lax.axis_index("rows") * ROWS + lax.axis_index("cols")).astype(jnp.int32).reshape(1)
    pairs, cd_local = doubles.shape
    width = integrals.shape[1]
    tiles = cd_local // TILE
    slots = tiles // GROUP * KEEP
    places = pltpu.SMEM((tiles + 1,), jnp.int32)
    sums_shape = jax.ShapeDtypeStruct((pairs, width), jnp.float32)
    half_block = jax.ShapeDtypeStruct((pairs // 2, slots * TILE), doubles.dtype)
    half_sums = jax.ShapeDtypeStruct((pairs // 2, width), jnp.float32)
    message = jax.ShapeDtypeStruct((pairs // 2 * width // TILE + HEAD, TILE), jnp.int16)
    doubles, doubles_kept, integrals, integral_kept = (
        pltpu.with_memory_space_constraint(x, pltpu.HBM) for x in (doubles, doubles_kept, integrals, integral_kept.T)
    )
    packed, first, second = pl.pallas_call(
        functools.partial(pack_kernel, tiles, slots),
        out_shape=[jax.ShapeDtypeStruct((pairs, slots * TILE), doubles.dtype), half_block, half_block],
        in_specs=[SMEM, HBM, HBM],
        out_specs=[VMEM] * 3,
        scratch_shapes=[
            pltpu.SMEM(doubles_kept.shape, jnp.int32),
            pltpu.VMEM(doubles.shape, doubles.dtype),
            places,
            pltpu.SemaphoreType.DMA((2,)),
        ],
        compiler_params=PARAMS,
        name="pack",
    )(me, doubles_kept, doubles)
    near_second = swap(second, "rows", 2)
    pair = swap(packed, "rows", 1)
    far_first = swap(first, "rows", 3)
    near_first = swap(first, "rows", 2)
    near_second = after(packed, near_second)
    far_second = swap(near_second, "rows", 1)
    gathered, product = pl.pallas_call(
        functools.partial(prepare_kernel, tiles, slots),
        out_shape=[jax.ShapeDtypeStruct((ROWS, slots * TILE, width), integrals.dtype), sums_shape],
        in_specs=[SMEM, HBM, HBM, HBM, VMEM],
        out_specs=[VMEM] * 2,
        scratch_shapes=[
            pltpu.SMEM(doubles_kept.shape, jnp.int32),
            pltpu.SMEM(integral_kept.shape, jnp.int32),
            pltpu.VMEM(integrals.shape, integrals.dtype),
            places,
            pltpu.SemaphoreType.DMA((3,)),
        ],
        compiler_params=PARAMS,
        cost_estimate=cost(0),
        name="prepare",
    )(me, doubles_kept, integral_kept, integrals, packed)
    total = residual
    for start, near, far in ((0, near_first, far_first), (pairs // 2, near_second, far_second)):
        kept_sums, *messages = pl.pallas_call(
            functools.partial(ladder_kernel, start),
            out_shape=[half_sums] + [message] * (ROWS - 1),
            in_specs=[SMEM] + [VMEM] * 5,
            out_specs=[VMEM] * ROWS,
            scratch_shapes=[pltpu.VMEM((ROWS,) + half_sums.shape, jnp.float32)],
            compiler_params=PARAMS,
            cost_estimate=cost(10**11 if start else 0),
            name="ladder",
        )(me, product, gathered, pair, far, near)
        messages = [swap(x, "cols", step) for step, x in reversed(list(enumerate(messages, 1)))]
        total = pl.pallas_call(
            functools.partial(finish_kernel, start),
            out_shape=sums_shape,
            in_specs=[VMEM] * (ROWS + 1),
            out_specs=VMEM,
            compiler_params=PARAMS,
            name="finish",
        )(total, kept_sums, *messages)
    return total


def local_many(doubles, doubles_kept, integrals, integral_kept, residual):
    pairs, cd_local = doubles.shape
    tiles = cd_local // TILE
    blocks = lax.all_gather(doubles, "rows", axis=0).reshape(-1, pairs, tiles, TILE)
    blocks = blocks * doubles_kept.astype(doubles.dtype)[:, None, :, None]
    tiles_ab = integrals.shape[1] // TILE
    masked = integrals.reshape(tiles, TILE, tiles_ab, TILE) * integral_kept.astype(integrals.dtype)[:, None, :, None]
    sums = jnp.dot(
        blocks.reshape(-1, cd_local), masked.reshape(integrals.shape), preferred_element_type=jnp.float32
    )
    return residual + lax.psum_scatter(sums, "cols", scatter_dimension=0, tiled=True)


def solution(mesh):
    few = mesh.shape["rows"] == mesh.shape["cols"] == ROWS
    in_specs = (
        P(("groups", "rows"), "cols"),
        P("groups", "cols"),
        P(("groups", "cols"), "rows"),
        P(("groups", "cols"), "rows"),
        P(("groups", "cols"), "rows"),
    )
    out_specs = P(("groups", "cols"), "rows")
    return jax.shard_map(
        local_few if few else local_many, mesh=mesh, in_specs=in_specs, out_specs=out_specs, check_vma=False
    )
```

```python
import functools

import jax
import jax.numpy as jnp
from jax import lax
from jax.experimental import pallas as pl
from jax.experimental.pallas import tpu as pltpu
from jax.sharding import PartitionSpec as P

TILE = 128
GROUP = 8
KEEP = 4
HEAD = 16
STEPS = 8

VMEM = pl.BlockSpec(memory_space=pltpu.VMEM)
SMEM = pl.BlockSpec(memory_space=pltpu.SMEM)
HBM = pl.BlockSpec(memory_space=pltpu.HBM)
PARAMS = pltpu.CompilerParams(vmem_limit_bytes=8 * 1024 * 1024)
ROWS = 4


def cost(flops):
    return pl.CostEstimate(flops=flops, bytes_accessed=1024, transcendentals=0)


def list_kept(kept, row, tiles, places):
    at = jnp.int32(0)
    for tile in range(tiles):
        places[at] = jnp.int32(tile)
        at = at + kept[row, tile]


def pack_kernel(tiles, slots, me, kept, doubles, packed, first, second, table, block, places, sems):
    table_copy = pltpu.make_async_copy(kept, table, sems.at[0])
    block_copy = pltpu.make_async_copy(doubles, block, sems.at[1])
    table_copy.start()
    block_copy.start()
    table_copy.wait()
    list_kept(table, me[0] // ROWS, tiles, places)
    block_copy.wait()
    half = first.shape[0]
    for slot in range(slots):
        tile = block[:, pl.ds(pl.multiple_of(places[slot] * TILE, TILE), TILE)]
        to = slice(slot * TILE, (slot + 1) * TILE)
        packed[:, to] = tile
        first[:, to] = tile[:half]
        second[:, to] = tile[half:]


def prepare_kernel(tiles, slots, me, kept, int_kept, integrals, own, gathered, product, table, int_table, held, places, sems):
    copies = [
        pltpu.make_async_copy(*pair, sems.at[i])
        for i, pair in enumerate(((kept, table), (int_kept, int_table), (integrals, held)))
    ]
    for copy in copies:
        copy.start()
    for copy in copies:
        copy.wait()
    row, col = me[0] // ROWS, me[0] % ROWS
    tiles_ab = integrals.shape[1] // TILE
    for n in range(ROWS):
        list_kept(table, col ^ n, tiles, places)
        for slot in range(slots):
            tile = places[slot]
            start = pl.multiple_of(tile * TILE, TILE)
            for ab in range(tiles_ab):
                part = held[pl.ds(start, TILE), ab * TILE : (ab + 1) * TILE]
                on = (int_table[ab, tile] != 0).astype(jnp.float32).astype(part.dtype)
                gathered[n, slot * TILE : (slot + 1) * TILE, ab * TILE : (ab + 1) * TILE] = part * on
    product[...] = jnp.dot(own[...], gathered[row ^ col], preferred_element_type=jnp.float32)


def encode(x, out):
    pairs, width = x.shape
    largest = jnp.max(jnp.abs(x), axis=0, keepdims=True)
    exponent = jnp.floor((14.95 - jnp.log2(jnp.maximum(largest, 1e-30))) * STEPS)
    code = jnp.round(x * jnp.exp2(exponent * (1.0 / STEPS))).astype(jnp.int32)
    bands = width // TILE
    each = HEAD // bands
    exponent = jnp.broadcast_to(exponent.astype(jnp.int32), (each, width))
    for band in range(bands):
        out[band * pairs : (band + 1) * pairs, :] = code[:, band * TILE : (band + 1) * TILE].astype(jnp.int16)
    head = jnp.concatenate([exponent[:, band * TILE : (band + 1) * TILE] for band in range(bands)], axis=0)
    out[bands * pairs :, :] = head.astype(jnp.int16)


def decode(message, pairs):
    bands = (message.shape[0] - HEAD) // pairs
    each = HEAD // bands
    head = message[bands * pairs :, :].astype(jnp.int32).astype(jnp.float32)
    parts = []
    for band in range(bands):
        scale = jnp.exp2(head[band * each : band * each + 1, :] * (-1.0 / STEPS))
        parts.append(message[band * pairs : (band + 1) * pairs, :].astype(jnp.int32).astype(jnp.float32) * scale)
    return jnp.concatenate(parts, axis=1)


def ladder_kernel(me, product, gathered, pair, near_first, near_second, far_first, far_second, kept_sums, *rest):
    outs, sums = rest[:-1], rest[-1]
    mine = me[0] // ROWS ^ me[0] % ROWS
    half = near_first.shape[0]
    sums[mine] = product[...]
    sums[mine ^ 1] = jnp.dot(pair[...], gathered[mine ^ 1], preferred_element_type=jnp.float32)
    for step, start, block in ((2, 0, near_first), (3, 0, far_first), (2, half, near_second), (3, half, far_second)):
        sums[mine ^ step, start : start + half, :] = jnp.dot(
            block[...], gathered[mine ^ step], preferred_element_type=jnp.float32
        )
    kept_sums[...] = sums[0]
    for n, out in enumerate(outs, 1):
        encode(sums[n], out)


def finish_kernel(residual, kept_sums, *rest):
    messages, out = rest[:-1], rest[-1]
    total = residual[...] + kept_sums[...]
    for message in messages:
        total = total + decode(message, total.shape[0])
    out[...] = total


def swap(x, axis, step):
    return lax.ppermute(x, axis, [(i, i ^ step) for i in range(ROWS)])


def local_few(doubles, doubles_kept, integrals, integral_kept, residual):
    me = (lax.axis_index("rows") * ROWS + lax.axis_index("cols")).astype(jnp.int32).reshape(1)
    pairs, cd_local = doubles.shape
    width = integrals.shape[1]
    tiles = cd_local // TILE
    slots = tiles // GROUP * KEEP
    places = pltpu.SMEM((tiles + 1,), jnp.int32)
    sums_shape = jax.ShapeDtypeStruct((pairs, width), jnp.float32)
    half_block = jax.ShapeDtypeStruct((pairs // 2, slots * TILE), doubles.dtype)
    message = jax.ShapeDtypeStruct((pairs * width // TILE + HEAD, TILE), jnp.int16)
    doubles, doubles_kept, integrals, integral_kept = (
        pltpu.with_memory_space_constraint(x, pltpu.HBM) for x in (doubles, doubles_kept, integrals, integral_kept.T)
    )
    packed, first, second = pl.pallas_call(
        functools.partial(pack_kernel, tiles, slots),
        out_shape=[jax.ShapeDtypeStruct((pairs, slots * TILE), doubles.dtype), half_block, half_block],
        in_specs=[SMEM, HBM, HBM],
        out_specs=[VMEM] * 3,
        scratch_shapes=[
            pltpu.SMEM(doubles_kept.shape, jnp.int32),
            pltpu.VMEM(doubles.shape, doubles.dtype),
            places,
            pltpu.SemaphoreType.DMA((2,)),
        ],
        compiler_params=PARAMS,
        name="pack",
    )(me, doubles_kept, doubles)
    near_second = swap(second, "rows", 2)
    pair = swap(packed, "rows", 1)
    far_first = swap(first, "rows", 3)
    near_first = swap(first, "rows", 2)
    far_second = swap(near_second, "rows", 1)
    gathered, product = pl.pallas_call(
        functools.partial(prepare_kernel, tiles, slots),
        out_shape=[jax.ShapeDtypeStruct((ROWS, slots * TILE, width), integrals.dtype), sums_shape],
        in_specs=[SMEM, HBM, HBM, HBM, VMEM],
        out_specs=[VMEM] * 2,
        scratch_shapes=[
            pltpu.SMEM(doubles_kept.shape, jnp.int32),
            pltpu.SMEM(integral_kept.shape, jnp.int32),
            pltpu.VMEM(integrals.shape, integrals.dtype),
            places,
            pltpu.SemaphoreType.DMA((3,)),
        ],
        compiler_params=PARAMS,
        cost_estimate=cost(0),
        name="prepare",
    )(me, doubles_kept, integral_kept, integrals, packed)
    kept_sums, *messages = pl.pallas_call(
        ladder_kernel,
        out_shape=[sums_shape] + [message] * (ROWS - 1),
        in_specs=[SMEM] + [VMEM] * 7,
        out_specs=[VMEM] * ROWS,
        scratch_shapes=[pltpu.VMEM((ROWS, pairs, width), jnp.float32)],
        compiler_params=PARAMS,
        cost_estimate=cost(10**11),
        name="ladder",
    )(me, product, gathered, pair, near_first, near_second, far_first, far_second)
    messages = [swap(messages[step - 1], "cols", step) for step in (2, 3, 1)]
    return pl.pallas_call(
        finish_kernel,
        out_shape=sums_shape,
        in_specs=[VMEM] * (ROWS + 1),
        out_specs=VMEM,
        compiler_params=PARAMS,
        name="finish",
    )(residual, kept_sums, *messages)


def local_many(doubles, doubles_kept, integrals, integral_kept, residual):
    pairs, cd_local = doubles.shape
    tiles = cd_local // TILE
    blocks = lax.all_gather(doubles, "rows", axis=0).reshape(-1, pairs, tiles, TILE)
    blocks = blocks * doubles_kept.astype(doubles.dtype)[:, None, :, None]
    tiles_ab = integrals.shape[1] // TILE
    masked = integrals.reshape(tiles, TILE, tiles_ab, TILE) * integral_kept.astype(integrals.dtype)[:, None, :, None]
    sums = jnp.dot(
        blocks.reshape(-1, cd_local), masked.reshape(integrals.shape), preferred_element_type=jnp.float32
    )
    return residual + lax.psum_scatter(sums, "cols", scatter_dimension=0, tiled=True)


def solution(mesh):
    few = mesh.shape["rows"] == mesh.shape["cols"] == ROWS
    in_specs = (
        P(("groups", "rows"), "cols"),
        P("groups", "cols"),
        P(("groups", "cols"), "rows"),
        P(("groups", "cols"), "rows"),
        P(("groups", "cols"), "rows"),
    )
    out_specs = P(("groups", "cols"), "rows")
    return jax.shard_map(
        local_few if few else local_many, mesh=mesh, in_specs=in_specs, out_specs=out_specs, check_vma=False
    )
```

```python
import functools

import jax
import jax.numpy as jnp
from jax import lax
from jax.experimental import pallas as pl
from jax.experimental.pallas import tpu as pltpu
from jax.sharding import PartitionSpec as P

TILE = 128
GROUP = 8
KEEP = 4
HEAD = 16
STEPS = 8

VMEM = pl.BlockSpec(memory_space=pltpu.VMEM)
HBM = pl.BlockSpec(memory_space=pltpu.HBM)
PARAMS = pltpu.CompilerParams(vmem_limit_bytes=8 * 1024 * 1024)
ROWS = 4


def cost(flops):
    return pl.CostEstimate(flops=flops, bytes_accessed=1024, transcendentals=0)


def list_kept(kept, row, tiles, places):
    at = jnp.int32(0)
    for tile in range(tiles):
        places[at] = jnp.int32(tile)
        at = at + kept[row, tile]


def pack_kernel(tiles, slots, kept, doubles, packed, first, second, table, block, places, sems):
    table_copy = pltpu.make_async_copy(kept, table, sems.at[0])
    block_copy = pltpu.make_async_copy(doubles, block, sems.at[1])
    table_copy.start()
    block_copy.start()
    table_copy.wait()
    list_kept(table, lax.axis_index("rows"), tiles, places)
    block_copy.wait()
    half = first.shape[0]
    for slot in range(slots):
        tile = block[:, pl.ds(pl.multiple_of(places[slot] * TILE, TILE), TILE)]
        to = slice(slot * TILE, (slot + 1) * TILE)
        packed[:, to] = tile
        first[:, to] = tile[:half]
        second[:, to] = tile[half:]


def prepare_kernel(tiles, slots, kept, int_kept, integrals, own, gathered, product, table, int_table, held, places, sems):
    copies = [
        pltpu.make_async_copy(*pair, sems.at[i])
        for i, pair in enumerate(((kept, table), (int_kept, int_table), (integrals, held)))
    ]
    for copy in copies:
        copy.start()
    for copy in copies:
        copy.wait()
    row, col = lax.axis_index("rows"), lax.axis_index("cols")
    tiles_ab = integrals.shape[1] // TILE
    for n in range(ROWS):
        list_kept(table, col ^ n, tiles, places)
        for slot in range(slots):
            tile = places[slot]
            start = pl.multiple_of(tile * TILE, TILE)
            for ab in range(tiles_ab):
                part = held[pl.ds(start, TILE), ab * TILE : (ab + 1) * TILE]
                on = (int_table[ab, tile] != 0).astype(jnp.float32).astype(part.dtype)
                gathered[n, slot * TILE : (slot + 1) * TILE, ab * TILE : (ab + 1) * TILE] = part * on
    product[...] = jnp.dot(own[...], gathered[row ^ col], preferred_element_type=jnp.float32)


def encode(x, out):
    pairs, width = x.shape
    largest = jnp.max(jnp.abs(x), axis=0, keepdims=True)
    exponent = jnp.floor((14.95 - jnp.log2(jnp.maximum(largest, 1e-30))) * STEPS)
    code = jnp.round(x * jnp.exp2(exponent * (1.0 / STEPS))).astype(jnp.int32)
    bands = width // TILE
    each = HEAD // bands
    exponent = jnp.broadcast_to(exponent.astype(jnp.int32), (each, width))
    for band in range(bands):
        out[band * pairs : (band + 1) * pairs, :] = code[:, band * TILE : (band + 1) * TILE].astype(jnp.int16)
    head = jnp.concatenate([exponent[:, band * TILE : (band + 1) * TILE] for band in range(bands)], axis=0)
    out[bands * pairs :, :] = head.astype(jnp.int16)


def decode(message, pairs):
    bands = (message.shape[0] - HEAD) // pairs
    each = HEAD // bands
    head = message[bands * pairs :, :].astype(jnp.int32).astype(jnp.float32)
    parts = []
    for band in range(bands):
        scale = jnp.exp2(head[band * each : band * each + 1, :] * (-1.0 / STEPS))
        parts.append(message[band * pairs : (band + 1) * pairs, :].astype(jnp.int32).astype(jnp.float32) * scale)
    return jnp.concatenate(parts, axis=1)


def ladder_kernel(product, gathered, pair, near_first, near_second, far_first, far_second, kept_sums, *rest):
    outs, sums = rest[:-1], rest[-1]
    mine = lax.axis_index("rows") ^ lax.axis_index("cols")
    half = near_first.shape[0]
    sums[mine] = product[...]
    sums[mine ^ 1] = jnp.dot(pair[...], gathered[mine ^ 1], preferred_element_type=jnp.float32)
    for step, start, block in ((2, 0, near_first), (3, 0, far_first), (2, half, near_second), (3, half, far_second)):
        sums[mine ^ step, start : start + half, :] = jnp.dot(
            block[...], gathered[mine ^ step], preferred_element_type=jnp.float32
        )
    kept_sums[...] = sums[0]
    for n, out in enumerate(outs, 1):
        encode(sums[n], out)


def finish_kernel(residual, kept_sums, *rest):
    messages, out = rest[:-1], rest[-1]
    total = residual[...] + kept_sums[...]
    for message in messages:
        total = total + decode(message, total.shape[0])
    out[...] = total


def swap(x, axis, step):
    return lax.ppermute(x, axis, [(i, i ^ step) for i in range(ROWS)])


def local_few(doubles, doubles_kept, integrals, integral_kept, residual):
    pairs, cd_local = doubles.shape
    width = integrals.shape[1]
    tiles = cd_local // TILE
    slots = tiles // GROUP * KEEP
    places = pltpu.SMEM((tiles + 1,), jnp.int32)
    sums_shape = jax.ShapeDtypeStruct((pairs, width), jnp.float32)
    half_block = jax.ShapeDtypeStruct((pairs // 2, slots * TILE), doubles.dtype)
    message = jax.ShapeDtypeStruct((pairs * width // TILE + HEAD, TILE), jnp.int16)
    doubles, doubles_kept, integrals, integral_kept = (
        pltpu.with_memory_space_constraint(x, pltpu.HBM) for x in (doubles, doubles_kept, integrals, integral_kept.T)
    )
    packed, first, second = pl.pallas_call(
        functools.partial(pack_kernel, tiles, slots),
        out_shape=[jax.ShapeDtypeStruct((pairs, slots * TILE), doubles.dtype), half_block, half_block],
        in_specs=[HBM, HBM],
        out_specs=[VMEM] * 3,
        scratch_shapes=[
            pltpu.SMEM(doubles_kept.shape, jnp.int32),
            pltpu.VMEM(doubles.shape, doubles.dtype),
            places,
            pltpu.SemaphoreType.DMA((2,)),
        ],
        compiler_params=PARAMS,
        name="pack",
    )(doubles_kept, doubles)
    near_second = swap(second, "rows", 2)
    pair = swap(packed, "rows", 1)
    far_first = swap(first, "rows", 3)
    near_first = swap(first, "rows", 2)
    far_second = swap(near_second, "rows", 1)
    gathered, product = pl.pallas_call(
        functools.partial(prepare_kernel, tiles, slots),
        out_shape=[jax.ShapeDtypeStruct((ROWS, slots * TILE, width), integrals.dtype), sums_shape],
        in_specs=[HBM, HBM, HBM, VMEM],
        out_specs=[VMEM] * 2,
        scratch_shapes=[
            pltpu.SMEM(doubles_kept.shape, jnp.int32),
            pltpu.SMEM(integral_kept.shape, jnp.int32),
            pltpu.VMEM(integrals.shape, integrals.dtype),
            places,
            pltpu.SemaphoreType.DMA((3,)),
        ],
        compiler_params=PARAMS,
        cost_estimate=cost(0),
        name="prepare",
    )(doubles_kept, integral_kept, integrals, packed)
    kept_sums, *messages = pl.pallas_call(
        ladder_kernel,
        out_shape=[sums_shape] + [message] * (ROWS - 1),
        in_specs=[VMEM] * 7,
        out_specs=[VMEM] * ROWS,
        scratch_shapes=[pltpu.VMEM((ROWS, pairs, width), jnp.float32)],
        compiler_params=PARAMS,
        cost_estimate=cost(10**11),
        name="ladder",
    )(product, gathered, pair, near_first, near_second, far_first, far_second)
    messages = [swap(messages[step - 1], "cols", step) for step in (2, 3, 1)]
    return pl.pallas_call(
        finish_kernel,
        out_shape=sums_shape,
        in_specs=[VMEM] * (ROWS + 1),
        out_specs=VMEM,
        compiler_params=PARAMS,
        name="finish",
    )(residual, kept_sums, *messages)


def local_many(doubles, doubles_kept, integrals, integral_kept, residual):
    pairs, cd_local = doubles.shape
    tiles = cd_local // TILE
    blocks = lax.all_gather(doubles, "rows", axis=0).reshape(-1, pairs, tiles, TILE)
    blocks = blocks * doubles_kept.astype(doubles.dtype)[:, None, :, None]
    tiles_ab = integrals.shape[1] // TILE
    masked = integrals.reshape(tiles, TILE, tiles_ab, TILE) * integral_kept.astype(integrals.dtype)[:, None, :, None]
    sums = jnp.dot(
        blocks.reshape(-1, cd_local), masked.reshape(integrals.shape), preferred_element_type=jnp.float32
    )
    return residual + lax.psum_scatter(sums, "cols", scatter_dimension=0, tiled=True)


def solution(mesh):
    few = mesh.shape["rows"] == mesh.shape["cols"] == ROWS
    in_specs = (
        P(("groups", "rows"), "cols"),
        P("groups", "cols"),
        P(("groups", "cols"), "rows"),
        P(("groups", "cols"), "rows"),
        P(("groups", "cols"), "rows"),
    )
    out_specs = P(("groups", "cols"), "rows")
    return jax.shard_map(
        local_few if few else local_many, mesh=mesh, in_specs=in_specs, out_specs=out_specs, check_vma=False
    )
```

```python
import functools

import jax
import jax.numpy as jnp
from jax import lax
from jax.experimental import pallas as pl
from jax.experimental.pallas import tpu as pltpu
from jax.sharding import PartitionSpec as P

TILE = 128
GROUP = 8
KEEP = 4
HEAD = 16
STEPS = 8

VMEM = pl.BlockSpec(memory_space=pltpu.VMEM)
HBM = pl.BlockSpec(memory_space=pltpu.HBM)
PARAMS = pltpu.CompilerParams(vmem_limit_bytes=8 * 1024 * 1024)
ROWS = 4


def cost(flops):
    return pl.CostEstimate(flops=flops, bytes_accessed=1024, transcendentals=0)


def list_kept(kept, row, tiles, places):
    at = jnp.int32(0)
    for tile in range(tiles):
        places[at] = jnp.int32(tile)
        at = at + kept[row, tile]


def pack_kernel(tiles, slots, kept, doubles, packed, first, second, table, block, places, sems):
    table_copy = pltpu.make_async_copy(kept, table, sems.at[0])
    block_copy = pltpu.make_async_copy(doubles, block, sems.at[1])
    table_copy.start()
    block_copy.start()
    table_copy.wait()
    list_kept(table, lax.axis_index("rows"), tiles, places)
    block_copy.wait()
    half = first.shape[0]
    for slot in range(slots):
        tile = block[:, pl.ds(pl.multiple_of(places[slot] * TILE, TILE), TILE)]
        to = slice(slot * TILE, (slot + 1) * TILE)
        packed[:, to] = tile
        first[:, to] = tile[:half]
        second[:, to] = tile[half:]


def prepare_kernel(tiles, slots, kept, int_kept, integrals, own, gathered, product, table, int_table, held, places, sems):
    copies = [
        pltpu.make_async_copy(*pair, sems.at[i])
        for i, pair in enumerate(((kept, table), (int_kept, int_table), (integrals, held)))
    ]
    for copy in copies:
        copy.start()
    for copy in copies:
        copy.wait()
    row, col = lax.axis_index("rows"), lax.axis_index("cols")
    tiles_ab = integrals.shape[1] // TILE
    for n in range(ROWS):
        list_kept(table, col ^ n, tiles, places)
        for slot in range(slots):
            tile = places[slot]
            start = pl.multiple_of(tile * TILE, TILE)
            for ab in range(tiles_ab):
                part = held[pl.ds(start, TILE), ab * TILE : (ab + 1) * TILE]
                on = (int_table[ab, tile] != 0).astype(jnp.float32).astype(part.dtype)
                gathered[n, slot * TILE : (slot + 1) * TILE, ab * TILE : (ab + 1) * TILE] = part * on
    product[...] = jnp.dot(own[...], gathered[row ^ col], preferred_element_type=jnp.float32)


def encode(x, out):
    pairs, width = x.shape
    largest = jnp.max(jnp.abs(x), axis=0, keepdims=True)
    exponent = jnp.floor((14.95 - jnp.log2(jnp.maximum(largest, 1e-30))) * STEPS)
    code = jnp.round(x * jnp.exp2(exponent * (1.0 / STEPS))).astype(jnp.int32)
    bands = width // TILE
    each = HEAD // bands
    exponent = jnp.broadcast_to(exponent.astype(jnp.int32), (each, width))
    for band in range(bands):
        out[band * pairs : (band + 1) * pairs, :] = code[:, band * TILE : (band + 1) * TILE].astype(jnp.int16)
    head = jnp.concatenate([exponent[:, band * TILE : (band + 1) * TILE] for band in range(bands)], axis=0)
    out[bands * pairs :, :] = head.astype(jnp.int16)


def decode(message, pairs):
    bands = (message.shape[0] - HEAD) // pairs
    each = HEAD // bands
    head = message[bands * pairs :, :].astype(jnp.int32).astype(jnp.float32)
    parts = []
    for band in range(bands):
        scale = jnp.exp2(head[band * each : band * each + 1, :] * (-1.0 / STEPS))
        parts.append(message[band * pairs : (band + 1) * pairs, :].astype(jnp.int32).astype(jnp.float32) * scale)
    return jnp.concatenate(parts, axis=1)


def half_of(ref, half):
    size = ref.shape[0] // 2
    return ref.at[pl.ds(pl.multiple_of(half * size, size), size)]


def early_half(step):
    return 1 - step % 2


def half_sums(late, product, gathered, pair, near, far, sums):
    mine = lax.axis_index("rows") ^ lax.axis_index("cols")
    half = product.shape[0] // 2
    rows = [slice(h * half, (h + 1) * half) for h in (early_half(step) ^ late for step in range(2))]
    sums[mine] = product[rows[0], :]
    for step, block in enumerate((pair[rows[1], :], near[...], far[...]), 1):
        sums[mine ^ step] = jnp.dot(block, gathered[mine ^ step], preferred_element_type=jnp.float32)


def early_kernel(product, gathered, pair, near, far, own_sums, core_sums, two, three, sums):
    half_sums(0, product, gathered, pair, near, far, sums)
    own_sums[...] = sums[0]
    core_sums[...] = sums[1]
    encode(sums[2], two)
    encode(sums[3], three)


def late_kernel(core_sums, product, gathered, pair, near, far, own_sums, one, two, three, sums):
    half_sums(1, product, gathered, pair, near, far, sums)
    own_sums[...] = sums[0]
    encode(sums[2], two)
    encode(sums[3], three)
    encode(core_sums[...], half_of(one, 0))
    encode(sums[1], half_of(one, 1))


def first_kernel(residual, own_sums, two, three, out):
    early = early_half(lax.axis_index("rows") ^ lax.axis_index("cols"))
    half = own_sums.shape[0]
    total = half_of(residual, early)[...] + own_sums[...]
    half_of(out, early)[...] = total + decode(two, half) + decode(three, half)
    half_of(out, 1 - early)[...] = half_of(residual, 1 - early)[...]


def last_kernel(base, own_sums, two, three, one, out):
    early = early_half(lax.axis_index("rows") ^ lax.axis_index("cols"))
    half = own_sums.shape[0]
    half_of(out, early)[...] = half_of(base, early)[...] + decode(half_of(one, 0), half)
    total = half_of(base, 1 - early)[...] + own_sums[...] + decode(half_of(one, 1), half)
    half_of(out, 1 - early)[...] = total + decode(two, half) + decode(three, half)


def swap(x, axis, step):
    return lax.ppermute(x, axis, [(i, i ^ step) for i in range(ROWS)])


def local_few(doubles, doubles_kept, integrals, integral_kept, residual):
    pairs, cd_local = doubles.shape
    width = integrals.shape[1]
    tiles = cd_local // TILE
    slots = tiles // GROUP * KEEP
    places = pltpu.SMEM((tiles + 1,), jnp.int32)
    sums_shape = jax.ShapeDtypeStruct((pairs, width), jnp.float32)
    half_block = jax.ShapeDtypeStruct((pairs // 2, slots * TILE), doubles.dtype)
    half_shape = jax.ShapeDtypeStruct((pairs // 2, width), jnp.float32)
    message = jax.ShapeDtypeStruct((pairs // 2 * width // TILE + HEAD, TILE), jnp.int16)
    double = jax.ShapeDtypeStruct((2 * message.shape[0], TILE), jnp.int16)
    doubles, doubles_kept, integrals, integral_kept = (
        pltpu.with_memory_space_constraint(x, pltpu.HBM) for x in (doubles, doubles_kept, integrals, integral_kept.T)
    )
    packed, first, second = pl.pallas_call(
        functools.partial(pack_kernel, tiles, slots),
        out_shape=[jax.ShapeDtypeStruct((pairs, slots * TILE), doubles.dtype), half_block, half_block],
        in_specs=[HBM, HBM],
        out_specs=[VMEM] * 3,
        scratch_shapes=[
            pltpu.SMEM(doubles_kept.shape, jnp.int32),
            pltpu.VMEM(doubles.shape, doubles.dtype),
            places,
            pltpu.SemaphoreType.DMA((2,)),
        ],
        compiler_params=PARAMS,
        name="pack",
    )(doubles_kept, doubles)
    near_second = swap(second, "rows", 2)
    pair = swap(packed, "rows", 1)
    far_first = swap(first, "rows", 3)
    near_first = swap(first, "rows", 2)
    far_second = swap(near_second, "rows", 1)
    gathered, product = pl.pallas_call(
        functools.partial(prepare_kernel, tiles, slots),
        out_shape=[jax.ShapeDtypeStruct((ROWS, slots * TILE, width), integrals.dtype), sums_shape],
        in_specs=[HBM, HBM, HBM, VMEM],
        out_specs=[VMEM] * 2,
        scratch_shapes=[
            pltpu.SMEM(doubles_kept.shape, jnp.int32),
            pltpu.SMEM(integral_kept.shape, jnp.int32),
            pltpu.VMEM(integrals.shape, integrals.dtype),
            places,
            pltpu.SemaphoreType.DMA((3,)),
        ],
        compiler_params=PARAMS,
        cost_estimate=cost(10**9),
        name="prepare",
    )(doubles_kept, integral_kept, integrals, packed)

    def on_vmem(kernel, name, flops, out_shape, *args, scratch=()):
        return pl.pallas_call(
            kernel,
            out_shape=out_shape,
            in_specs=[VMEM] * len(args),
            out_specs=jax.tree.map(lambda _: VMEM, out_shape),
            scratch_shapes=scratch,
            compiler_params=PARAMS,
            cost_estimate=cost(flops),
            name=name,
        )(*args)

    sums = [pltpu.VMEM((ROWS, pairs // 2, width), jnp.float32)]
    own_early, core_early, two, three = on_vmem(
        early_kernel,
        "early",
        0,
        [half_shape] * 2 + [message] * 2,
        product,
        gathered,
        pair,
        near_second,
        far_first,
        scratch=sums,
    )
    two, three = swap(two, "cols", 2), swap(three, "cols", 3)
    own_late, one, two_late, three_late = on_vmem(
        late_kernel,
        "late",
        10**11,
        [half_shape, double] + [message] * 2,
        core_early,
        product,
        gathered,
        pair,
        near_first,
        far_second,
        scratch=sums,
    )
    two_late, three_late = swap(two_late, "cols", 2), swap(three_late, "cols", 3)
    one = swap(one, "cols", 1)
    base = on_vmem(first_kernel, "first", 10**11, sums_shape, residual, own_early, two, three)
    return on_vmem(last_kernel, "last", 0, sums_shape, base, own_late, two_late, three_late, one)


def local_many(doubles, doubles_kept, integrals, integral_kept, residual):
    pairs, cd_local = doubles.shape
    tiles = cd_local // TILE
    blocks = lax.all_gather(doubles, "rows", axis=0).reshape(-1, pairs, tiles, TILE)
    blocks = blocks * doubles_kept.astype(doubles.dtype)[:, None, :, None]
    tiles_ab = integrals.shape[1] // TILE
    masked = integrals.reshape(tiles, TILE, tiles_ab, TILE) * integral_kept.astype(integrals.dtype)[:, None, :, None]
    sums = jnp.dot(
        blocks.reshape(-1, cd_local), masked.reshape(integrals.shape), preferred_element_type=jnp.float32
    )
    return residual + lax.psum_scatter(sums, "cols", scatter_dimension=0, tiled=True)


def solution(mesh):
    few = mesh.shape["rows"] == mesh.shape["cols"] == ROWS
    in_specs = (
        P(("groups", "rows"), "cols"),
        P("groups", "cols"),
        P(("groups", "cols"), "rows"),
        P(("groups", "cols"), "rows"),
        P(("groups", "cols"), "rows"),
    )
    out_specs = P(("groups", "cols"), "rows")
    return jax.shard_map(
        local_few if few else local_many, mesh=mesh, in_specs=in_specs, out_specs=out_specs, check_vma=False
    )
```

```python
import functools

import jax
import jax.numpy as jnp
from jax import lax
from jax.experimental import pallas as pl
from jax.experimental.pallas import tpu as pltpu
from jax.sharding import PartitionSpec as P

TILE = 128
GROUP = 8
KEEP = 4
HEAD = 16
STEPS = 8

VMEM = pl.BlockSpec(memory_space=pltpu.VMEM)
HBM = pl.BlockSpec(memory_space=pltpu.HBM)
PARAMS = pltpu.CompilerParams(vmem_limit_bytes=8 * 1024 * 1024)

ROWS = 4


def cost(flops):
    return pl.CostEstimate(flops=flops, bytes_accessed=1024, transcendentals=0)


def list_kept(kept, row, tiles, places):
    at = jnp.int32(0)
    for tile in range(tiles):
        places[at] = jnp.int32(tile)
        at = at + kept[row, tile]


def pack_kernel(tiles, slots, kept, doubles, first, second, table, block, places, sems):
    table_copy = pltpu.make_async_copy(kept, table, sems.at[0])
    block_copy = pltpu.make_async_copy(doubles, block, sems.at[1])
    table_copy.start()
    block_copy.start()
    table_copy.wait()
    list_kept(table, lax.axis_index("rows"), tiles, places)
    block_copy.wait()
    half = first.shape[0]
    for slot in range(slots):
        tile = pl.ds(pl.multiple_of(places[slot] * TILE, TILE), TILE)
        to = slice(slot * TILE, (slot + 1) * TILE)
        first[:, to] = block[:half, tile]
        second[:, to] = block[half:, tile]


def prepare_kernel(tiles, slots, kept, int_kept, integrals, first, second, gathered, product, table, int_table, held, places, sems):
    copies = [
        pltpu.make_async_copy(*pair, sems.at[i])
        for i, pair in enumerate(((kept, table), (int_kept, int_table), (integrals, held)))
    ]
    for copy in copies:
        copy.start()
    for copy in copies:
        copy.wait()
    row, col = lax.axis_index("rows"), lax.axis_index("cols")
    tiles_ab = integrals.shape[1] // TILE
    for n in range(ROWS):
        list_kept(table, col ^ n, tiles, places)
        for slot in range(slots):
            tile = places[slot]
            start = pl.multiple_of(tile * TILE, TILE)
            for ab in range(tiles_ab):
                part = held[pl.ds(start, TILE), ab * TILE : (ab + 1) * TILE]
                on = (int_table[ab, tile] != 0).astype(jnp.float32).astype(part.dtype)
                gathered[n, slot * TILE : (slot + 1) * TILE, ab * TILE : (ab + 1) * TILE] = part * on
    half = first.shape[0]
    for start, own in ((0, first), (half, second)):
        product[start : start + half, :] = jnp.dot(
            own[...], gathered[row ^ col], preferred_element_type=jnp.float32
        )


def encode(x, out):
    pairs, width = x.shape
    largest = jnp.max(jnp.abs(x), axis=0, keepdims=True)
    exponent = jnp.floor((14.95 - jnp.log2(jnp.maximum(largest, 1e-30))) * STEPS)
    code = jnp.round(x * jnp.exp2(exponent * (1.0 / STEPS))).astype(jnp.int32)
    bands = width // TILE
    each = HEAD // bands
    exponent = jnp.broadcast_to(exponent.astype(jnp.int32), (each, width))
    for band in range(bands):
        out[band * pairs : (band + 1) * pairs, :] = code[:, band * TILE : (band + 1) * TILE].astype(jnp.int16)
    head = jnp.concatenate([exponent[:, band * TILE : (band + 1) * TILE] for band in range(bands)], axis=0)
    out[bands * pairs :, :] = head.astype(jnp.int16)


def decode(message, pairs):
    bands = (message.shape[0] - HEAD) // pairs
    each = HEAD // bands
    head = message[bands * pairs :, :].astype(jnp.int32).astype(jnp.float32)
    parts = []
    for band in range(bands):
        scale = jnp.exp2(head[band * each : band * each + 1, :] * (-1.0 / STEPS))
        parts.append(message[band * pairs : (band + 1) * pairs, :].astype(jnp.int32).astype(jnp.float32) * scale)
    return jnp.concatenate(parts, axis=1)


def half_of(ref, half):
    size = ref.shape[0] // 2
    return ref.at[pl.ds(pl.multiple_of(half * size, size), size)]


def early_half(step):
    return 1 - step % 2


def half_sums(late, product, gathered, near, far, pair, sums):
    mine = lax.axis_index("rows") ^ lax.axis_index("cols")
    half = product.shape[0] // 2
    start = (early_half(0) ^ late) * half
    sums[mine] = product[start : start + half, :]
    for step, block in zip((2, 3, 1), (near, far, pair)):
        sums[mine ^ step] = jnp.dot(block[...], gathered[mine ^ step], preferred_element_type=jnp.float32)


def early_kernel(product, gathered, near, far, pair, own_sums, core_sums, two, three, sums):
    half_sums(0, product, gathered, near, far, pair, sums)
    own_sums[...] = sums[0]
    core_sums[...] = sums[1]
    encode(sums[2], two)
    encode(sums[3], three)


def late_kernel(core_sums, product, gathered, near, far, pair, own_sums, one, two, three, sums):
    half_sums(1, product, gathered, near, far, pair, sums)
    own_sums[...] = sums[0]
    encode(sums[2], two)
    encode(sums[3], three)
    encode(core_sums[...], half_of(one, 0))
    encode(sums[1], half_of(one, 1))


def first_kernel(residual, own_sums, two, three, out):
    early = early_half(lax.axis_index("rows") ^ lax.axis_index("cols"))
    half = own_sums.shape[0]
    total = half_of(residual, early)[...] + own_sums[...]
    half_of(out, early)[...] = total + decode(two, half) + decode(three, half)
    half_of(out, 1 - early)[...] = half_of(residual, 1 - early)[...]


def last_kernel(base, own_sums, two, three, one, out):
    early = early_half(lax.axis_index("rows") ^ lax.axis_index("cols"))
    half = own_sums.shape[0]
    half_of(out, early)[...] = half_of(base, early)[...] + decode(half_of(one, 0), half)
    total = half_of(base, 1 - early)[...] + own_sums[...] + decode(half_of(one, 1), half)
    half_of(out, 1 - early)[...] = total + decode(two, half) + decode(three, half)


def swap(x, axis, step):
    return lax.ppermute(x, axis, [(i, i ^ step) for i in range(ROWS)])


def local_few(doubles, doubles_kept, integrals, integral_kept, residual):
    pairs, cd_local = doubles.shape
    width = integrals.shape[1]
    tiles = cd_local // TILE
    slots = tiles // GROUP * KEEP
    places = pltpu.SMEM((tiles + 1,), jnp.int32)
    sums_shape = jax.ShapeDtypeStruct((pairs, width), jnp.float32)
    half_block = jax.ShapeDtypeStruct((pairs // 2, slots * TILE), doubles.dtype)
    half_shape = jax.ShapeDtypeStruct((pairs // 2, width), jnp.float32)
    message = jax.ShapeDtypeStruct((pairs // 2 * width // TILE + HEAD, TILE), jnp.int16)
    double = jax.ShapeDtypeStruct((2 * message.shape[0], TILE), jnp.int16)
    doubles, doubles_kept, integrals, integral_kept = (
        pltpu.with_memory_space_constraint(x, pltpu.HBM) for x in (doubles, doubles_kept, integrals, integral_kept.T)
    )
    first, second = pl.pallas_call(
        functools.partial(pack_kernel, tiles, slots),
        out_shape=[half_block] * 2,
        in_specs=[HBM, HBM],
        out_specs=[VMEM] * 2,
        scratch_shapes=[
            pltpu.SMEM(doubles_kept.shape, jnp.int32),
            pltpu.VMEM(doubles.shape, doubles.dtype),
            places,
            pltpu.SemaphoreType.DMA((2,)),
        ],
        compiler_params=PARAMS,
        name="pack",
    )(doubles_kept, doubles)
    near_second = swap(second, "rows", 2)
    far_first = swap(first, "rows", 3)
    pair_first = swap(first, "rows", 1)
    near_first = swap(first, "rows", 2)
    pair_second = swap(second, "rows", 1)
    far_second = swap(near_second, "rows", 1)
    gathered, product = pl.pallas_call(
        functools.partial(prepare_kernel, tiles, slots),
        out_shape=[jax.ShapeDtypeStruct((ROWS, slots * TILE, width), integrals.dtype), sums_shape],
        in_specs=[HBM] * 3 + [VMEM] * 2,
        out_specs=[VMEM] * 2,
        scratch_shapes=[
            pltpu.SMEM(doubles_kept.shape, jnp.int32),
            pltpu.SMEM(integral_kept.shape, jnp.int32),
            pltpu.VMEM(integrals.shape, integrals.dtype),
            places,
            pltpu.SemaphoreType.DMA((3,)),
        ],
        compiler_params=PARAMS,
        cost_estimate=cost(0),
        name="prepare",
    )(doubles_kept, integral_kept, integrals, first, second)

    def on_vmem(kernel, name, flops, out_shape, *args, scratch=()):
        return pl.pallas_call(
            kernel,
            out_shape=out_shape,
            in_specs=[VMEM] * len(args),
            out_specs=jax.tree.map(lambda _: VMEM, out_shape),
            scratch_shapes=scratch,
            compiler_params=PARAMS,
            cost_estimate=cost(flops),
            name=name,
        )(*args)

    sums = [pltpu.VMEM((ROWS, pairs // 2, width), jnp.float32)]
    own_early, core_early, two, three = on_vmem(
        early_kernel,
        "early",
        0,
        [half_shape] * 2 + [message] * 2,
        product,
        gathered,
        near_second,
        far_first,
        pair_first,
        scratch=sums,
    )
    two, three = swap(two, "cols", 2), swap(three, "cols", 3)
    own_late, one, two_late, three_late = on_vmem(
        late_kernel,
        "late",
        10**11,
        [half_shape, double] + [message] * 2,
        core_early,
        product,
        gathered,
        near_first,
        far_second,
        pair_second,
        scratch=sums,
    )
    two_late, three_late = swap(two_late, "cols", 2), swap(three_late, "cols", 3)
    one = swap(one, "cols", 1)
    base = on_vmem(first_kernel, "first", 10**11, sums_shape, residual, own_early, two, three)
    return on_vmem(last_kernel, "last", 0, sums_shape, base, own_late, two_late, three_late, one)


def local_many(doubles, doubles_kept, integrals, integral_kept, residual):
    pairs, cd_local = doubles.shape
    tiles = cd_local // TILE
    blocks = lax.all_gather(doubles, "rows", axis=0).reshape(-1, pairs, tiles, TILE)
    blocks = blocks * doubles_kept.astype(doubles.dtype)[:, None, :, None]
    tiles_ab = integrals.shape[1] // TILE
    masked = integrals.reshape(tiles, TILE, tiles_ab, TILE) * integral_kept.astype(integrals.dtype)[:, None, :, None]
    sums = jnp.dot(
        blocks.reshape(-1, cd_local), masked.reshape(integrals.shape), preferred_element_type=jnp.float32
    )
    return residual + lax.psum_scatter(sums, "cols", scatter_dimension=0, tiled=True)


def solution(mesh):
    few = mesh.shape["rows"] == mesh.shape["cols"] == ROWS
    in_specs = (
        P(("groups", "rows"), "cols"),
        P("groups", "cols"),
        P(("groups", "cols"), "rows"),
        P(("groups", "cols"), "rows"),
        P(("groups", "cols"), "rows"),
    )
    out_specs = P(("groups", "cols"), "rows")
    return jax.shard_map(
        local_few if few else local_many, mesh=mesh, in_specs=in_specs, out_specs=out_specs, check_vma=False
    )
```

```python
import functools

import jax
import jax.numpy as jnp
from jax import lax
from jax.experimental import pallas as pl
from jax.experimental.pallas import tpu as pltpu
from jax.sharding import PartitionSpec as P

TILE = 128
GROUP = 8
KEEP = 4
HEAD = 16
STEPS = 8

VMEM = pl.BlockSpec(memory_space=pltpu.VMEM)
HBM = pl.BlockSpec(memory_space=pltpu.HBM)
PARAMS = pltpu.CompilerParams(vmem_limit_bytes=8 * 1024 * 1024)

ROWS = 4


def cost(flops):
    return pl.CostEstimate(flops=flops, bytes_accessed=1024, transcendentals=0)


def list_kept(kept, row, tiles, places):
    at = jnp.int32(0)
    for tile in range(tiles):
        places[at] = jnp.int32(tile)
        at = at + kept[row, tile]


def pack_kernel(tiles, slots, kept, doubles, first, second, second_too, table, block, places, sems):
    table_copy = pltpu.make_async_copy(kept, table, sems.at[0])
    block_copy = pltpu.make_async_copy(doubles, block, sems.at[1])
    table_copy.start()
    block_copy.start()
    table_copy.wait()
    list_kept(table, lax.axis_index("rows"), tiles, places)
    block_copy.wait()
    half = first.shape[0]
    for slot in range(slots):
        tile = pl.ds(pl.multiple_of(places[slot] * TILE, TILE), TILE)
        to = slice(slot * TILE, (slot + 1) * TILE)
        first[:, to] = block[:half, tile]
        second[:, to] = block[half:, tile]
        second_too[:, to] = block[half:, tile]


def prepare_kernel(tiles, slots, kept, int_kept, integrals, first, second, gathered, product, table, int_table, held, places, sems):
    copies = [
        pltpu.make_async_copy(*pair, sems.at[i])
        for i, pair in enumerate(((kept, table), (int_kept, int_table), (integrals, held)))
    ]
    for copy in copies:
        copy.start()
    for copy in copies:
        copy.wait()
    row, col = lax.axis_index("rows"), lax.axis_index("cols")
    tiles_ab = integrals.shape[1] // TILE
    for n in range(ROWS):
        list_kept(table, col ^ n, tiles, places)
        for slot in range(slots):
            tile = places[slot]
            start = pl.multiple_of(tile * TILE, TILE)
            for ab in range(tiles_ab):
                part = held[pl.ds(start, TILE), ab * TILE : (ab + 1) * TILE]
                on = (int_table[ab, tile] != 0).astype(jnp.float32).astype(part.dtype)
                gathered[n, slot * TILE : (slot + 1) * TILE, ab * TILE : (ab + 1) * TILE] = part * on
    half = first.shape[0]
    for start, own in ((0, first), (half, second)):
        product[start : start + half, :] = jnp.dot(
            own[...], gathered[row ^ col], preferred_element_type=jnp.float32
        )


def after_kernel(token, x, out):
    pass


def encode(x, out):
    pairs, width = x.shape
    largest = jnp.max(jnp.abs(x), axis=0, keepdims=True)
    exponent = jnp.floor((14.95 - jnp.log2(jnp.maximum(largest, 1e-30))) * STEPS)
    code = jnp.round(x * jnp.exp2(exponent * (1.0 / STEPS))).astype(jnp.int32)
    bands = width // TILE
    each = HEAD // bands
    exponent = jnp.broadcast_to(exponent.astype(jnp.int32), (each, width))
    for band in range(bands):
        out[band * pairs : (band + 1) * pairs, :] = code[:, band * TILE : (band + 1) * TILE].astype(jnp.int16)
    head = jnp.concatenate([exponent[:, band * TILE : (band + 1) * TILE] for band in range(bands)], axis=0)
    out[bands * pairs :, :] = head.astype(jnp.int16)


def decode(message, pairs):
    bands = (message.shape[0] - HEAD) // pairs
    each = HEAD // bands
    head = message[bands * pairs :, :].astype(jnp.int32).astype(jnp.float32)
    parts = []
    for band in range(bands):
        scale = jnp.exp2(head[band * each : band * each + 1, :] * (-1.0 / STEPS))
        parts.append(message[band * pairs : (band + 1) * pairs, :].astype(jnp.int32).astype(jnp.float32) * scale)
    return jnp.concatenate(parts, axis=1)


def half_of(ref, half):
    size = ref.shape[0] // 2
    return ref.at[pl.ds(pl.multiple_of(half * size, size), size)]


def early_half(step):
    return 1 - step % 2


def half_sums(late, product, gathered, near, far, pair, sums):
    mine = lax.axis_index("rows") ^ lax.axis_index("cols")
    half = product.shape[0] // 2
    start = (early_half(0) ^ late) * half
    sums[mine] = product[start : start + half, :]
    for step, block in zip((2, 3, 1), (near, far, pair)):
        sums[mine ^ step] = jnp.dot(block[...], gathered[mine ^ step], preferred_element_type=jnp.float32)


def early_kernel(product, gathered, near, far, pair, own_sums, core_sums, two, three, sums):
    half_sums(0, product, gathered, near, far, pair, sums)
    own_sums[...] = sums[0]
    core_sums[...] = sums[1]
    encode(sums[2], two)
    encode(sums[3], three)


def late_kernel(core_sums, product, gathered, near, far, pair, own_sums, one, two, three, sums):
    half_sums(1, product, gathered, near, far, pair, sums)
    own_sums[...] = sums[0]
    encode(sums[2], two)
    encode(sums[3], three)
    encode(core_sums[...], half_of(one, 0))
    encode(sums[1], half_of(one, 1))


def first_kernel(residual, own_sums, two, three, out):
    early = early_half(lax.axis_index("rows") ^ lax.axis_index("cols"))
    half = own_sums.shape[0]
    total = half_of(residual, early)[...] + own_sums[...]
    half_of(out, early)[...] = total + decode(two, half) + decode(three, half)
    half_of(out, 1 - early)[...] = half_of(residual, 1 - early)[...]


def last_kernel(base, own_sums, two, three, one, out):
    early = early_half(lax.axis_index("rows") ^ lax.axis_index("cols"))
    half = own_sums.shape[0]
    half_of(out, early)[...] = half_of(base, early)[...] + decode(half_of(one, 0), half)
    total = half_of(base, 1 - early)[...] + own_sums[...] + decode(half_of(one, 1), half)
    half_of(out, 1 - early)[...] = total + decode(two, half) + decode(three, half)


def after(token, x):
    return pl.pallas_call(
        after_kernel,
        out_shape=jax.ShapeDtypeStruct(x.shape, x.dtype),
        in_specs=[pl.BlockSpec(memory_space=pl.ANY)] * 2,
        out_specs=pl.BlockSpec(memory_space=pl.ANY),
        input_output_aliases={1: 0},
        compiler_params=PARAMS,
        cost_estimate=cost(0),
        name="after",
    )(token, x)


def swap(x, axis, step):
    return lax.ppermute(x, axis, [(i, i ^ step) for i in range(ROWS)])


def local_few(doubles, doubles_kept, integrals, integral_kept, residual):
    pairs, cd_local = doubles.shape
    width = integrals.shape[1]
    tiles = cd_local // TILE
    slots = tiles // GROUP * KEEP
    places = pltpu.SMEM((tiles + 1,), jnp.int32)
    sums_shape = jax.ShapeDtypeStruct((pairs, width), jnp.float32)
    half_block = jax.ShapeDtypeStruct((pairs // 2, slots * TILE), doubles.dtype)
    half_shape = jax.ShapeDtypeStruct((pairs // 2, width), jnp.float32)
    message = jax.ShapeDtypeStruct((pairs // 2 * width // TILE + HEAD, TILE), jnp.int16)
    double = jax.ShapeDtypeStruct((2 * message.shape[0], TILE), jnp.int16)
    doubles, doubles_kept, integrals, integral_kept = (
        pltpu.with_memory_space_constraint(x, pltpu.HBM) for x in (doubles, doubles_kept, integrals, integral_kept.T)
    )
    first, second, second_too = pl.pallas_call(
        functools.partial(pack_kernel, tiles, slots),
        out_shape=[half_block] * 3,
        in_specs=[HBM, HBM],
        out_specs=[VMEM] * 3,
        scratch_shapes=[
            pltpu.SMEM(doubles_kept.shape, jnp.int32),
            pltpu.VMEM(doubles.shape, doubles.dtype),
            places,
            pltpu.SemaphoreType.DMA((2,)),
        ],
        compiler_params=PARAMS,
        name="pack",
    )(doubles_kept, doubles)
    near_second = swap(second, "rows", 2)
    far_first = swap(first, "rows", 3)
    pair_first = swap(first, "rows", 1)
    near_first = swap(first, "rows", 2)
    far_second = swap(near_second, "rows", 1)
    pair_second = swap(after(near_second, second_too), "rows", 1)
    gathered, product = pl.pallas_call(
        functools.partial(prepare_kernel, tiles, slots),
        out_shape=[jax.ShapeDtypeStruct((ROWS, slots * TILE, width), integrals.dtype), sums_shape],
        in_specs=[HBM] * 3 + [VMEM] * 2,
        out_specs=[VMEM] * 2,
        scratch_shapes=[
            pltpu.SMEM(doubles_kept.shape, jnp.int32),
            pltpu.SMEM(integral_kept.shape, jnp.int32),
            pltpu.VMEM(integrals.shape, integrals.dtype),
            places,
            pltpu.SemaphoreType.DMA((3,)),
        ],
        compiler_params=PARAMS,
        cost_estimate=cost(0),
        name="prepare",
    )(doubles_kept, integral_kept, integrals, first, second)

    def on_vmem(kernel, name, flops, out_shape, *args, scratch=()):
        return pl.pallas_call(
            kernel,
            out_shape=out_shape,
            in_specs=[VMEM] * len(args),
            out_specs=jax.tree.map(lambda _: VMEM, out_shape),
            scratch_shapes=scratch,
            compiler_params=PARAMS,
            cost_estimate=cost(flops),
            name=name,
        )(*args)

    sums = [pltpu.VMEM((ROWS, pairs // 2, width), jnp.float32)]
    own_early, core_early, two, three = on_vmem(
        early_kernel,
        "early",
        0,
        [half_shape] * 2 + [message] * 2,
        product,
        gathered,
        near_second,
        far_first,
        pair_first,
        scratch=sums,
    )
    two, three = swap(two, "cols", 2), swap(three, "cols", 3)
    own_late, one, two_late, three_late = on_vmem(
        late_kernel,
        "late",
        10**11,
        [half_shape, double] + [message] * 2,
        core_early,
        product,
        gathered,
        near_first,
        far_second,
        pair_second,
        scratch=sums,
    )
    two_late, three_late = swap(two_late, "cols", 2), swap(three_late, "cols", 3)
    one = swap(one, "cols", 1)
    base = on_vmem(first_kernel, "first", 10**11, sums_shape, residual, own_early, two, three)
    return on_vmem(last_kernel, "last", 0, sums_shape, base, own_late, two_late, three_late, one)


def local_many(doubles, doubles_kept, integrals, integral_kept, residual):
    pairs, cd_local = doubles.shape
    tiles = cd_local // TILE
    blocks = lax.all_gather(doubles, "rows", axis=0).reshape(-1, pairs, tiles, TILE)
    blocks = blocks * doubles_kept.astype(doubles.dtype)[:, None, :, None]
    tiles_ab = integrals.shape[1] // TILE
    masked = integrals.reshape(tiles, TILE, tiles_ab, TILE) * integral_kept.astype(integrals.dtype)[:, None, :, None]
    sums = jnp.dot(
        blocks.reshape(-1, cd_local), masked.reshape(integrals.shape), preferred_element_type=jnp.float32
    )
    return residual + lax.psum_scatter(sums, "cols", scatter_dimension=0, tiled=True)


def solution(mesh):
    few = mesh.shape["rows"] == mesh.shape["cols"] == ROWS
    in_specs = (
        P(("groups", "rows"), "cols"),
        P("groups", "cols"),
        P(("groups", "cols"), "rows"),
        P(("groups", "cols"), "rows"),
        P(("groups", "cols"), "rows"),
    )
    out_specs = P(("groups", "cols"), "rows")
    return jax.shard_map(
        local_few if few else local_many, mesh=mesh, in_specs=in_specs, out_specs=out_specs, check_vma=False
    )
```

```python
import functools

import jax
import jax.numpy as jnp
from jax import lax
from jax.experimental import pallas as pl
from jax.experimental.pallas import tpu as pltpu
from jax.sharding import PartitionSpec as P

TILE = 128
GROUP = 8
KEEP = 4
HEAD = 16
STEPS = 8

VMEM = pl.BlockSpec(memory_space=pltpu.VMEM)
HBM = pl.BlockSpec(memory_space=pltpu.HBM)
PARAMS = pltpu.CompilerParams(vmem_limit_bytes=8 * 1024 * 1024)
ROWS = 4


def cost(flops):
    return pl.CostEstimate(flops=flops, bytes_accessed=1024, transcendentals=0)


def list_kept(kept, row, tiles, places):
    at = jnp.int32(0)
    for tile in range(tiles):
        places[at] = jnp.int32(tile)
        at = at + kept[row, tile]


def pack_kernel(tiles, slots, kept, doubles, packed, first, second, table, block, places, sems):
    table_copy = pltpu.make_async_copy(kept, table, sems.at[0])
    block_copy = pltpu.make_async_copy(doubles, block, sems.at[1])
    table_copy.start()
    block_copy.start()
    table_copy.wait()
    list_kept(table, lax.axis_index("rows"), tiles, places)
    block_copy.wait()
    half = first.shape[0]
    for slot in range(slots):
        tile = block[:, pl.ds(pl.multiple_of(places[slot] * TILE, TILE), TILE)]
        to = slice(slot * TILE, (slot + 1) * TILE)
        packed[:, to] = tile
        first[:, to] = tile[:half]
        second[:, to] = tile[half:]


def prepare_kernel(tiles, slots, kept, int_kept, integrals, own, gathered, product, table, int_table, held, places, sems):
    copies = [
        pltpu.make_async_copy(*pair, sems.at[i])
        for i, pair in enumerate(((kept, table), (int_kept, int_table), (integrals, held)))
    ]
    for copy in copies:
        copy.start()
    for copy in copies:
        copy.wait()
    row, col = lax.axis_index("rows"), lax.axis_index("cols")
    tiles_ab = integrals.shape[1] // TILE
    for n in range(ROWS):
        list_kept(table, col ^ n, tiles, places)
        for slot in range(slots):
            tile = places[slot]
            start = pl.multiple_of(tile * TILE, TILE)
            for ab in range(tiles_ab):
                part = held[pl.ds(start, TILE), ab * TILE : (ab + 1) * TILE]
                on = (int_table[ab, tile] != 0).astype(jnp.float32).astype(part.dtype)
                gathered[n, slot * TILE : (slot + 1) * TILE, ab * TILE : (ab + 1) * TILE] = part * on
    product[...] = jnp.dot(own[...], gathered[row ^ col], preferred_element_type=jnp.float32)


def encode(x, out):
    pairs, width = x.shape
    largest = jnp.max(jnp.abs(x), axis=0, keepdims=True)
    exponent = jnp.floor((14.95 - jnp.log2(jnp.maximum(largest, 1e-30))) * STEPS)
    code = jnp.round(x * jnp.exp2(exponent * (1.0 / STEPS))).astype(jnp.int32)
    bands = width // TILE
    each = HEAD // bands
    exponent = jnp.broadcast_to(exponent.astype(jnp.int32), (each, width))
    for band in range(bands):
        out[band * pairs : (band + 1) * pairs, :] = code[:, band * TILE : (band + 1) * TILE].astype(jnp.int16)
    head = jnp.concatenate([exponent[:, band * TILE : (band + 1) * TILE] for band in range(bands)], axis=0)
    out[bands * pairs :, :] = head.astype(jnp.int16)


def decode(message, pairs):
    bands = (message.shape[0] - HEAD) // pairs
    each = HEAD // bands
    head = message[bands * pairs :, :].astype(jnp.int32).astype(jnp.float32)
    parts = []
    for band in range(bands):
        scale = jnp.exp2(head[band * each : band * each + 1, :] * (-1.0 / STEPS))
        parts.append(message[band * pairs : (band + 1) * pairs, :].astype(jnp.int32).astype(jnp.float32) * scale)
    return jnp.concatenate(parts, axis=1)


def place():
    return lax.axis_index("rows") ^ lax.axis_index("cols")


def early_kernel(product, gathered, pair, near_second, far_first, sums):
    mine = place()
    half = near_second.shape[0]
    sums[mine] = product[...]
    sums[mine ^ 1] = jnp.dot(pair[...], gathered[mine ^ 1], preferred_element_type=jnp.float32)
    for step, start, block in ((2, half, near_second), (3, 0, far_first)):
        sums[mine ^ step, start : start + half, :] = jnp.dot(
            block[...], gathered[mine ^ step], preferred_element_type=jnp.float32
        )


def whole(n, early, near_sums, far_sums, out):
    half = near_sums.shape[0]
    step = place() ^ n
    out[...] = early[n]

    @pl.when(step == 2)
    def _():
        out[:half, :] = near_sums[...]

    @pl.when(step == 3)
    def _():
        out[half:, :] = far_sums[...]


def late_kernel(early, gathered, near_first, far_second, near_sums, far_sums, two, held):
    mine = place()
    near_sums[...] = jnp.dot(near_first[...], gathered[mine ^ 2], preferred_element_type=jnp.float32)
    far_sums[...] = jnp.dot(far_second[...], gathered[mine ^ 3], preferred_element_type=jnp.float32)
    whole(2, early, near_sums, far_sums, held)
    encode(held[...], two)


def rest_kernel(early, near_sums, far_sums, one, three, kept_sums, held):
    for n, out in ((3, three), (1, one)):
        whole(n, early, near_sums, far_sums, held)
        encode(held[...], out)
    whole(0, early, near_sums, far_sums, kept_sums)


def first_kernel(residual, kept_sums, two, out):
    out[...] = residual[...] + kept_sums[...] + decode(two, out.shape[0])


def last_kernel(base, three, one, out):
    out[...] = base[...] + decode(three, out.shape[0]) + decode(one, out.shape[0])


def swap(x, axis, step):
    return lax.ppermute(x, axis, [(i, i ^ step) for i in range(ROWS)])


def local_few(doubles, doubles_kept, integrals, integral_kept, residual):
    pairs, cd_local = doubles.shape
    width = integrals.shape[1]
    tiles = cd_local // TILE
    slots = tiles // GROUP * KEEP
    places = pltpu.SMEM((tiles + 1,), jnp.int32)
    sums_shape = jax.ShapeDtypeStruct((pairs, width), jnp.float32)
    half_block = jax.ShapeDtypeStruct((pairs // 2, slots * TILE), doubles.dtype)
    message = jax.ShapeDtypeStruct((pairs * width // TILE + HEAD, TILE), jnp.int16)
    doubles, doubles_kept, integrals, integral_kept = (
        pltpu.with_memory_space_constraint(x, pltpu.HBM) for x in (doubles, doubles_kept, integrals, integral_kept.T)
    )
    packed, first, second = pl.pallas_call(
        functools.partial(pack_kernel, tiles, slots),
        out_shape=[jax.ShapeDtypeStruct((pairs, slots * TILE), doubles.dtype), half_block, half_block],
        in_specs=[HBM, HBM],
        out_specs=[VMEM] * 3,
        scratch_shapes=[
            pltpu.SMEM(doubles_kept.shape, jnp.int32),
            pltpu.VMEM(doubles.shape, doubles.dtype),
            places,
            pltpu.SemaphoreType.DMA((2,)),
        ],
        compiler_params=PARAMS,
        name="pack",
    )(doubles_kept, doubles)
    near_second = swap(second, "rows", 2)
    pair = swap(packed, "rows", 1)
    far_first = swap(first, "rows", 3)
    near_first = swap(first, "rows", 2)
    far_second = swap(near_second, "rows", 1)
    gathered, product = pl.pallas_call(
        functools.partial(prepare_kernel, tiles, slots),
        out_shape=[jax.ShapeDtypeStruct((ROWS, slots * TILE, width), integrals.dtype), sums_shape],
        in_specs=[HBM, HBM, HBM, VMEM],
        out_specs=[VMEM] * 2,
        scratch_shapes=[
            pltpu.SMEM(doubles_kept.shape, jnp.int32),
            pltpu.SMEM(integral_kept.shape, jnp.int32),
            pltpu.VMEM(integrals.shape, integrals.dtype),
            places,
            pltpu.SemaphoreType.DMA((3,)),
        ],
        compiler_params=PARAMS,
        cost_estimate=cost(10**9),
        name="prepare",
    )(doubles_kept, integral_kept, integrals, packed)

    def on_vmem(kernel, name, flops, out_shape, *args, scratch=()):
        return pl.pallas_call(
            kernel,
            out_shape=out_shape,
            in_specs=[VMEM] * len(args),
            out_specs=jax.tree.map(lambda _: VMEM, out_shape),
            scratch_shapes=scratch,
            compiler_params=PARAMS,
            cost_estimate=cost(flops),
            name=name,
        )(*args)

    held = [pltpu.VMEM((pairs, width), jnp.float32)]
    half_sums = jax.ShapeDtypeStruct((pairs // 2, width), jnp.float32)
    all_sums = jax.ShapeDtypeStruct((ROWS, pairs, width), jnp.float32)
    early = on_vmem(early_kernel, "early", 0, all_sums, product, gathered, pair, near_second, far_first)
    near_sums, far_sums, two = on_vmem(
        late_kernel, "late", 10**11, [half_sums] * 2 + [message], early, gathered, near_first, far_second, scratch=held
    )
    one, three, kept_sums = on_vmem(
        rest_kernel, "rest", 0, [message] * 2 + [sums_shape], early, near_sums, far_sums, scratch=held
    )
    two, three, one = swap(two, "cols", 2), swap(three, "cols", 3), swap(one, "cols", 1)
    base = on_vmem(first_kernel, "first", 0, sums_shape, residual, kept_sums, two)
    return on_vmem(last_kernel, "last", 0, sums_shape, base, three, one)


def local_many(doubles, doubles_kept, integrals, integral_kept, residual):
    pairs, cd_local = doubles.shape
    tiles = cd_local // TILE
    blocks = lax.all_gather(doubles, "rows", axis=0).reshape(-1, pairs, tiles, TILE)
    blocks = blocks * doubles_kept.astype(doubles.dtype)[:, None, :, None]
    tiles_ab = integrals.shape[1] // TILE
    masked = integrals.reshape(tiles, TILE, tiles_ab, TILE) * integral_kept.astype(integrals.dtype)[:, None, :, None]
    sums = jnp.dot(
        blocks.reshape(-1, cd_local), masked.reshape(integrals.shape), preferred_element_type=jnp.float32
    )
    return residual + lax.psum_scatter(sums, "cols", scatter_dimension=0, tiled=True)


def solution(mesh):
    few = mesh.shape["rows"] == mesh.shape["cols"] == ROWS
    in_specs = (
        P(("groups", "rows"), "cols"),
        P("groups", "cols"),
        P(("groups", "cols"), "rows"),
        P(("groups", "cols"), "rows"),
        P(("groups", "cols"), "rows"),
    )
    out_specs = P(("groups", "cols"), "rows")
    return jax.shard_map(
        local_few if few else local_many, mesh=mesh, in_specs=in_specs, out_specs=out_specs, check_vma=False
    )
```

```python
import functools

import jax
import jax.numpy as jnp
from jax import lax
from jax.experimental import pallas as pl
from jax.experimental.pallas import tpu as pltpu
from jax.sharding import PartitionSpec as P

TILE = 128
GROUP = 8
KEEP = 4
HEAD = 16
STEPS = 8

VMEM = pl.BlockSpec(memory_space=pltpu.VMEM)
HBM = pl.BlockSpec(memory_space=pltpu.HBM)
PARAMS = pltpu.CompilerParams(vmem_limit_bytes=8 * 1024 * 1024)
PIECES = 4
ROWS = 4


def cost(flops):
    return pl.CostEstimate(flops=flops, bytes_accessed=1024, transcendentals=0)


def list_kept(kept, row, tiles, places):
    at = jnp.int32(0)
    for tile in range(tiles):
        places[at] = jnp.int32(tile)
        at = at + kept[row, tile]


def copies(source, target, sems):
    size = source.shape[0] // PIECES
    rows = [pl.ds(i * size, size) for i in range(PIECES)]
    return [pltpu.make_async_copy(source.at[r], target.at[r], sems.at[i]) for i, r in enumerate(rows)]


def pack_kernel(tiles, slots, kept, doubles, packed, first, second, table, block, places, sems):
    table_copy = pltpu.make_async_copy(kept, table, sems.at[PIECES])
    block_copies = copies(doubles, block, sems)
    table_copy.start()
    for copy in block_copies:
        copy.start()
    table_copy.wait()
    list_kept(table, lax.axis_index("rows"), tiles, places)
    for copy in block_copies:
        copy.wait()
    half = first.shape[0]
    for slot in range(slots):
        tile = block[:, pl.ds(pl.multiple_of(places[slot] * TILE, TILE), TILE)]
        to = slice(slot * TILE, (slot + 1) * TILE)
        packed[:, to] = tile
        first[:, to] = tile[:half]
        second[:, to] = tile[half:]


def prepare_kernel(tiles, slots, kept, int_kept, integrals, own, gathered, product, table, int_table, held, places, sems):
    started = copies(integrals, held, sems)
    for i, pair in enumerate(((kept, table), (int_kept, int_table)), PIECES):
        started.append(pltpu.make_async_copy(*pair, sems.at[i]))
    for copy in started:
        copy.start()
    for copy in started:
        copy.wait()
    row, col = lax.axis_index("rows"), lax.axis_index("cols")
    tiles_ab = integrals.shape[1] // TILE
    for n in range(ROWS):
        list_kept(table, col ^ n, tiles, places)
        for slot in range(slots):
            tile = places[slot]
            start = pl.multiple_of(tile * TILE, TILE)
            for ab in range(tiles_ab):
                part = held[pl.ds(start, TILE), ab * TILE : (ab + 1) * TILE]
                on = (int_table[ab, tile] != 0).astype(jnp.float32).astype(part.dtype)
                gathered[n, slot * TILE : (slot + 1) * TILE, ab * TILE : (ab + 1) * TILE] = part * on
    product[...] = jnp.dot(own[...], gathered[row ^ col], preferred_element_type=jnp.float32)


def encode(x, out):
    pairs, width = x.shape
    largest = jnp.max(jnp.abs(x), axis=0, keepdims=True)
    exponent = jnp.floor((14.95 - jnp.log2(jnp.maximum(largest, 1e-30))) * STEPS)
    code = jnp.round(x * jnp.exp2(exponent * (1.0 / STEPS))).astype(jnp.int32)
    bands = width // TILE
    each = HEAD // bands
    exponent = jnp.broadcast_to(exponent.astype(jnp.int32), (each, width))
    for band in range(bands):
        out[band * pairs : (band + 1) * pairs, :] = code[:, band * TILE : (band + 1) * TILE].astype(jnp.int16)
    head = jnp.concatenate([exponent[:, band * TILE : (band + 1) * TILE] for band in range(bands)], axis=0)
    out[bands * pairs :, :] = head.astype(jnp.int16)


def decode(message, pairs, start, stop):
    bands = (message.shape[0] - HEAD) // pairs
    each = HEAD // bands
    head = message[bands * pairs :, :].astype(jnp.int32).astype(jnp.float32)
    parts = []
    for band in range(bands):
        scale = jnp.exp2(head[band * each : band * each + 1, :] * (-1.0 / STEPS))
        code = message[band * pairs + start : band * pairs + stop, :]
        parts.append(code.astype(jnp.int32).astype(jnp.float32) * scale)
    return jnp.concatenate(parts, axis=1)


def place():
    return lax.axis_index("rows") ^ lax.axis_index("cols")


def early_kernel(product, gathered, pair, near_second, far_first, sums):
    mine = place()
    half = near_second.shape[0]
    sums[mine] = product[...]
    sums[mine ^ 1] = jnp.dot(pair[...], gathered[mine ^ 1], preferred_element_type=jnp.float32)
    for step, start, block in ((2, half, near_second), (3, 0, far_first)):
        sums[mine ^ step, start : start + half, :] = jnp.dot(
            block[...], gathered[mine ^ step], preferred_element_type=jnp.float32
        )


def whole(n, early, near_sums, far_sums, out):
    half = near_sums.shape[0]
    step = place() ^ n
    out[...] = early[n]

    @pl.when(step == 2)
    def _():
        out[:half, :] = near_sums[...]

    @pl.when(step == 3)
    def _():
        out[half:, :] = far_sums[...]


def late_kernel(early, gathered, near_first, far_second, near_sums, far_sums, two, held):
    mine = place()
    near_sums[...] = jnp.dot(near_first[...], gathered[mine ^ 2], preferred_element_type=jnp.float32)
    far_sums[...] = jnp.dot(far_second[...], gathered[mine ^ 3], preferred_element_type=jnp.float32)
    whole(2, early, near_sums, far_sums, held)
    encode(held[...], two)


def rest_kernel(early, near_sums, far_sums, one, three, kept_sums, held):
    for n, out in ((3, three), (1, one)):
        whole(n, early, near_sums, far_sums, held)
        encode(held[...], out)
    whole(0, early, near_sums, far_sums, kept_sums)


def first_kernel(residual, kept_sums, two, out):
    pairs = out.shape[0]
    out[...] = residual[...] + kept_sums[...] + decode(two, pairs, 0, pairs)


def last_kernel(base, three, one, out, total, sems):
    pairs = total.shape[0]
    size = pairs // PIECES
    started = copies(total, out, sems)
    for i, copy in enumerate(started):
        rows = (i * size, (i + 1) * size)
        total[rows[0] : rows[1], :] = base[rows[0] : rows[1], :] + decode(three, pairs, *rows) + decode(one, pairs, *rows)
        copy.start()
    for copy in started:
        copy.wait()


def swap(x, axis, step):
    return lax.ppermute(x, axis, [(i, i ^ step) for i in range(ROWS)])


def local_few(doubles, doubles_kept, integrals, integral_kept, residual):
    pairs, cd_local = doubles.shape
    width = integrals.shape[1]
    tiles = cd_local // TILE
    slots = tiles // GROUP * KEEP
    places = pltpu.SMEM((tiles + 1,), jnp.int32)
    sums_shape = jax.ShapeDtypeStruct((pairs, width), jnp.float32)
    half_block = jax.ShapeDtypeStruct((pairs // 2, slots * TILE), doubles.dtype)
    message = jax.ShapeDtypeStruct((pairs * width // TILE + HEAD, TILE), jnp.int16)
    doubles, doubles_kept, integrals, integral_kept = (
        pltpu.with_memory_space_constraint(x, pltpu.HBM) for x in (doubles, doubles_kept, integrals, integral_kept.T)
    )
    packed, first, second = pl.pallas_call(
        functools.partial(pack_kernel, tiles, slots),
        out_shape=[jax.ShapeDtypeStruct((pairs, slots * TILE), doubles.dtype), half_block, half_block],
        in_specs=[HBM, HBM],
        out_specs=[VMEM] * 3,
        scratch_shapes=[
            pltpu.SMEM(doubles_kept.shape, jnp.int32),
            pltpu.VMEM(doubles.shape, doubles.dtype),
            places,
            pltpu.SemaphoreType.DMA((PIECES + 1,)),
        ],
        compiler_params=PARAMS,
        name="pack",
    )(doubles_kept, doubles)
    near_second = swap(second, "rows", 2)
    pair = swap(packed, "rows", 1)
    far_first = swap(first, "rows", 3)
    near_first = swap(first, "rows", 2)
    far_second = swap(near_second, "rows", 1)
    gathered, product = pl.pallas_call(
        functools.partial(prepare_kernel, tiles, slots),
        out_shape=[jax.ShapeDtypeStruct((ROWS, slots * TILE, width), integrals.dtype), sums_shape],
        in_specs=[HBM, HBM, HBM, VMEM],
        out_specs=[VMEM] * 2,
        scratch_shapes=[
            pltpu.SMEM(doubles_kept.shape, jnp.int32),
            pltpu.SMEM(integral_kept.shape, jnp.int32),
            pltpu.VMEM(integrals.shape, integrals.dtype),
            places,
            pltpu.SemaphoreType.DMA((PIECES + 2,)),
        ],
        compiler_params=PARAMS,
        cost_estimate=cost(10**9),
        name="prepare",
    )(doubles_kept, integral_kept, integrals, packed)

    def on_vmem(kernel, name, flops, out_shape, *args, scratch=()):
        return pl.pallas_call(
            kernel,
            out_shape=out_shape,
            in_specs=[VMEM] * len(args),
            out_specs=jax.tree.map(lambda _: VMEM, out_shape),
            scratch_shapes=scratch,
            compiler_params=PARAMS,
            cost_estimate=cost(flops),
            name=name,
        )(*args)

    held = [pltpu.VMEM((pairs, width), jnp.float32)]
    half_sums = jax.ShapeDtypeStruct((pairs // 2, width), jnp.float32)
    all_sums = jax.ShapeDtypeStruct((ROWS, pairs, width), jnp.float32)
    early = on_vmem(early_kernel, "early", 0, all_sums, product, gathered, pair, near_second, far_first)
    near_sums, far_sums, two = on_vmem(
        late_kernel, "late", 10**11, [half_sums] * 2 + [message], early, gathered, near_first, far_second, scratch=held
    )
    one, three, kept_sums = on_vmem(
        rest_kernel, "rest", 0, [message] * 2 + [sums_shape], early, near_sums, far_sums, scratch=held
    )
    two, three, one = swap(two, "cols", 2), swap(three, "cols", 3), swap(one, "cols", 1)
    base = on_vmem(first_kernel, "first", 0, sums_shape, residual, kept_sums, two)
    return pl.pallas_call(
        last_kernel,
        out_shape=sums_shape,
        in_specs=[VMEM] * 3,
        out_specs=HBM,
        scratch_shapes=[pltpu.VMEM((pairs, width), jnp.float32), pltpu.SemaphoreType.DMA((PIECES,))],
        compiler_params=PARAMS,
        cost_estimate=cost(0),
        name="last",
    )(base, three, one)


def local_many(doubles, doubles_kept, integrals, integral_kept, residual):
    pairs, cd_local = doubles.shape
    tiles = cd_local // TILE
    blocks = lax.all_gather(doubles, "rows", axis=0).reshape(-1, pairs, tiles, TILE)
    blocks = blocks * doubles_kept.astype(doubles.dtype)[:, None, :, None]
    tiles_ab = integrals.shape[1] // TILE
    masked = integrals.reshape(tiles, TILE, tiles_ab, TILE) * integral_kept.astype(integrals.dtype)[:, None, :, None]
    sums = jnp.dot(
        blocks.reshape(-1, cd_local), masked.reshape(integrals.shape), preferred_element_type=jnp.float32
    )
    return residual + lax.psum_scatter(sums, "cols", scatter_dimension=0, tiled=True)


def solution(mesh):
    few = mesh.shape["rows"] == mesh.shape["cols"] == ROWS
    in_specs = (
        P(("groups", "rows"), "cols"),
        P("groups", "cols"),
        P(("groups", "cols"), "rows"),
        P(("groups", "cols"), "rows"),
        P(("groups", "cols"), "rows"),
    )
    out_specs = P(("groups", "cols"), "rows")
    return jax.shard_map(
        local_few if few else local_many, mesh=mesh, in_specs=in_specs, out_specs=out_specs, check_vma=False
    )
```

```python
import functools

import jax
import jax.numpy as jnp
from jax import lax
from jax.experimental import pallas as pl
from jax.experimental.pallas import tpu as pltpu
from jax.sharding import PartitionSpec as P

TILE = 128
GROUP = 8
KEEP = 4
HEAD = 16
STEPS = 8

VMEM = pl.BlockSpec(memory_space=pltpu.VMEM)
HBM = pl.BlockSpec(memory_space=pltpu.HBM)
PARAMS = pltpu.CompilerParams(vmem_limit_bytes=8 * 1024 * 1024)
PIECES = 4
ROWS = 4


def cost(flops):
    return pl.CostEstimate(flops=flops, bytes_accessed=1024, transcendentals=0)


def list_kept(kept, row, tiles, places):
    at = jnp.int32(0)
    for tile in range(tiles):
        places[at] = jnp.int32(tile)
        at = at + kept[row, tile]


def copies(source, target, sems):
    size = source.shape[0] // PIECES
    rows = [pl.ds(i * size, size) for i in range(PIECES)]
    return [pltpu.make_async_copy(source.at[r], target.at[r], sems.at[i]) for i, r in enumerate(rows)]


def pack_kernel(tiles, slots, kept, doubles, packed, packed_too, first, second, table, block, places, sems):
    table_copy = pltpu.make_async_copy(kept, table, sems.at[PIECES])
    block_copies = copies(doubles, block, sems)
    table_copy.start()
    for copy in block_copies:
        copy.start()
    table_copy.wait()
    list_kept(table, lax.axis_index("rows"), tiles, places)
    for copy in block_copies:
        copy.wait()
    half = first.shape[0]
    for slot in range(slots):
        tile = block[:, pl.ds(pl.multiple_of(places[slot] * TILE, TILE), TILE)]
        to = slice(slot * TILE, (slot + 1) * TILE)
        packed[:, to] = tile
        packed_too[:, to] = tile
        first[:, to] = tile[:half]
        second[:, to] = tile[half:]


def prepare_kernel(tiles, slots, kept, int_kept, integrals, own, gathered, product, table, int_table, held, places, sems):
    started = copies(integrals, held, sems)
    for i, pair in enumerate(((kept, table), (int_kept, int_table)), PIECES):
        started.append(pltpu.make_async_copy(*pair, sems.at[i]))
    for copy in started:
        copy.start()
    for copy in started:
        copy.wait()
    row, col = lax.axis_index("rows"), lax.axis_index("cols")
    tiles_ab = integrals.shape[1] // TILE
    for n in range(ROWS):
        list_kept(table, col ^ n, tiles, places)
        for slot in range(slots):
            tile = places[slot]
            start = pl.multiple_of(tile * TILE, TILE)
            for ab in range(tiles_ab):
                part = held[pl.ds(start, TILE), ab * TILE : (ab + 1) * TILE]
                on = (int_table[ab, tile] != 0).astype(jnp.float32).astype(part.dtype)
                gathered[n, slot * TILE : (slot + 1) * TILE, ab * TILE : (ab + 1) * TILE] = part * on
    product[...] = jnp.dot(own[...], gathered[row ^ col], preferred_element_type=jnp.float32)


def after_kernel(token, x, out):
    pass


def encode(x, out):
    pairs, width = x.shape
    largest = jnp.max(jnp.abs(x), axis=0, keepdims=True)
    exponent = jnp.floor((14.95 - jnp.log2(jnp.maximum(largest, 1e-30))) * STEPS)
    code = jnp.round(x * jnp.exp2(exponent * (1.0 / STEPS))).astype(jnp.int32)
    bands = width // TILE
    each = HEAD // bands
    exponent = jnp.broadcast_to(exponent.astype(jnp.int32), (each, width))
    for band in range(bands):
        out[band * pairs : (band + 1) * pairs, :] = code[:, band * TILE : (band + 1) * TILE].astype(jnp.int16)
    head = jnp.concatenate([exponent[:, band * TILE : (band + 1) * TILE] for band in range(bands)], axis=0)
    out[bands * pairs :, :] = head.astype(jnp.int16)


def decode(message, pairs, start, stop):
    bands = (message.shape[0] - HEAD) // pairs
    each = HEAD // bands
    head = message[bands * pairs :, :].astype(jnp.int32).astype(jnp.float32)
    parts = []
    for band in range(bands):
        scale = jnp.exp2(head[band * each : band * each + 1, :] * (-1.0 / STEPS))
        code = message[band * pairs + start : band * pairs + stop, :]
        parts.append(code.astype(jnp.int32).astype(jnp.float32) * scale)
    return jnp.concatenate(parts, axis=1)


def place():
    return lax.axis_index("rows") ^ lax.axis_index("cols")


def early_kernel(product, gathered, pair_down, near_second, far_first, sums):
    mine = place()
    half = near_second.shape[0]
    sums[mine] = product[...]

    @pl.when(lax.axis_index("rows") % 2 == 0)
    def _():
        sums[mine ^ 1] = jnp.dot(pair_down[...], gathered[mine ^ 1], preferred_element_type=jnp.float32)

    for step, start, block in ((2, half, near_second), (3, 0, far_first)):
        sums[mine ^ step, start : start + half, :] = jnp.dot(
            block[...], gathered[mine ^ step], preferred_element_type=jnp.float32
        )


def whole(n, early, pair_sums, near_sums, far_sums, out):
    half = near_sums.shape[0]
    step = place() ^ n
    up = (step == 1) & (lax.axis_index("rows") % 2 == 1)

    @pl.when(jnp.logical_not(up))
    def _():
        out[...] = early[n]

    @pl.when(up)
    def _():
        out[...] = pair_sums[...]

    @pl.when(step == 2)
    def _():
        out[:half, :] = near_sums[...]

    @pl.when(step == 3)
    def _():
        out[half:, :] = far_sums[...]


def late_kernel(early, gathered, near_first, far_second, pair_up, pair_sums, near_sums, far_sums, two, held):
    mine = place()

    @pl.when(lax.axis_index("rows") % 2 == 1)
    def _():
        pair_sums[...] = jnp.dot(pair_up[...], gathered[mine ^ 1], preferred_element_type=jnp.float32)

    near_sums[...] = jnp.dot(near_first[...], gathered[mine ^ 2], preferred_element_type=jnp.float32)
    far_sums[...] = jnp.dot(far_second[...], gathered[mine ^ 3], preferred_element_type=jnp.float32)
    whole(2, early, pair_sums, near_sums, far_sums, held)
    encode(held[...], two)


def rest_kernel(early, pair_sums, near_sums, far_sums, one, three, kept_sums, held):
    for n, out in ((3, three), (1, one)):
        whole(n, early, pair_sums, near_sums, far_sums, held)
        encode(held[...], out)
    whole(0, early, pair_sums, near_sums, far_sums, kept_sums)


def first_kernel(residual, kept_sums, two, out):
    pairs = out.shape[0]
    out[...] = residual[...] + kept_sums[...] + decode(two, pairs, 0, pairs)


def last_kernel(base, three, one, out, total, sems):
    pairs = total.shape[0]
    size = pairs // PIECES
    started = copies(total, out, sems)
    for i, copy in enumerate(started):
        rows = (i * size, (i + 1) * size)
        total[rows[0] : rows[1], :] = base[rows[0] : rows[1], :] + decode(three, pairs, *rows) + decode(one, pairs, *rows)
        copy.start()
    for copy in started:
        copy.wait()


def after(token, x):
    return pl.pallas_call(
        after_kernel,
        out_shape=jax.ShapeDtypeStruct(x.shape, x.dtype),
        in_specs=[pl.BlockSpec(memory_space=pl.ANY)] * 2,
        out_specs=pl.BlockSpec(memory_space=pl.ANY),
        input_output_aliases={1: 0},
        compiler_params=PARAMS,
        cost_estimate=cost(0),
        name="after",
    )(token, x)


def swap(x, axis, step):
    return lax.ppermute(x, axis, [(i, i ^ step) for i in range(ROWS)])


def local_few(doubles, doubles_kept, integrals, integral_kept, residual):
    pairs, cd_local = doubles.shape
    width = integrals.shape[1]
    tiles = cd_local // TILE
    slots = tiles // GROUP * KEEP
    places = pltpu.SMEM((tiles + 1,), jnp.int32)
    sums_shape = jax.ShapeDtypeStruct((pairs, width), jnp.float32)
    half_block = jax.ShapeDtypeStruct((pairs // 2, slots * TILE), doubles.dtype)
    message = jax.ShapeDtypeStruct((pairs * width // TILE + HEAD, TILE), jnp.int16)
    doubles, doubles_kept, integrals, integral_kept = (
        pltpu.with_memory_space_constraint(x, pltpu.HBM) for x in (doubles, doubles_kept, integrals, integral_kept.T)
    )
    packed, packed_too, first, second = pl.pallas_call(
        functools.partial(pack_kernel, tiles, slots),
        out_shape=[jax.ShapeDtypeStruct((pairs, slots * TILE), doubles.dtype)] * 2 + [half_block] * 2,
        in_specs=[HBM, HBM],
        out_specs=[VMEM] * 4,
        scratch_shapes=[
            pltpu.SMEM(doubles_kept.shape, jnp.int32),
            pltpu.VMEM(doubles.shape, doubles.dtype),
            places,
            pltpu.SemaphoreType.DMA((PIECES + 1,)),
        ],
        compiler_params=PARAMS,
        name="pack",
    )(doubles_kept, doubles)
    near_second = swap(second, "rows", 2)
    pair_down = lax.ppermute(packed, "rows", [(i + 1, i) for i in range(0, ROWS, 2)])
    far_first = swap(first, "rows", 3)
    near_first = swap(first, "rows", 2)
    near_second = after(pair_down, near_second)
    far_second = swap(near_second, "rows", 1)
    pair_up = lax.ppermute(after(near_second, packed_too), "rows", [(i, i + 1) for i in range(0, ROWS, 2)])
    gathered, product = pl.pallas_call(
        functools.partial(prepare_kernel, tiles, slots),
        out_shape=[jax.ShapeDtypeStruct((ROWS, slots * TILE, width), integrals.dtype), sums_shape],
        in_specs=[HBM, HBM, HBM, VMEM],
        out_specs=[VMEM] * 2,
        scratch_shapes=[
            pltpu.SMEM(doubles_kept.shape, jnp.int32),
            pltpu.SMEM(integral_kept.shape, jnp.int32),
            pltpu.VMEM(integrals.shape, integrals.dtype),
            places,
            pltpu.SemaphoreType.DMA((PIECES + 2,)),
        ],
        compiler_params=PARAMS,
        cost_estimate=cost(10**11),
        name="prepare",
    )(doubles_kept, integral_kept, integrals, packed)

    def on_vmem(kernel, name, flops, out_shape, *args, scratch=()):
        return pl.pallas_call(
            kernel,
            out_shape=out_shape,
            in_specs=[VMEM] * len(args),
            out_specs=jax.tree.map(lambda _: VMEM, out_shape),
            scratch_shapes=scratch,
            compiler_params=PARAMS,
            cost_estimate=cost(flops),
            name=name,
        )(*args)

    held = [pltpu.VMEM((pairs, width), jnp.float32)]
    half_sums = jax.ShapeDtypeStruct((pairs // 2, width), jnp.float32)
    all_sums = jax.ShapeDtypeStruct((ROWS, pairs, width), jnp.float32)
    early = on_vmem(early_kernel, "early", 0, all_sums, product, gathered, pair_down, near_second, far_first)
    pair_sums, near_sums, far_sums, two = on_vmem(
        late_kernel,
        "late",
        10**11,
        [sums_shape] + [half_sums] * 2 + [message],
        early,
        gathered,
        near_first,
        far_second,
        pair_up,
        scratch=held,
    )
    one, three, kept_sums = on_vmem(
        rest_kernel,
        "rest",
        0,
        [message] * 2 + [sums_shape],
        early,
        pair_sums,
        near_sums,
        far_sums,
        scratch=held,
    )
    two, three, one = swap(two, "cols", 2), swap(three, "cols", 3), swap(one, "cols", 1)
    base = on_vmem(first_kernel, "first", 0, sums_shape, residual, kept_sums, two)
    return pl.pallas_call(
        last_kernel,
        out_shape=sums_shape,
        in_specs=[VMEM] * 3,
        out_specs=HBM,
        scratch_shapes=[pltpu.VMEM((pairs, width), jnp.float32), pltpu.SemaphoreType.DMA((PIECES,))],
        compiler_params=PARAMS,
        cost_estimate=cost(0),
        name="last",
    )(base, three, one)


def local_many(doubles, doubles_kept, integrals, integral_kept, residual):
    pairs, cd_local = doubles.shape
    tiles = cd_local // TILE
    blocks = lax.all_gather(doubles, "rows", axis=0).reshape(-1, pairs, tiles, TILE)
    blocks = blocks * doubles_kept.astype(doubles.dtype)[:, None, :, None]
    tiles_ab = integrals.shape[1] // TILE
    masked = integrals.reshape(tiles, TILE, tiles_ab, TILE) * integral_kept.astype(integrals.dtype)[:, None, :, None]
    sums = jnp.dot(
        blocks.reshape(-1, cd_local), masked.reshape(integrals.shape), preferred_element_type=jnp.float32
    )
    return residual + lax.psum_scatter(sums, "cols", scatter_dimension=0, tiled=True)


def solution(mesh):
    few = mesh.shape["rows"] == mesh.shape["cols"] == ROWS
    in_specs = (
        P(("groups", "rows"), "cols"),
        P("groups", "cols"),
        P(("groups", "cols"), "rows"),
        P(("groups", "cols"), "rows"),
        P(("groups", "cols"), "rows"),
    )
    out_specs = P(("groups", "cols"), "rows")
    return jax.shard_map(
        local_few if few else local_many, mesh=mesh, in_specs=in_specs, out_specs=out_specs, check_vma=False
    )
```

```python
import functools

import jax
import jax.numpy as jnp
from jax import lax
from jax.experimental import pallas as pl
from jax.experimental.pallas import tpu as pltpu
from jax.sharding import PartitionSpec as P

TILE = 128
GROUP = 8
KEEP = 4
HEAD = 16
STEPS = 8

VMEM = pl.BlockSpec(memory_space=pltpu.VMEM)
HBM = pl.BlockSpec(memory_space=pltpu.HBM)
PARAMS = pltpu.CompilerParams(vmem_limit_bytes=8 * 1024 * 1024)
DIRECT = 48
PIECES = 4
ROWS = 4


def cost(flops):
    return pl.CostEstimate(flops=flops, bytes_accessed=1024, transcendentals=0)


def list_kept(kept, row, tiles, places):
    at = jnp.int32(0)
    for tile in range(tiles):
        places[at] = jnp.int32(tile)
        at = at + kept[row, tile]


def copies(source, target, sems):
    size = source.shape[0] // PIECES
    rows = [pl.ds(i * size, size) for i in range(PIECES)]
    return [pltpu.make_async_copy(source.at[r], target.at[r], sems.at[i]) for i, r in enumerate(rows)]


def pack_kernel(tiles, slots, kept, doubles, packed, first, second, table, block, places, sems):
    table_copy = pltpu.make_async_copy(kept, table, sems.at[PIECES])
    block_copies = copies(doubles, block, sems)
    table_copy.start()
    for copy in block_copies:
        copy.start()
    table_copy.wait()
    list_kept(table, lax.axis_index("rows"), tiles, places)
    for copy in block_copies:
        copy.wait()
    cut = first.shape[0]
    for slot in range(slots):
        tile = block[:, pl.ds(pl.multiple_of(places[slot] * TILE, TILE), TILE)]
        to = slice(slot * TILE, (slot + 1) * TILE)
        packed[:, to] = tile
        first[:, to] = tile[:cut]
        second[:, to] = tile[cut:]


def prepare_kernel(tiles, slots, kept, int_kept, integrals, own, gathered, product, table, int_table, held, places, sems):
    started = copies(integrals, held, sems)
    for i, pair in enumerate(((kept, table), (int_kept, int_table)), PIECES):
        started.append(pltpu.make_async_copy(*pair, sems.at[i]))
    for copy in started:
        copy.start()
    for copy in started:
        copy.wait()
    row, col = lax.axis_index("rows"), lax.axis_index("cols")
    tiles_ab = integrals.shape[1] // TILE
    for n in range(ROWS):
        list_kept(table, col ^ n, tiles, places)
        for slot in range(slots):
            tile = places[slot]
            start = pl.multiple_of(tile * TILE, TILE)
            for ab in range(tiles_ab):
                part = held[pl.ds(start, TILE), ab * TILE : (ab + 1) * TILE]
                on = (int_table[ab, tile] != 0).astype(jnp.float32).astype(part.dtype)
                gathered[n, slot * TILE : (slot + 1) * TILE, ab * TILE : (ab + 1) * TILE] = part * on
    product[...] = jnp.dot(own[...], gathered[row ^ col], preferred_element_type=jnp.float32)


def encode(x, out):
    pairs, width = x.shape
    largest = jnp.max(jnp.abs(x), axis=0, keepdims=True)
    exponent = jnp.floor((14.95 - jnp.log2(jnp.maximum(largest, 1e-30))) * STEPS)
    code = jnp.round(x * jnp.exp2(exponent * (1.0 / STEPS))).astype(jnp.int32)
    bands = width // TILE
    each = HEAD // bands
    exponent = jnp.broadcast_to(exponent.astype(jnp.int32), (each, width))
    for band in range(bands):
        out[band * pairs : (band + 1) * pairs, :] = code[:, band * TILE : (band + 1) * TILE].astype(jnp.int16)
    head = jnp.concatenate([exponent[:, band * TILE : (band + 1) * TILE] for band in range(bands)], axis=0)
    out[bands * pairs :, :] = head.astype(jnp.int16)


def decode(message, pairs, start, stop):
    bands = (message.shape[0] - HEAD) // pairs
    each = HEAD // bands
    head = message[bands * pairs :, :].astype(jnp.int32).astype(jnp.float32)
    parts = []
    for band in range(bands):
        scale = jnp.exp2(head[band * each : band * each + 1, :] * (-1.0 / STEPS))
        code = message[band * pairs + start : band * pairs + stop, :]
        parts.append(code.astype(jnp.int32).astype(jnp.float32) * scale)
    return jnp.concatenate(parts, axis=1)


def place():
    return lax.axis_index("rows") ^ lax.axis_index("cols")


def early_kernel(product, gathered, pair, near_second, far_first, sums):
    mine = place()
    cut = far_first.shape[0]
    sums[mine] = product[...]
    sums[mine ^ 1] = jnp.dot(pair[...], gathered[mine ^ 1], preferred_element_type=jnp.float32)
    for step, start, block in ((2, cut, near_second), (3, 0, far_first)):
        sums[mine ^ step, start : start + block.shape[0], :] = jnp.dot(
            block[...], gathered[mine ^ step], preferred_element_type=jnp.float32
        )


def whole(n, early, near_sums, far_sums, out):
    cut = near_sums.shape[0]
    step = place() ^ n
    out[...] = early[n]

    @pl.when(step == 2)
    def _():
        out[:cut, :] = near_sums[...]

    @pl.when(step == 3)
    def _():
        out[cut:, :] = far_sums[...]


def late_kernel(early, gathered, near_first, far_second, near_sums, far_sums, two, held):
    mine = place()
    near_sums[...] = jnp.dot(near_first[...], gathered[mine ^ 2], preferred_element_type=jnp.float32)
    far_sums[...] = jnp.dot(far_second[...], gathered[mine ^ 3], preferred_element_type=jnp.float32)
    whole(2, early, near_sums, far_sums, held)
    encode(held[...], two)


def rest_kernel(early, near_sums, far_sums, one, three, kept_sums, held):
    for n, out in ((3, three), (1, one)):
        whole(n, early, near_sums, far_sums, held)
        encode(held[...], out)
    whole(0, early, near_sums, far_sums, kept_sums)


def first_kernel(residual, kept_sums, two, out):
    pairs = out.shape[0]
    out[...] = residual[...] + kept_sums[...] + decode(two, pairs, 0, pairs)


def last_kernel(base, three, one, out, total, sems):
    pairs = total.shape[0]
    size = pairs // PIECES
    started = copies(total, out, sems)
    for i, copy in enumerate(started):
        rows = (i * size, (i + 1) * size)
        total[rows[0] : rows[1], :] = base[rows[0] : rows[1], :] + decode(three, pairs, *rows) + decode(one, pairs, *rows)
        copy.start()
    for copy in started:
        copy.wait()


def swap(x, axis, step):
    return lax.ppermute(x, axis, [(i, i ^ step) for i in range(ROWS)])


def local_few(doubles, doubles_kept, integrals, integral_kept, residual):
    pairs, cd_local = doubles.shape
    width = integrals.shape[1]
    tiles = cd_local // TILE
    slots = tiles // GROUP * KEEP
    places = pltpu.SMEM((tiles + 1,), jnp.int32)
    sums_shape = jax.ShapeDtypeStruct((pairs, width), jnp.float32)
    parts = (DIRECT, pairs - DIRECT)
    blocks = [jax.ShapeDtypeStruct((rows, slots * TILE), doubles.dtype) for rows in parts]
    message = jax.ShapeDtypeStruct((pairs * width // TILE + HEAD, TILE), jnp.int16)
    doubles, doubles_kept, integrals, integral_kept = (
        pltpu.with_memory_space_constraint(x, pltpu.HBM) for x in (doubles, doubles_kept, integrals, integral_kept.T)
    )
    packed, first, second = pl.pallas_call(
        functools.partial(pack_kernel, tiles, slots),
        out_shape=[jax.ShapeDtypeStruct((pairs, slots * TILE), doubles.dtype)] + blocks,
        in_specs=[HBM, HBM],
        out_specs=[VMEM] * 3,
        scratch_shapes=[
            pltpu.SMEM(doubles_kept.shape, jnp.int32),
            pltpu.VMEM(doubles.shape, doubles.dtype),
            places,
            pltpu.SemaphoreType.DMA((PIECES + 1,)),
        ],
        compiler_params=PARAMS,
        name="pack",
    )(doubles_kept, doubles)
    near_second = swap(second, "rows", 2)
    pair = swap(packed, "rows", 1)
    far_first = swap(first, "rows", 3)
    near_first = swap(first, "rows", 2)
    far_second = swap(near_second, "rows", 1)
    gathered, product = pl.pallas_call(
        functools.partial(prepare_kernel, tiles, slots),
        out_shape=[jax.ShapeDtypeStruct((ROWS, slots * TILE, width), integrals.dtype), sums_shape],
        in_specs=[HBM, HBM, HBM, VMEM],
        out_specs=[VMEM] * 2,
        scratch_shapes=[
            pltpu.SMEM(doubles_kept.shape, jnp.int32),
            pltpu.SMEM(integral_kept.shape, jnp.int32),
            pltpu.VMEM(integrals.shape, integrals.dtype),
            places,
            pltpu.SemaphoreType.DMA((PIECES + 2,)),
        ],
        compiler_params=PARAMS,
        cost_estimate=cost(115 * 10**7),
        name="prepare",
    )(doubles_kept, integral_kept, integrals, packed)

    def on_vmem(kernel, name, flops, out_shape, *args, scratch=()):
        return pl.pallas_call(
            kernel,
            out_shape=out_shape,
            in_specs=[VMEM] * len(args),
            out_specs=jax.tree.map(lambda _: VMEM, out_shape),
            scratch_shapes=scratch,
            compiler_params=PARAMS,
            cost_estimate=cost(flops),
            name=name,
        )(*args)

    held = [pltpu.VMEM((pairs, width), jnp.float32)]
    part_sums = [jax.ShapeDtypeStruct((rows, width), jnp.float32) for rows in parts]
    all_sums = jax.ShapeDtypeStruct((ROWS, pairs, width), jnp.float32)
    early = on_vmem(early_kernel, "early", 0, all_sums, product, gathered, pair, near_second, far_first)
    near_sums, far_sums, two = on_vmem(
        late_kernel, "late", 10**11, part_sums + [message], early, gathered, near_first, far_second, scratch=held
    )
    one, three, kept_sums = on_vmem(
        rest_kernel, "rest", 0, [message] * 2 + [sums_shape], early, near_sums, far_sums, scratch=held
    )
    two, three, one = swap(two, "cols", 2), swap(three, "cols", 3), swap(one, "cols", 1)
    base = on_vmem(first_kernel, "first", 0, sums_shape, residual, kept_sums, two)
    return pl.pallas_call(
        last_kernel,
        out_shape=sums_shape,
        in_specs=[VMEM] * 3,
        out_specs=HBM,
        scratch_shapes=[pltpu.VMEM((pairs, width), jnp.float32), pltpu.SemaphoreType.DMA((PIECES,))],
        compiler_params=PARAMS,
        cost_estimate=cost(0),
        name="last",
    )(base, three, one)


def local_many(doubles, doubles_kept, integrals, integral_kept, residual):
    pairs, cd_local = doubles.shape
    tiles = cd_local // TILE
    blocks = lax.all_gather(doubles, "rows", axis=0).reshape(-1, pairs, tiles, TILE)
    blocks = blocks * doubles_kept.astype(doubles.dtype)[:, None, :, None]
    tiles_ab = integrals.shape[1] // TILE
    masked = integrals.reshape(tiles, TILE, tiles_ab, TILE) * integral_kept.astype(integrals.dtype)[:, None, :, None]
    sums = jnp.dot(
        blocks.reshape(-1, cd_local), masked.reshape(integrals.shape), preferred_element_type=jnp.float32
    )
    return residual + lax.psum_scatter(sums, "cols", scatter_dimension=0, tiled=True)


def solution(mesh):
    few = mesh.shape["rows"] == mesh.shape["cols"] == ROWS
    in_specs = (
        P(("groups", "rows"), "cols"),
        P("groups", "cols"),
        P(("groups", "cols"), "rows"),
        P(("groups", "cols"), "rows"),
        P(("groups", "cols"), "rows"),
    )
    out_specs = P(("groups", "cols"), "rows")
    return jax.shard_map(
        local_few if few else local_many, mesh=mesh, in_specs=in_specs, out_specs=out_specs, check_vma=False
    )
```

```python
import functools

import jax
import jax.numpy as jnp
from jax import lax
from jax.experimental import pallas as pl
from jax.experimental.pallas import tpu as pltpu
from jax.sharding import PartitionSpec as P

TILE = 128
GROUP = 8
KEEP = 4
HEAD = 16
STEPS = 8

VMEM = pl.BlockSpec(memory_space=pltpu.VMEM)
HBM = pl.BlockSpec(memory_space=pltpu.HBM)
PARAMS = pltpu.CompilerParams(vmem_limit_bytes=8 * 1024 * 1024)
DIRECT = 48
PIECES = 4
ROWS = 4


def cost(flops):
    return pl.CostEstimate(flops=flops, bytes_accessed=1024, transcendentals=0)


def list_kept(kept, row, tiles, places):
    at = jnp.int32(0)
    for tile in range(tiles):
        places[at] = jnp.int32(tile)
        at = at + kept[row, tile]


def copies(source, target, sems):
    size = source.shape[0] // PIECES
    rows = [pl.ds(i * size, size) for i in range(PIECES)]
    return [pltpu.make_async_copy(source.at[r], target.at[r], sems.at[i]) for i, r in enumerate(rows)]


def pack_kernel(tiles, slots, kept, doubles, packed, first, second, table, block, places, sems):
    table_copy = pltpu.make_async_copy(kept, table, sems.at[PIECES])
    block_copies = copies(doubles, block, sems)
    table_copy.start()
    for copy in block_copies:
        copy.start()
    table_copy.wait()
    list_kept(table, lax.axis_index("rows"), tiles, places)
    for copy in block_copies:
        copy.wait()
    cut = first.shape[0]
    for slot in range(slots):
        tile = block[:, pl.ds(pl.multiple_of(places[slot] * TILE, TILE), TILE)]
        to = slice(slot * TILE, (slot + 1) * TILE)
        packed[:, to] = tile
        first[:, to] = tile[:cut]
        second[:, to] = tile[cut:]


def prepare_kernel(tiles, slots, kept, int_kept, integrals, own, gathered, product, table, int_table, held, places, sems):
    started = copies(integrals, held, sems)
    for i, pair in enumerate(((kept, table), (int_kept, int_table)), PIECES):
        started.append(pltpu.make_async_copy(*pair, sems.at[i]))
    for copy in started:
        copy.start()
    for copy in started:
        copy.wait()
    row, col = lax.axis_index("rows"), lax.axis_index("cols")
    tiles_ab = integrals.shape[1] // TILE
    for n in range(ROWS):
        list_kept(table, col ^ n, tiles, places)
        for slot in range(slots):
            tile = places[slot]
            start = pl.multiple_of(tile * TILE, TILE)
            for ab in range(tiles_ab):
                part = held[pl.ds(start, TILE), ab * TILE : (ab + 1) * TILE]
                on = (int_table[ab, tile] != 0).astype(jnp.float32).astype(part.dtype)
                gathered[n, slot * TILE : (slot + 1) * TILE, ab * TILE : (ab + 1) * TILE] = part * on
    product[...] = jnp.dot(own[...], gathered[row ^ col], preferred_element_type=jnp.float32)


def encode(x, out):
    pairs, width = x.shape
    largest = jnp.max(jnp.abs(x), axis=0, keepdims=True)
    exponent = jnp.floor((14.95 - jnp.log2(jnp.maximum(largest, 1e-30))) * STEPS)
    code = jnp.round(x * jnp.exp2(exponent * (1.0 / STEPS))).astype(jnp.int32)
    bands = width // TILE
    each = HEAD // bands
    exponent = jnp.broadcast_to(exponent.astype(jnp.int32), (each, width))
    for band in range(bands):
        out[band * pairs : (band + 1) * pairs, :] = code[:, band * TILE : (band + 1) * TILE].astype(jnp.int16)
    head = jnp.concatenate([exponent[:, band * TILE : (band + 1) * TILE] for band in range(bands)], axis=0)
    out[bands * pairs :, :] = head.astype(jnp.int16)


def decode(message, pairs, start, stop):
    bands = (message.shape[0] - HEAD) // pairs
    each = HEAD // bands
    head = message[bands * pairs :, :].astype(jnp.int32).astype(jnp.float32)
    parts = []
    for band in range(bands):
        scale = jnp.exp2(head[band * each : band * each + 1, :] * (-1.0 / STEPS))
        code = message[band * pairs + start : band * pairs + stop, :]
        parts.append(code.astype(jnp.int32).astype(jnp.float32) * scale)
    return jnp.concatenate(parts, axis=1)


def place():
    return lax.axis_index("rows") ^ lax.axis_index("cols")


def early_kernel(product, gathered, pair, near_second, far_first, sums):
    mine = place()
    cut = far_first.shape[0]
    sums[mine] = product[...]
    sums[mine ^ 1] = jnp.dot(pair[...], gathered[mine ^ 1], preferred_element_type=jnp.float32)
    for step, start, block in ((2, cut, near_second), (3, 0, far_first)):
        sums[mine ^ step, start : start + block.shape[0], :] = jnp.dot(
            block[...], gathered[mine ^ step], preferred_element_type=jnp.float32
        )


def whole(n, early, near_sums, far_sums, out):
    cut = near_sums.shape[0]
    step = place() ^ n
    out[...] = early[n]

    @pl.when(step == 2)
    def _():
        out[:cut, :] = near_sums[...]

    @pl.when(step == 3)
    def _():
        out[cut:, :] = far_sums[...]


def late_kernel(early, gathered, near_first, far_second, near_sums, far_sums, three, held):
    mine = place()
    near_sums[...] = jnp.dot(near_first[...], gathered[mine ^ 2], preferred_element_type=jnp.float32)
    far_sums[...] = jnp.dot(far_second[...], gathered[mine ^ 3], preferred_element_type=jnp.float32)
    whole(3, early, near_sums, far_sums, held)
    encode(held[...], three)


def rest_kernel(early, near_sums, far_sums, one, two, kept_sums, held):
    for n, out in ((2, two), (1, one)):
        whole(n, early, near_sums, far_sums, held)
        encode(held[...], out)
    whole(0, early, near_sums, far_sums, kept_sums)


def first_kernel(residual, kept_sums, three, out):
    pairs = out.shape[0]
    out[...] = residual[...] + kept_sums[...] + decode(three, pairs, 0, pairs)


def last_kernel(base, two, one, out, total, sems):
    pairs = total.shape[0]
    size = pairs // PIECES
    started = copies(total, out, sems)
    for i, copy in enumerate(started):
        rows = (i * size, (i + 1) * size)
        total[rows[0] : rows[1], :] = base[rows[0] : rows[1], :] + decode(two, pairs, *rows) + decode(one, pairs, *rows)
        copy.start()
    for copy in started:
        copy.wait()


def swap(x, axis, step):
    return lax.ppermute(x, axis, [(i, i ^ step) for i in range(ROWS)])


def local_few(doubles, doubles_kept, integrals, integral_kept, residual):
    pairs, cd_local = doubles.shape
    width = integrals.shape[1]
    tiles = cd_local // TILE
    slots = tiles // GROUP * KEEP
    places = pltpu.SMEM((tiles + 1,), jnp.int32)
    sums_shape = jax.ShapeDtypeStruct((pairs, width), jnp.float32)
    parts = (DIRECT, pairs - DIRECT)
    blocks = [jax.ShapeDtypeStruct((rows, slots * TILE), doubles.dtype) for rows in parts]
    message = jax.ShapeDtypeStruct((pairs * width // TILE + HEAD, TILE), jnp.int16)
    doubles, doubles_kept, integrals, integral_kept = (
        pltpu.with_memory_space_constraint(x, pltpu.HBM) for x in (doubles, doubles_kept, integrals, integral_kept.T)
    )
    packed, first, second = pl.pallas_call(
        functools.partial(pack_kernel, tiles, slots),
        out_shape=[jax.ShapeDtypeStruct((pairs, slots * TILE), doubles.dtype)] + blocks,
        in_specs=[HBM, HBM],
        out_specs=[VMEM] * 3,
        scratch_shapes=[
            pltpu.SMEM(doubles_kept.shape, jnp.int32),
            pltpu.VMEM(doubles.shape, doubles.dtype),
            places,
            pltpu.SemaphoreType.DMA((PIECES + 1,)),
        ],
        compiler_params=PARAMS,
        name="pack",
    )(doubles_kept, doubles)
    near_second = swap(second, "rows", 2)
    pair = swap(packed, "rows", 1)
    far_first = swap(first, "rows", 3)
    near_first = swap(first, "rows", 2)
    far_second = swap(near_second, "rows", 1)
    gathered, product = pl.pallas_call(
        functools.partial(prepare_kernel, tiles, slots),
        out_shape=[jax.ShapeDtypeStruct((ROWS, slots * TILE, width), integrals.dtype), sums_shape],
        in_specs=[HBM, HBM, HBM, VMEM],
        out_specs=[VMEM] * 2,
        scratch_shapes=[
            pltpu.SMEM(doubles_kept.shape, jnp.int32),
            pltpu.SMEM(integral_kept.shape, jnp.int32),
            pltpu.VMEM(integrals.shape, integrals.dtype),
            places,
            pltpu.SemaphoreType.DMA((PIECES + 2,)),
        ],
        compiler_params=PARAMS,
        cost_estimate=cost(115 * 10**7),
        name="prepare",
    )(doubles_kept, integral_kept, integrals, packed)

    def on_vmem(kernel, name, flops, out_shape, *args, scratch=()):
        return pl.pallas_call(
            kernel,
            out_shape=out_shape,
            in_specs=[VMEM] * len(args),
            out_specs=jax.tree.map(lambda _: VMEM, out_shape),
            scratch_shapes=scratch,
            compiler_params=PARAMS,
            cost_estimate=cost(flops),
            name=name,
        )(*args)

    held = [pltpu.VMEM((pairs, width), jnp.float32)]
    part_sums = [jax.ShapeDtypeStruct((rows, width), jnp.float32) for rows in parts]
    all_sums = jax.ShapeDtypeStruct((ROWS, pairs, width), jnp.float32)
    early = on_vmem(early_kernel, "early", 0, all_sums, product, gathered, pair, near_second, far_first)
    near_sums, far_sums, three = on_vmem(
        late_kernel, "late", 10**11, part_sums + [message], early, gathered, near_first, far_second, scratch=held
    )
    one, two, kept_sums = on_vmem(
        rest_kernel, "rest", 0, [message] * 2 + [sums_shape], early, near_sums, far_sums, scratch=held
    )
    two, three, one = swap(two, "cols", 2), swap(three, "cols", 3), swap(one, "cols", 1)
    base = on_vmem(first_kernel, "first", 0, sums_shape, residual, kept_sums, three)
    return pl.pallas_call(
        last_kernel,
        out_shape=sums_shape,
        in_specs=[VMEM] * 3,
        out_specs=HBM,
        scratch_shapes=[pltpu.VMEM((pairs, width), jnp.float32), pltpu.SemaphoreType.DMA((PIECES,))],
        compiler_params=PARAMS,
        cost_estimate=cost(0),
        name="last",
    )(base, two, one)


def local_many(doubles, doubles_kept, integrals, integral_kept, residual):
    pairs, cd_local = doubles.shape
    tiles = cd_local // TILE
    blocks = lax.all_gather(doubles, "rows", axis=0).reshape(-1, pairs, tiles, TILE)
    blocks = blocks * doubles_kept.astype(doubles.dtype)[:, None, :, None]
    tiles_ab = integrals.shape[1] // TILE
    masked = integrals.reshape(tiles, TILE, tiles_ab, TILE) * integral_kept.astype(integrals.dtype)[:, None, :, None]
    sums = jnp.dot(
        blocks.reshape(-1, cd_local), masked.reshape(integrals.shape), preferred_element_type=jnp.float32
    )
    return residual + lax.psum_scatter(sums, "cols", scatter_dimension=0, tiled=True)


def solution(mesh):
    few = mesh.shape["rows"] == mesh.shape["cols"] == ROWS
    in_specs = (
        P(("groups", "rows"), "cols"),
        P("groups", "cols"),
        P(("groups", "cols"), "rows"),
        P(("groups", "cols"), "rows"),
        P(("groups", "cols"), "rows"),
    )
    out_specs = P(("groups", "cols"), "rows")
    return jax.shard_map(
        local_few if few else local_many, mesh=mesh, in_specs=in_specs, out_specs=out_specs, check_vma=False
    )
```

```python
import functools

import jax
import jax.numpy as jnp
from jax import lax
from jax.experimental import pallas as pl
from jax.experimental.pallas import tpu as pltpu
from jax.sharding import PartitionSpec as P

TILE = 128
GROUP = 8
KEEP = 4
HEAD = 16
STEPS = 8

VMEM = pl.BlockSpec(memory_space=pltpu.VMEM)
HBM = pl.BlockSpec(memory_space=pltpu.HBM)
PARAMS = pltpu.CompilerParams(vmem_limit_bytes=8 * 1024 * 1024)
DIRECT = 32
PIECES = 4
ROWS = 4


def cost(flops):
    return pl.CostEstimate(flops=flops, bytes_accessed=1024, transcendentals=0)


def list_kept(kept, row, tiles, places):
    at = jnp.int32(0)
    for tile in range(tiles):
        places[at] = jnp.int32(tile)
        at = at + kept[row, tile]


def copies(source, target, sems):
    size = source.shape[0] // PIECES
    rows = [pl.ds(i * size, size) for i in range(PIECES)]
    return [pltpu.make_async_copy(source.at[r], target.at[r], sems.at[i]) for i, r in enumerate(rows)]


def pack_kernel(tiles, slots, kept, doubles, packed, first, second, table, block, places, sems):
    table_copy = pltpu.make_async_copy(kept, table, sems.at[PIECES])
    block_copies = copies(doubles, block, sems)
    table_copy.start()
    for copy in block_copies:
        copy.start()
    table_copy.wait()
    list_kept(table, lax.axis_index("rows"), tiles, places)
    for copy in block_copies:
        copy.wait()
    cut = first.shape[0]
    for slot in range(slots):
        tile = block[:, pl.ds(pl.multiple_of(places[slot] * TILE, TILE), TILE)]
        to = slice(slot * TILE, (slot + 1) * TILE)
        packed[:, to] = tile
        first[:, to] = tile[:cut]
        second[:, to] = tile[cut:]


def prepare_kernel(tiles, slots, kept, int_kept, integrals, own, gathered, product, table, int_table, held, places, sems):
    started = copies(integrals, held, sems)
    for i, pair in enumerate(((kept, table), (int_kept, int_table)), PIECES):
        started.append(pltpu.make_async_copy(*pair, sems.at[i]))
    for copy in started:
        copy.start()
    for copy in started:
        copy.wait()
    row, col = lax.axis_index("rows"), lax.axis_index("cols")
    tiles_ab = integrals.shape[1] // TILE
    for n in range(ROWS):
        list_kept(table, col ^ n, tiles, places)
        for slot in range(slots):
            tile = places[slot]
            start = pl.multiple_of(tile * TILE, TILE)
            for ab in range(tiles_ab):
                part = held[pl.ds(start, TILE), ab * TILE : (ab + 1) * TILE]
                on = (int_table[ab, tile] != 0).astype(jnp.float32).astype(part.dtype)
                gathered[n, slot * TILE : (slot + 1) * TILE, ab * TILE : (ab + 1) * TILE] = part * on
    product[...] = jnp.dot(own[...], gathered[row ^ col], preferred_element_type=jnp.float32)


def encode(x, out):
    pairs, width = x.shape
    largest = jnp.max(jnp.abs(x), axis=0, keepdims=True)
    exponent = jnp.floor((14.95 - jnp.log2(jnp.maximum(largest, 1e-30))) * STEPS)
    code = jnp.round(x * jnp.exp2(exponent * (1.0 / STEPS))).astype(jnp.int32)
    bands = width // TILE
    each = HEAD // bands
    exponent = jnp.broadcast_to(exponent.astype(jnp.int32), (each, width))
    for band in range(bands):
        out[band * pairs : (band + 1) * pairs, :] = code[:, band * TILE : (band + 1) * TILE].astype(jnp.int16)
    head = jnp.concatenate([exponent[:, band * TILE : (band + 1) * TILE] for band in range(bands)], axis=0)
    out[bands * pairs :, :] = head.astype(jnp.int16)


def decode(message, pairs, start, stop):
    bands = (message.shape[0] - HEAD) // pairs
    each = HEAD // bands
    head = message[bands * pairs :, :].astype(jnp.int32).astype(jnp.float32)
    parts = []
    for band in range(bands):
        scale = jnp.exp2(head[band * each : band * each + 1, :] * (-1.0 / STEPS))
        code = message[band * pairs + start : band * pairs + stop, :]
        parts.append(code.astype(jnp.int32).astype(jnp.float32) * scale)
    return jnp.concatenate(parts, axis=1)


def place():
    return lax.axis_index("rows") ^ lax.axis_index("cols")


def early_kernel(product, gathered, pair, near_second, far_first, sums):
    mine = place()
    cut = far_first.shape[0]
    sums[mine] = product[...]
    sums[mine ^ 1] = jnp.dot(pair[...], gathered[mine ^ 1], preferred_element_type=jnp.float32)
    for step, start, block in ((2, cut, near_second), (3, 0, far_first)):
        sums[mine ^ step, start : start + block.shape[0], :] = jnp.dot(
            block[...], gathered[mine ^ step], preferred_element_type=jnp.float32
        )


def whole(n, early, near_sums, far_sums, out):
    cut = near_sums.shape[0]
    step = place() ^ n
    out[...] = early[n]

    @pl.when(step == 2)
    def _():
        out[:cut, :] = near_sums[...]

    @pl.when(step == 3)
    def _():
        out[cut:, :] = far_sums[...]


def late_kernel(early, gathered, near_first, far_second, near_sums, far_sums, two, held):
    mine = place()
    near_sums[...] = jnp.dot(near_first[...], gathered[mine ^ 2], preferred_element_type=jnp.float32)
    far_sums[...] = jnp.dot(far_second[...], gathered[mine ^ 3], preferred_element_type=jnp.float32)
    whole(2, early, near_sums, far_sums, held)
    encode(held[...], two)


def rest_kernel(early, near_sums, far_sums, one, three, kept_sums, held):
    for n, out in ((3, three), (1, one)):
        whole(n, early, near_sums, far_sums, held)
        encode(held[...], out)
    whole(0, early, near_sums, far_sums, kept_sums)


def first_kernel(residual, kept_sums, two, out):
    pairs = out.shape[0]
    out[...] = residual[...] + kept_sums[...] + decode(two, pairs, 0, pairs)


def last_kernel(base, three, one, out, total, sems):
    pairs = total.shape[0]
    size = pairs // PIECES
    started = copies(total, out, sems)
    for i, copy in enumerate(started):
        rows = (i * size, (i + 1) * size)
        total[rows[0] : rows[1], :] = base[rows[0] : rows[1], :] + decode(three, pairs, *rows) + decode(one, pairs, *rows)
        copy.start()
    for copy in started:
        copy.wait()


def swap(x, axis, step):
    return lax.ppermute(x, axis, [(i, i ^ step) for i in range(ROWS)])


def local_few(doubles, doubles_kept, integrals, integral_kept, residual):
    pairs, cd_local = doubles.shape
    width = integrals.shape[1]
    tiles = cd_local // TILE
    slots = tiles // GROUP * KEEP
    places = pltpu.SMEM((tiles + 1,), jnp.int32)
    sums_shape = jax.ShapeDtypeStruct((pairs, width), jnp.float32)
    parts = (DIRECT, pairs - DIRECT)
    blocks = [jax.ShapeDtypeStruct((rows, slots * TILE), doubles.dtype) for rows in parts]
    message = jax.ShapeDtypeStruct((pairs * width // TILE + HEAD, TILE), jnp.int16)
    doubles, doubles_kept, integrals, integral_kept = (
        pltpu.with_memory_space_constraint(x, pltpu.HBM) for x in (doubles, doubles_kept, integrals, integral_kept.T)
    )
    packed, first, second = pl.pallas_call(
        functools.partial(pack_kernel, tiles, slots),
        out_shape=[jax.ShapeDtypeStruct((pairs, slots * TILE), doubles.dtype)] + blocks,
        in_specs=[HBM, HBM],
        out_specs=[VMEM] * 3,
        scratch_shapes=[
            pltpu.SMEM(doubles_kept.shape, jnp.int32),
            pltpu.VMEM(doubles.shape, doubles.dtype),
            places,
            pltpu.SemaphoreType.DMA((PIECES + 1,)),
        ],
        compiler_params=PARAMS,
        name="pack",
    )(doubles_kept, doubles)
    near_second = swap(second, "rows", 2)
    pair = swap(packed, "rows", 1)
    far_first = swap(first, "rows", 3)
    near_first = swap(first, "rows", 2)
    far_second = swap(near_second, "rows", 1)
    gathered, product = pl.pallas_call(
        functools.partial(prepare_kernel, tiles, slots),
        out_shape=[jax.ShapeDtypeStruct((ROWS, slots * TILE, width), integrals.dtype), sums_shape],
        in_specs=[HBM, HBM, HBM, VMEM],
        out_specs=[VMEM] * 2,
        scratch_shapes=[
            pltpu.SMEM(doubles_kept.shape, jnp.int32),
            pltpu.SMEM(integral_kept.shape, jnp.int32),
            pltpu.VMEM(integrals.shape, integrals.dtype),
            places,
            pltpu.SemaphoreType.DMA((PIECES + 2,)),
        ],
        compiler_params=PARAMS,
        cost_estimate=cost(115 * 10**7),
        name="prepare",
    )(doubles_kept, integral_kept, integrals, packed)

    def on_vmem(kernel, name, flops, out_shape, *args, scratch=()):
        return pl.pallas_call(
            kernel,
            out_shape=out_shape,
            in_specs=[VMEM] * len(args),
            out_specs=jax.tree.map(lambda _: VMEM, out_shape),
            scratch_shapes=scratch,
            compiler_params=PARAMS,
            cost_estimate=cost(flops),
            name=name,
        )(*args)

    held = [pltpu.VMEM((pairs, width), jnp.float32)]
    part_sums = [jax.ShapeDtypeStruct((rows, width), jnp.float32) for rows in parts]
    all_sums = jax.ShapeDtypeStruct((ROWS, pairs, width), jnp.float32)
    early = on_vmem(early_kernel, "early", 0, all_sums, product, gathered, pair, near_second, far_first)
    near_sums, far_sums, two = on_vmem(
        late_kernel, "late", 10**11, part_sums + [message], early, gathered, near_first, far_second, scratch=held
    )
    one, three, kept_sums = on_vmem(
        rest_kernel, "rest", 0, [message] * 2 + [sums_shape], early, near_sums, far_sums, scratch=held
    )
    two, three, one = swap(two, "cols", 2), swap(three, "cols", 3), swap(one, "cols", 1)
    base = on_vmem(first_kernel, "first", 0, sums_shape, residual, kept_sums, two)
    return pl.pallas_call(
        last_kernel,
        out_shape=sums_shape,
        in_specs=[VMEM] * 3,
        out_specs=HBM,
        scratch_shapes=[pltpu.VMEM((pairs, width), jnp.float32), pltpu.SemaphoreType.DMA((PIECES,))],
        compiler_params=PARAMS,
        cost_estimate=cost(0),
        name="last",
    )(base, three, one)


def local_many(doubles, doubles_kept, integrals, integral_kept, residual):
    pairs, cd_local = doubles.shape
    tiles = cd_local // TILE
    blocks = lax.all_gather(doubles, "rows", axis=0).reshape(-1, pairs, tiles, TILE)
    blocks = blocks * doubles_kept.astype(doubles.dtype)[:, None, :, None]
    tiles_ab = integrals.shape[1] // TILE
    masked = integrals.reshape(tiles, TILE, tiles_ab, TILE) * integral_kept.astype(integrals.dtype)[:, None, :, None]
    sums = jnp.dot(
        blocks.reshape(-1, cd_local), masked.reshape(integrals.shape), preferred_element_type=jnp.float32
    )
    return residual + lax.psum_scatter(sums, "cols", scatter_dimension=0, tiled=True)


def solution(mesh):
    few = mesh.shape["rows"] == mesh.shape["cols"] == ROWS
    in_specs = (
        P(("groups", "rows"), "cols"),
        P("groups", "cols"),
        P(("groups", "cols"), "rows"),
        P(("groups", "cols"), "rows"),
        P(("groups", "cols"), "rows"),
    )
    out_specs = P(("groups", "cols"), "rows")
    return jax.shard_map(
        local_few if few else local_many, mesh=mesh, in_specs=in_specs, out_specs=out_specs, check_vma=False
    )
```

```python
import functools

import jax
import jax.numpy as jnp
from jax import lax
from jax.experimental import pallas as pl
from jax.experimental.pallas import tpu as pltpu
from jax.sharding import PartitionSpec as P

TILE = 128
GROUP = 8
KEEP = 4
HEAD = 16
STEPS = 8

VMEM = pl.BlockSpec(memory_space=pltpu.VMEM)
HBM = pl.BlockSpec(memory_space=pltpu.HBM)
PARAMS = pltpu.CompilerParams(vmem_limit_bytes=8 * 1024 * 1024)
DIRECT = 48
PIECES = 4
ROWS = 4


def cost(flops):
    return pl.CostEstimate(flops=flops, bytes_accessed=1024, transcendentals=0)


def list_kept(kept, row, tiles, places):
    at = jnp.int32(0)
    for tile in range(tiles):
        places[at] = jnp.int32(tile)
        at = at + kept[row, tile]


def copies(source, target, sems):
    size = source.shape[0] // PIECES
    rows = [pl.ds(i * size, size) for i in range(PIECES)]
    return [pltpu.make_async_copy(source.at[r], target.at[r], sems.at[i]) for i, r in enumerate(rows)]


def pack_kernel(tiles, slots, kept, doubles, packed, first, second, table, block, places, sems):
    table_copy = pltpu.make_async_copy(kept, table, sems.at[PIECES])
    block_copies = copies(doubles, block, sems)
    table_copy.start()
    for copy in block_copies:
        copy.start()
    table_copy.wait()
    list_kept(table, lax.axis_index("rows"), tiles, places)
    for copy in block_copies:
        copy.wait()
    cut = first.shape[0]
    for slot in range(slots):
        tile = block[:, pl.ds(pl.multiple_of(places[slot] * TILE, TILE), TILE)]
        to = slice(slot * TILE, (slot + 1) * TILE)
        packed[:, to] = tile
        first[:, to] = tile[:cut]
        second[:, to] = tile[cut:]


def prepare_kernel(tiles, slots, kept, int_kept, integrals, own, gathered, product, table, int_table, held, places, sems):
    started = copies(integrals, held, sems)
    for i, pair in enumerate(((kept, table), (int_kept, int_table)), PIECES):
        started.append(pltpu.make_async_copy(*pair, sems.at[i]))
    for copy in started:
        copy.start()
    for copy in started:
        copy.wait()
    row, col = lax.axis_index("rows"), lax.axis_index("cols")
    tiles_ab = integrals.shape[1] // TILE
    for n in range(ROWS):
        list_kept(table, col ^ n, tiles, places)
        for slot in range(slots):
            tile = places[slot]
            start = pl.multiple_of(tile * TILE, TILE)
            for ab in range(tiles_ab):
                part = held[pl.ds(start, TILE), ab * TILE : (ab + 1) * TILE]
                on = (int_table[ab, tile] != 0).astype(jnp.float32).astype(part.dtype)
                gathered[n, slot * TILE : (slot + 1) * TILE, ab * TILE : (ab + 1) * TILE] = part * on
    product[...] = jnp.dot(own[...], gathered[row ^ col], preferred_element_type=jnp.float32)


def encode(x, out):
    pairs, width = x.shape
    largest = jnp.max(jnp.abs(x), axis=0, keepdims=True)
    exponent = jnp.floor((14.95 - jnp.log2(jnp.maximum(largest, 1e-30))) * STEPS)
    code = jnp.round(x * jnp.exp2(exponent * (1.0 / STEPS))).astype(jnp.int32)
    bands = width // TILE
    each = HEAD // bands
    exponent = jnp.broadcast_to(exponent.astype(jnp.int32), (each, width))
    for band in range(bands):
        out[band * pairs : (band + 1) * pairs, :] = code[:, band * TILE : (band + 1) * TILE].astype(jnp.int16)
    head = jnp.concatenate([exponent[:, band * TILE : (band + 1) * TILE] for band in range(bands)], axis=0)
    out[bands * pairs :, :] = head.astype(jnp.int16)


def decode(message, pairs, start, stop):
    bands = (message.shape[0] - HEAD) // pairs
    each = HEAD // bands
    head = message[bands * pairs :, :].astype(jnp.int32).astype(jnp.float32)
    parts = []
    for band in range(bands):
        scale = jnp.exp2(head[band * each : band * each + 1, :] * (-1.0 / STEPS))
        code = message[band * pairs + start : band * pairs + stop, :]
        parts.append(code.astype(jnp.int32).astype(jnp.float32) * scale)
    return jnp.concatenate(parts, axis=1)


def place():
    return lax.axis_index("rows") ^ lax.axis_index("cols")


def far_steps(col):
    return 3 - col // 2, 2 + col // 2


def early_kernel(product, gathered, pair, near_second, far_first, sums):
    mine = place()
    cut = far_first.shape[0]
    sums[mine] = product[...]
    sums[mine ^ 1] = jnp.dot(pair[...], gathered[mine ^ 1], preferred_element_type=jnp.float32)
    for step, start, block in ((2, cut, near_second), (3, 0, far_first)):
        sums[mine ^ step, start : start + block.shape[0], :] = jnp.dot(
            block[...], gathered[mine ^ step], preferred_element_type=jnp.float32
        )


def whole(n, early, near_sums, far_sums, out):
    cut = near_sums.shape[0]
    step = place() ^ n
    out[...] = early[n]

    @pl.when(step == 2)
    def _():
        out[:cut, :] = near_sums[...]

    @pl.when(step == 3)
    def _():
        out[cut:, :] = far_sums[...]


def late_kernel(early, gathered, near_first, far_second, near_sums, far_sums, one_far, held):
    mine = place()
    near_sums[...] = jnp.dot(near_first[...], gathered[mine ^ 2], preferred_element_type=jnp.float32)
    far_sums[...] = jnp.dot(far_second[...], gathered[mine ^ 3], preferred_element_type=jnp.float32)
    whole(far_steps(lax.axis_index("cols"))[0], early, near_sums, far_sums, held)
    encode(held[...], one_far)


def rest_kernel(early, near_sums, far_sums, one, other_far, kept_sums, held):
    for n, out in ((far_steps(lax.axis_index("cols"))[1], other_far), (1, one)):
        whole(n, early, near_sums, far_sums, held)
        encode(held[...], out)
    whole(0, early, near_sums, far_sums, kept_sums)


def first_kernel(residual, kept_sums, one_far, out):
    pairs = out.shape[0]
    out[...] = residual[...] + kept_sums[...] + decode(one_far, pairs, 0, pairs)


def last_kernel(base, other_far, one, out, total, sems):
    pairs = total.shape[0]
    size = pairs // PIECES
    started = copies(total, out, sems)
    for i, copy in enumerate(started):
        rows = (i * size, (i + 1) * size)
        total[rows[0] : rows[1], :] = base[rows[0] : rows[1], :] + decode(other_far, pairs, *rows) + decode(one, pairs, *rows)
        copy.start()
    for copy in started:
        copy.wait()


def swap(x, axis, step):
    return lax.ppermute(x, axis, [(i, i ^ step) for i in range(ROWS)])


def local_few(doubles, doubles_kept, integrals, integral_kept, residual):
    pairs, cd_local = doubles.shape
    width = integrals.shape[1]
    tiles = cd_local // TILE
    slots = tiles // GROUP * KEEP
    places = pltpu.SMEM((tiles + 1,), jnp.int32)
    sums_shape = jax.ShapeDtypeStruct((pairs, width), jnp.float32)
    parts = (DIRECT, pairs - DIRECT)
    blocks = [jax.ShapeDtypeStruct((rows, slots * TILE), doubles.dtype) for rows in parts]
    message = jax.ShapeDtypeStruct((pairs * width // TILE + HEAD, TILE), jnp.int16)
    doubles, doubles_kept, integrals, integral_kept = (
        pltpu.with_memory_space_constraint(x, pltpu.HBM) for x in (doubles, doubles_kept, integrals, integral_kept.T)
    )
    packed, first, second = pl.pallas_call(
        functools.partial(pack_kernel, tiles, slots),
        out_shape=[jax.ShapeDtypeStruct((pairs, slots * TILE), doubles.dtype)] + blocks,
        in_specs=[HBM, HBM],
        out_specs=[VMEM] * 3,
        scratch_shapes=[
            pltpu.SMEM(doubles_kept.shape, jnp.int32),
            pltpu.VMEM(doubles.shape, doubles.dtype),
            places,
            pltpu.SemaphoreType.DMA((PIECES + 1,)),
        ],
        compiler_params=PARAMS,
        name="pack",
    )(doubles_kept, doubles)
    near_second = swap(second, "rows", 2)
    pair = swap(packed, "rows", 1)
    far_first = swap(first, "rows", 3)
    near_first = swap(first, "rows", 2)
    far_second = swap(near_second, "rows", 1)
    gathered, product = pl.pallas_call(
        functools.partial(prepare_kernel, tiles, slots),
        out_shape=[jax.ShapeDtypeStruct((ROWS, slots * TILE, width), integrals.dtype), sums_shape],
        in_specs=[HBM, HBM, HBM, VMEM],
        out_specs=[VMEM] * 2,
        scratch_shapes=[
            pltpu.SMEM(doubles_kept.shape, jnp.int32),
            pltpu.SMEM(integral_kept.shape, jnp.int32),
            pltpu.VMEM(integrals.shape, integrals.dtype),
            places,
            pltpu.SemaphoreType.DMA((PIECES + 2,)),
        ],
        compiler_params=PARAMS,
        cost_estimate=cost(115 * 10**7),
        name="prepare",
    )(doubles_kept, integral_kept, integrals, packed)

    def on_vmem(kernel, name, flops, out_shape, *args, scratch=()):
        return pl.pallas_call(
            kernel,
            out_shape=out_shape,
            in_specs=[VMEM] * len(args),
            out_specs=jax.tree.map(lambda _: VMEM, out_shape),
            scratch_shapes=scratch,
            compiler_params=PARAMS,
            cost_estimate=cost(flops),
            name=name,
        )(*args)

    held = [pltpu.VMEM((pairs, width), jnp.float32)]
    part_sums = [jax.ShapeDtypeStruct((rows, width), jnp.float32) for rows in parts]
    all_sums = jax.ShapeDtypeStruct((ROWS, pairs, width), jnp.float32)
    early = on_vmem(early_kernel, "early", 0, all_sums, product, gathered, pair, near_second, far_first)
    near_sums, far_sums, one_far = on_vmem(
        late_kernel, "late", 10**11, part_sums + [message], early, gathered, near_first, far_second, scratch=held
    )
    one, other_far, kept_sums = on_vmem(
        rest_kernel, "rest", 0, [message] * 2 + [sums_shape], early, near_sums, far_sums, scratch=held
    )
    one_far, other_far = (
        lax.ppermute(x, "cols", [(col, col ^ far_steps(col)[i]) for col in range(ROWS)])
        for i, x in enumerate((one_far, other_far))
    )
    one = swap(one, "cols", 1)
    base = on_vmem(first_kernel, "first", 0, sums_shape, residual, kept_sums, one_far)
    return pl.pallas_call(
        last_kernel,
        out_shape=sums_shape,
        in_specs=[VMEM] * 3,
        out_specs=HBM,
        scratch_shapes=[pltpu.VMEM((pairs, width), jnp.float32), pltpu.SemaphoreType.DMA((PIECES,))],
        compiler_params=PARAMS,
        cost_estimate=cost(0),
        name="last",
    )(base, other_far, one)


def local_many(doubles, doubles_kept, integrals, integral_kept, residual):
    pairs, cd_local = doubles.shape
    tiles = cd_local // TILE
    blocks = lax.all_gather(doubles, "rows", axis=0).reshape(-1, pairs, tiles, TILE)
    blocks = blocks * doubles_kept.astype(doubles.dtype)[:, None, :, None]
    tiles_ab = integrals.shape[1] // TILE
    masked = integrals.reshape(tiles, TILE, tiles_ab, TILE) * integral_kept.astype(integrals.dtype)[:, None, :, None]
    sums = jnp.dot(
        blocks.reshape(-1, cd_local), masked.reshape(integrals.shape), preferred_element_type=jnp.float32
    )
    return residual + lax.psum_scatter(sums, "cols", scatter_dimension=0, tiled=True)


def solution(mesh):
    few = mesh.shape["rows"] == mesh.shape["cols"] == ROWS
    in_specs = (
        P(("groups", "rows"), "cols"),
        P("groups", "cols"),
        P(("groups", "cols"), "rows"),
        P(("groups", "cols"), "rows"),
        P(("groups", "cols"), "rows"),
    )
    out_specs = P(("groups", "cols"), "rows")
    return jax.shard_map(
        local_few if few else local_many, mesh=mesh, in_specs=in_specs, out_specs=out_specs, check_vma=False
    )
```

```python
import functools

import jax
import jax.numpy as jnp
from jax import lax
from jax.experimental import pallas as pl
from jax.experimental.pallas import tpu as pltpu
from jax.sharding import PartitionSpec as P

TILE = 128
GROUP = 8
KEEP = 4
HEAD = 16
STEPS = 8

VMEM = pl.BlockSpec(memory_space=pltpu.VMEM)
HBM = pl.BlockSpec(memory_space=pltpu.HBM)
PARAMS = pltpu.CompilerParams(vmem_limit_bytes=8 * 1024 * 1024)
DIRECT = 64
PIECES = 4
ROWS = 4


def cost(flops):
    return pl.CostEstimate(flops=flops, bytes_accessed=1024, transcendentals=0)


def list_kept(kept, row, tiles, places):
    at = jnp.int32(0)
    for tile in range(tiles):
        places[at] = jnp.int32(tile)
        at = at + kept[row, tile]


def copies(source, target, sems):
    size = source.shape[0] // PIECES
    rows = [pl.ds(i * size, size) for i in range(PIECES)]
    return [pltpu.make_async_copy(source.at[r], target.at[r], sems.at[i]) for i, r in enumerate(rows)]


def pack_kernel(tiles, slots, kept, doubles, packed, first, second, table, block, places, sems):
    table_copy = pltpu.make_async_copy(kept, table, sems.at[PIECES])
    block_copies = copies(doubles, block, sems)
    table_copy.start()
    for copy in block_copies:
        copy.start()
    table_copy.wait()
    list_kept(table, lax.axis_index("rows"), tiles, places)
    for copy in block_copies:
        copy.wait()
    cut = first.shape[0]
    for slot in range(slots):
        tile = block[:, pl.ds(pl.multiple_of(places[slot] * TILE, TILE), TILE)]
        to = slice(slot * TILE, (slot + 1) * TILE)
        packed[:, to] = tile
        first[:, to] = tile[:cut]
        second[:, to] = tile[cut:]


def prepare_kernel(tiles, slots, kept, int_kept, integrals, own, gathered, product, table, int_table, held, places, sems):
    started = copies(integrals, held, sems)
    for i, pair in enumerate(((kept, table), (int_kept, int_table)), PIECES):
        started.append(pltpu.make_async_copy(*pair, sems.at[i]))
    for copy in started:
        copy.start()
    for copy in started:
        copy.wait()
    row, col = lax.axis_index("rows"), lax.axis_index("cols")
    tiles_ab = integrals.shape[1] // TILE
    for n in range(ROWS):
        list_kept(table, col ^ n, tiles, places)
        for slot in range(slots):
            tile = places[slot]
            start = pl.multiple_of(tile * TILE, TILE)
            for ab in range(tiles_ab):
                part = held[pl.ds(start, TILE), ab * TILE : (ab + 1) * TILE]
                on = (int_table[ab, tile] != 0).astype(jnp.float32).astype(part.dtype)
                gathered[n, slot * TILE : (slot + 1) * TILE, ab * TILE : (ab + 1) * TILE] = part * on
    product[...] = jnp.dot(own[...], gathered[row ^ col], preferred_element_type=jnp.float32)


def encode(x, out):
    pairs, width = x.shape
    largest = jnp.max(jnp.abs(x), axis=0, keepdims=True)
    exponent = jnp.floor((14.95 - jnp.log2(jnp.maximum(largest, 1e-30))) * STEPS)
    code = jnp.round(x * jnp.exp2(exponent * (1.0 / STEPS))).astype(jnp.int32)
    bands = width // TILE
    each = HEAD // bands
    exponent = jnp.broadcast_to(exponent.astype(jnp.int32), (each, width))
    for band in range(bands):
        out[band * pairs : (band + 1) * pairs, :] = code[:, band * TILE : (band + 1) * TILE].astype(jnp.int16)
    head = jnp.concatenate([exponent[:, band * TILE : (band + 1) * TILE] for band in range(bands)], axis=0)
    out[bands * pairs :, :] = head.astype(jnp.int16)


def decode(message, pairs, start, stop):
    bands = (message.shape[0] - HEAD) // pairs
    each = HEAD // bands
    head = message[bands * pairs :, :].astype(jnp.int32).astype(jnp.float32)
    parts = []
    for band in range(bands):
        scale = jnp.exp2(head[band * each : band * each + 1, :] * (-1.0 / STEPS))
        code = message[band * pairs + start : band * pairs + stop, :]
        parts.append(code.astype(jnp.int32).astype(jnp.float32) * scale)
    return jnp.concatenate(parts, axis=1)


def place():
    return lax.axis_index("rows") ^ lax.axis_index("cols")


def far_steps(col):
    return 3 - col // 2, 2 + col // 2


def early_kernel(product, gathered, pair, near_second, far_first, sums):
    mine = place()
    cut = far_first.shape[0]
    sums[mine] = product[...]
    sums[mine ^ 1] = jnp.dot(pair[...], gathered[mine ^ 1], preferred_element_type=jnp.float32)
    for step, start, block in ((2, cut, near_second), (3, 0, far_first)):
        sums[mine ^ step, start : start + block.shape[0], :] = jnp.dot(
            block[...], gathered[mine ^ step], preferred_element_type=jnp.float32
        )


def whole(n, early, near_sums, far_sums, out):
    cut = near_sums.shape[0]
    step = place() ^ n
    out[...] = early[n]

    @pl.when(step == 2)
    def _():
        out[:cut, :] = near_sums[...]

    @pl.when(step == 3)
    def _():
        out[cut:, :] = far_sums[...]


def late_kernel(early, gathered, near_first, far_second, near_sums, far_sums, one_far, held):
    mine = place()
    near_sums[...] = jnp.dot(near_first[...], gathered[mine ^ 2], preferred_element_type=jnp.float32)
    far_sums[...] = jnp.dot(far_second[...], gathered[mine ^ 3], preferred_element_type=jnp.float32)
    whole(far_steps(lax.axis_index("cols"))[0], early, near_sums, far_sums, held)
    encode(held[...], one_far)


def rest_kernel(early, near_sums, far_sums, one, other_far, kept_sums, held):
    for n, out in ((far_steps(lax.axis_index("cols"))[1], other_far), (1, one)):
        whole(n, early, near_sums, far_sums, held)
        encode(held[...], out)
    whole(0, early, near_sums, far_sums, kept_sums)


def first_kernel(residual, kept_sums, one_far, out):
    pairs = out.shape[0]
    out[...] = residual[...] + kept_sums[...] + decode(one_far, pairs, 0, pairs)


def last_kernel(base, other_far, one, out, total, sems):
    pairs = total.shape[0]
    size = pairs // PIECES
    started = copies(total, out, sems)
    for i, copy in enumerate(started):
        rows = (i * size, (i + 1) * size)
        total[rows[0] : rows[1], :] = base[rows[0] : rows[1], :] + decode(other_far, pairs, *rows) + decode(one, pairs, *rows)
        copy.start()
    for copy in started:
        copy.wait()


def swap(x, axis, step):
    return lax.ppermute(x, axis, [(i, i ^ step) for i in range(ROWS)])


def local_few(doubles, doubles_kept, integrals, integral_kept, residual):
    pairs, cd_local = doubles.shape
    width = integrals.shape[1]
    tiles = cd_local // TILE
    slots = tiles // GROUP * KEEP
    places = pltpu.SMEM((tiles + 1,), jnp.int32)
    sums_shape = jax.ShapeDtypeStruct((pairs, width), jnp.float32)
    parts = (DIRECT, pairs - DIRECT)
    blocks = [jax.ShapeDtypeStruct((rows, slots * TILE), doubles.dtype) for rows in parts]
    message = jax.ShapeDtypeStruct((pairs * width // TILE + HEAD, TILE), jnp.int16)
    doubles, doubles_kept, integrals, integral_kept = (
        pltpu.with_memory_space_constraint(x, pltpu.HBM) for x in (doubles, doubles_kept, integrals, integral_kept.T)
    )
    packed, first, second = pl.pallas_call(
        functools.partial(pack_kernel, tiles, slots),
        out_shape=[jax.ShapeDtypeStruct((pairs, slots * TILE), doubles.dtype)] + blocks,
        in_specs=[HBM, HBM],
        out_specs=[VMEM] * 3,
        scratch_shapes=[
            pltpu.SMEM(doubles_kept.shape, jnp.int32),
            pltpu.VMEM(doubles.shape, doubles.dtype),
            places,
            pltpu.SemaphoreType.DMA((PIECES + 1,)),
        ],
        compiler_params=PARAMS,
        name="pack",
    )(doubles_kept, doubles)
    near_second = swap(second, "rows", 2)
    pair = swap(packed, "rows", 1)
    far_first = swap(first, "rows", 3)
    near_first = swap(first, "rows", 2)
    far_second = swap(near_second, "rows", 1)
    gathered, product = pl.pallas_call(
        functools.partial(prepare_kernel, tiles, slots),
        out_shape=[jax.ShapeDtypeStruct((ROWS, slots * TILE, width), integrals.dtype), sums_shape],
        in_specs=[HBM, HBM, HBM, VMEM],
        out_specs=[VMEM] * 2,
        scratch_shapes=[
            pltpu.SMEM(doubles_kept.shape, jnp.int32),
            pltpu.SMEM(integral_kept.shape, jnp.int32),
            pltpu.VMEM(integrals.shape, integrals.dtype),
            places,
            pltpu.SemaphoreType.DMA((PIECES + 2,)),
        ],
        compiler_params=PARAMS,
        cost_estimate=cost(10**9),
        name="prepare",
    )(doubles_kept, integral_kept, integrals, packed)

    def on_vmem(kernel, name, flops, out_shape, *args, scratch=()):
        return pl.pallas_call(
            kernel,
            out_shape=out_shape,
            in_specs=[VMEM] * len(args),
            out_specs=jax.tree.map(lambda _: VMEM, out_shape),
            scratch_shapes=scratch,
            compiler_params=PARAMS,
            cost_estimate=cost(flops),
            name=name,
        )(*args)

    held = [pltpu.VMEM((pairs, width), jnp.float32)]
    part_sums = [jax.ShapeDtypeStruct((rows, width), jnp.float32) for rows in parts]
    all_sums = jax.ShapeDtypeStruct((ROWS, pairs, width), jnp.float32)
    early = on_vmem(early_kernel, "early", 0, all_sums, product, gathered, pair, near_second, far_first)
    near_sums, far_sums, one_far = on_vmem(
        late_kernel, "late", 10**11, part_sums + [message], early, gathered, near_first, far_second, scratch=held
    )
    one, other_far, kept_sums = on_vmem(
        rest_kernel, "rest", 0, [message] * 2 + [sums_shape], early, near_sums, far_sums, scratch=held
    )
    one_far, other_far = (
        lax.ppermute(x, "cols", [(col, col ^ far_steps(col)[i]) for col in range(ROWS)])
        for i, x in enumerate((one_far, other_far))
    )
    one = swap(one, "cols", 1)
    base = on_vmem(first_kernel, "first", 0, sums_shape, residual, kept_sums, one_far)
    return pl.pallas_call(
        last_kernel,
        out_shape=sums_shape,
        in_specs=[VMEM] * 3,
        out_specs=HBM,
        scratch_shapes=[pltpu.VMEM((pairs, width), jnp.float32), pltpu.SemaphoreType.DMA((PIECES,))],
        compiler_params=PARAMS,
        cost_estimate=cost(0),
        name="last",
    )(base, other_far, one)


def local_many(doubles, doubles_kept, integrals, integral_kept, residual):
    pairs, cd_local = doubles.shape
    tiles = cd_local // TILE
    blocks = lax.all_gather(doubles, "rows", axis=0).reshape(-1, pairs, tiles, TILE)
    blocks = blocks * doubles_kept.astype(doubles.dtype)[:, None, :, None]
    tiles_ab = integrals.shape[1] // TILE
    masked = integrals.reshape(tiles, TILE, tiles_ab, TILE) * integral_kept.astype(integrals.dtype)[:, None, :, None]
    sums = jnp.dot(
        blocks.reshape(-1, cd_local), masked.reshape(integrals.shape), preferred_element_type=jnp.float32
    )
    return residual + lax.psum_scatter(sums, "cols", scatter_dimension=0, tiled=True)


def solution(mesh):
    few = mesh.shape["rows"] == mesh.shape["cols"] == ROWS
    in_specs = (
        P(("groups", "rows"), "cols"),
        P("groups", "cols"),
        P(("groups", "cols"), "rows"),
        P(("groups", "cols"), "rows"),
        P(("groups", "cols"), "rows"),
    )
    out_specs = P(("groups", "cols"), "rows")
    return jax.shard_map(
        local_few if few else local_many, mesh=mesh, in_specs=in_specs, out_specs=out_specs, check_vma=False
    )
```

```python
import functools

import jax
import jax.numpy as jnp
from jax import lax
from jax.experimental import pallas as pl
from jax.experimental.pallas import tpu as pltpu
from jax.sharding import PartitionSpec as P

TILE = 128
GROUP = 8
KEEP = 4
HEAD = 16
STEPS = 8

VMEM = pl.BlockSpec(memory_space=pltpu.VMEM)
HBM = pl.BlockSpec(memory_space=pltpu.HBM)
PARAMS = pltpu.CompilerParams(vmem_limit_bytes=8 * 1024 * 1024)
DIRECT = 48
PIECES = 4
ROWS = 4


def cost(flops):
    return pl.CostEstimate(flops=flops, bytes_accessed=1024, transcendentals=0)


def list_kept(kept, row, tiles, places):
    at = jnp.int32(0)
    for tile in range(tiles):
        places[at] = jnp.int32(tile)
        at = at + kept[row, tile]


def copies(source, target, sems):
    size = source.shape[0] // PIECES
    rows = [pl.ds(i * size, size) for i in range(PIECES)]
    return [pltpu.make_async_copy(source.at[r], target.at[r], sems.at[i]) for i, r in enumerate(rows)]


def pack_kernel(tiles, slots, kept, doubles, packed, first, second, table, block, places, sems):
    table_copy = pltpu.make_async_copy(kept, table, sems.at[PIECES])
    block_copies = copies(doubles, block, sems)
    table_copy.start()
    for copy in block_copies:
        copy.start()
    table_copy.wait()
    list_kept(table, lax.axis_index("rows"), tiles, places)
    for copy in block_copies:
        copy.wait()
    cut = first.shape[0]
    for slot in range(slots):
        tile = block[:, pl.ds(pl.multiple_of(places[slot] * TILE, TILE), TILE)]
        to = slice(slot * TILE, (slot + 1) * TILE)
        packed[:, to] = tile
        first[:, to] = tile[:cut]
        second[:, to] = tile[cut:]


def prepare_kernel(tiles, slots, kept, int_kept, integrals, own, gathered, product, table, int_table, held, places, sems):
    started = copies(integrals, held, sems)
    for i, pair in enumerate(((kept, table), (int_kept, int_table)), PIECES):
        started.append(pltpu.make_async_copy(*pair, sems.at[i]))
    for copy in started:
        copy.start()
    for copy in started:
        copy.wait()
    row, col = lax.axis_index("rows"), lax.axis_index("cols")
    tiles_ab = integrals.shape[1] // TILE
    for n in range(ROWS):
        list_kept(table, col ^ n, tiles, places)
        for slot in range(slots):
            tile = places[slot]
            start = pl.multiple_of(tile * TILE, TILE)
            for ab in range(tiles_ab):
                part = held[pl.ds(start, TILE), ab * TILE : (ab + 1) * TILE]
                on = (int_table[ab, tile] != 0).astype(jnp.float32).astype(part.dtype)
                gathered[n, slot * TILE : (slot + 1) * TILE, ab * TILE : (ab + 1) * TILE] = part * on
    product[...] = jnp.dot(own[...], gathered[row ^ col], preferred_element_type=jnp.float32)


def encode(x, out):
    pairs, width = x.shape
    largest = jnp.max(jnp.abs(x), axis=0, keepdims=True)
    exponent = jnp.floor((14.95 - jnp.log2(jnp.maximum(largest, 1e-30))) * STEPS)
    code = jnp.round(x * jnp.exp2(exponent * (1.0 / STEPS))).astype(jnp.int32)
    bands = width // TILE
    each = HEAD // bands
    exponent = jnp.broadcast_to(exponent.astype(jnp.int32), (each, width))
    for band in range(bands):
        out[band * pairs : (band + 1) * pairs, :] = code[:, band * TILE : (band + 1) * TILE].astype(jnp.int16)
    head = jnp.concatenate([exponent[:, band * TILE : (band + 1) * TILE] for band in range(bands)], axis=0)
    out[bands * pairs :, :] = head.astype(jnp.int16)


def decode(message, pairs, start, stop):
    bands = (message.shape[0] - HEAD) // pairs
    each = HEAD // bands
    head = message[bands * pairs :, :].astype(jnp.int32).astype(jnp.float32)
    parts = []
    for band in range(bands):
        scale = jnp.exp2(head[band * each : band * each + 1, :] * (-1.0 / STEPS))
        code = message[band * pairs + start : band * pairs + stop, :]
        parts.append(code.astype(jnp.int32).astype(jnp.float32) * scale)
    return jnp.concatenate(parts, axis=1)


def place():
    return lax.axis_index("rows") ^ lax.axis_index("cols")


def far_steps(col):
    return 3 - col // 2, 2 + col // 2


def early_kernel(product, gathered, pair, near_second, far_first, near_first, sums):
    mine = place()
    cut = far_first.shape[0]
    sums[mine] = product[...]
    sums[mine ^ 1] = jnp.dot(pair[...], gathered[mine ^ 1], preferred_element_type=jnp.float32)
    for step, start, block in ((2, cut, near_second), (3, 0, far_first), (2, 0, near_first)):
        sums[mine ^ step, start : start + block.shape[0], :] = jnp.dot(
            block[...], gathered[mine ^ step], preferred_element_type=jnp.float32
        )


def whole(n, early, far_sums, out):
    out[...] = early[n]

    @pl.when((place() ^ n) == 3)
    def _():
        out[out.shape[0] - far_sums.shape[0] :, :] = far_sums[...]


def late_kernel(early, gathered, far_second, far_sums, one_far, held):
    far_sums[...] = jnp.dot(far_second[...], gathered[place() ^ 3], preferred_element_type=jnp.float32)
    whole(far_steps(lax.axis_index("cols"))[0], early, far_sums, held)
    encode(held[...], one_far)


def rest_kernel(early, far_sums, one, other_far, kept_sums, held):
    for n, out in ((far_steps(lax.axis_index("cols"))[1], other_far), (1, one)):
        whole(n, early, far_sums, held)
        encode(held[...], out)
    whole(0, early, far_sums, kept_sums)


def first_kernel(residual, kept_sums, one_far, out):
    pairs = out.shape[0]
    out[...] = residual[...] + kept_sums[...] + decode(one_far, pairs, 0, pairs)


def last_kernel(base, other_far, one, out, total, sems):
    pairs = total.shape[0]
    size = pairs // PIECES
    started = copies(total, out, sems)
    for i, copy in enumerate(started):
        rows = (i * size, (i + 1) * size)
        total[rows[0] : rows[1], :] = base[rows[0] : rows[1], :] + decode(other_far, pairs, *rows) + decode(one, pairs, *rows)
        copy.start()
    for copy in started:
        copy.wait()


def swap(x, axis, step):
    return lax.ppermute(x, axis, [(i, i ^ step) for i in range(ROWS)])


def local_few(doubles, doubles_kept, integrals, integral_kept, residual):
    pairs, cd_local = doubles.shape
    width = integrals.shape[1]
    tiles = cd_local // TILE
    slots = tiles // GROUP * KEEP
    places = pltpu.SMEM((tiles + 1,), jnp.int32)
    sums_shape = jax.ShapeDtypeStruct((pairs, width), jnp.float32)
    parts = (DIRECT, pairs - DIRECT)
    blocks = [jax.ShapeDtypeStruct((rows, slots * TILE), doubles.dtype) for rows in parts]
    message = jax.ShapeDtypeStruct((pairs * width // TILE + HEAD, TILE), jnp.int16)
    doubles, doubles_kept, integrals, integral_kept = (
        pltpu.with_memory_space_constraint(x, pltpu.HBM) for x in (doubles, doubles_kept, integrals, integral_kept.T)
    )
    packed, first, second = pl.pallas_call(
        functools.partial(pack_kernel, tiles, slots),
        out_shape=[jax.ShapeDtypeStruct((pairs, slots * TILE), doubles.dtype)] + blocks,
        in_specs=[HBM, HBM],
        out_specs=[VMEM] * 3,
        scratch_shapes=[
            pltpu.SMEM(doubles_kept.shape, jnp.int32),
            pltpu.VMEM(doubles.shape, doubles.dtype),
            places,
            pltpu.SemaphoreType.DMA((PIECES + 1,)),
        ],
        compiler_params=PARAMS,
        name="pack",
    )(doubles_kept, doubles)
    near_second = swap(second, "rows", 2)
    pair = swap(packed, "rows", 1)
    far_first = swap(first, "rows", 3)
    near_first = swap(first, "rows", 2)
    far_second = swap(near_second, "rows", 1)
    gathered, product = pl.pallas_call(
        functools.partial(prepare_kernel, tiles, slots),
        out_shape=[jax.ShapeDtypeStruct((ROWS, slots * TILE, width), integrals.dtype), sums_shape],
        in_specs=[HBM, HBM, HBM, VMEM],
        out_specs=[VMEM] * 2,
        scratch_shapes=[
            pltpu.SMEM(doubles_kept.shape, jnp.int32),
            pltpu.SMEM(integral_kept.shape, jnp.int32),
            pltpu.VMEM(integrals.shape, integrals.dtype),
            places,
            pltpu.SemaphoreType.DMA((PIECES + 2,)),
        ],
        compiler_params=PARAMS,
        cost_estimate=cost(115 * 10**7),
        name="prepare",
    )(doubles_kept, integral_kept, integrals, packed)

    def on_vmem(kernel, name, flops, out_shape, *args, scratch=()):
        return pl.pallas_call(
            kernel,
            out_shape=out_shape,
            in_specs=[VMEM] * len(args),
            out_specs=jax.tree.map(lambda _: VMEM, out_shape),
            scratch_shapes=scratch,
            compiler_params=PARAMS,
            cost_estimate=cost(flops),
            name=name,
        )(*args)

    held = [pltpu.VMEM((pairs, width), jnp.float32)]
    late_sums = jax.ShapeDtypeStruct((parts[1], width), jnp.float32)
    all_sums = jax.ShapeDtypeStruct((ROWS, pairs, width), jnp.float32)
    early = on_vmem(early_kernel, "early", 0, all_sums, product, gathered, pair, near_second, far_first, near_first)
    far_sums, one_far = on_vmem(
        late_kernel, "late", 10**11, [late_sums, message], early, gathered, far_second, scratch=held
    )
    one, other_far, kept_sums = on_vmem(
        rest_kernel, "rest", 0, [message] * 2 + [sums_shape], early, far_sums, scratch=held
    )
    one_far, other_far = (
        lax.ppermute(x, "cols", [(col, col ^ far_steps(col)[i]) for col in range(ROWS)])
        for i, x in enumerate((one_far, other_far))
    )
    one = swap(one, "cols", 1)
    base = on_vmem(first_kernel, "first", 0, sums_shape, residual, kept_sums, one_far)
    return pl.pallas_call(
        last_kernel,
        out_shape=sums_shape,
        in_specs=[VMEM] * 3,
        out_specs=HBM,
        scratch_shapes=[pltpu.VMEM((pairs, width), jnp.float32), pltpu.SemaphoreType.DMA((PIECES,))],
        compiler_params=PARAMS,
        cost_estimate=cost(0),
        name="last",
    )(base, other_far, one)


def local_many(doubles, doubles_kept, integrals, integral_kept, residual):
    pairs, cd_local = doubles.shape
    tiles = cd_local // TILE
    blocks = lax.all_gather(doubles, "rows", axis=0).reshape(-1, pairs, tiles, TILE)
    blocks = blocks * doubles_kept.astype(doubles.dtype)[:, None, :, None]
    tiles_ab = integrals.shape[1] // TILE
    masked = integrals.reshape(tiles, TILE, tiles_ab, TILE) * integral_kept.astype(integrals.dtype)[:, None, :, None]
    sums = jnp.dot(
        blocks.reshape(-1, cd_local), masked.reshape(integrals.shape), preferred_element_type=jnp.float32
    )
    return residual + lax.psum_scatter(sums, "cols", scatter_dimension=0, tiled=True)


def solution(mesh):
    few = mesh.shape["rows"] == mesh.shape["cols"] == ROWS
    in_specs = (
        P(("groups", "rows"), "cols"),
        P("groups", "cols"),
        P(("groups", "cols"), "rows"),
        P(("groups", "cols"), "rows"),
        P(("groups", "cols"), "rows"),
    )
    out_specs = P(("groups", "cols"), "rows")
    return jax.shard_map(
        local_few if few else local_many, mesh=mesh, in_specs=in_specs, out_specs=out_specs, check_vma=False
    )
```

```python
import functools

import jax
import jax.numpy as jnp
from jax import lax
from jax.experimental import pallas as pl
from jax.experimental.pallas import tpu as pltpu
from jax.sharding import PartitionSpec as P

TILE = 128
GROUP = 8
KEEP = 4
HEAD = 16
STEPS = 8

VMEM = pl.BlockSpec(memory_space=pltpu.VMEM)
HBM = pl.BlockSpec(memory_space=pltpu.HBM)
PARAMS = pltpu.CompilerParams(vmem_limit_bytes=8 * 1024 * 1024)
DIRECT = 48
PIECES = 4
ROWS = 4


def cost(flops):
    return pl.CostEstimate(flops=flops, bytes_accessed=1024, transcendentals=0)


def list_kept(kept, row, tiles, places):
    at = jnp.int32(0)
    for tile in range(tiles):
        places[at] = jnp.int32(tile)
        at = at + kept[row, tile]


def copies(source, target, sems):
    size = source.shape[0] // PIECES
    rows = [pl.ds(i * size, size) for i in range(PIECES)]
    return [pltpu.make_async_copy(source.at[r], target.at[r], sems.at[i]) for i, r in enumerate(rows)]


def pack_kernel(tiles, slots, kept, doubles, packed, first, second, table, block, places, sems):
    table_copy = pltpu.make_async_copy(kept, table, sems.at[PIECES])
    block_copies = copies(doubles, block, sems)
    table_copy.start()
    for copy in block_copies:
        copy.start()
    table_copy.wait()
    list_kept(table, lax.axis_index("rows"), tiles, places)
    cut, size = first.shape[0], block.shape[0] // PIECES
    tiles_kept = [pl.ds(pl.multiple_of(places[slot] * TILE, TILE), TILE) for slot in range(slots)]
    for i, copy in enumerate(block_copies):
        copy.wait()
        begin, end = i * size, (i + 1) * size
        for slot, tile in enumerate(tiles_kept):
            to = slice(slot * TILE, (slot + 1) * TILE)
            for target, low, high in ((packed, 0, block.shape[0]), (first, 0, cut), (second, cut, block.shape[0])):
                start, stop = max(begin, low), min(end, high)
                if start < stop:
                    target[start - low : stop - low, to] = block[start:stop, tile]


def prepare_kernel(tiles, slots, kept, int_kept, integrals, own, gathered, product, table, int_table, held, places, sems):
    started = copies(integrals, held, sems)
    for i, pair in enumerate(((kept, table), (int_kept, int_table)), PIECES):
        started.append(pltpu.make_async_copy(*pair, sems.at[i]))
    for copy in started:
        copy.start()
    for copy in started:
        copy.wait()
    row, col = lax.axis_index("rows"), lax.axis_index("cols")
    tiles_ab = integrals.shape[1] // TILE
    for n in range(ROWS):
        list_kept(table, col ^ n, tiles, places)
        for slot in range(slots):
            tile = places[slot]
            start = pl.multiple_of(tile * TILE, TILE)
            for ab in range(tiles_ab):
                part = held[pl.ds(start, TILE), ab * TILE : (ab + 1) * TILE]
                on = (int_table[ab, tile] != 0).astype(jnp.float32).astype(part.dtype)
                gathered[n, slot * TILE : (slot + 1) * TILE, ab * TILE : (ab + 1) * TILE] = part * on
    product[...] = jnp.dot(own[...], gathered[row ^ col], preferred_element_type=jnp.float32)


def encode(x, out):
    pairs, width = x.shape
    largest = jnp.max(jnp.abs(x), axis=0, keepdims=True)
    exponent = jnp.floor((14.95 - jnp.log2(jnp.maximum(largest, 1e-30))) * STEPS)
    code = jnp.round(x * jnp.exp2(exponent * (1.0 / STEPS))).astype(jnp.int32)
    bands = width // TILE
    each = HEAD // bands
    exponent = jnp.broadcast_to(exponent.astype(jnp.int32), (each, width))
    for band in range(bands):
        out[band * pairs : (band + 1) * pairs, :] = code[:, band * TILE : (band + 1) * TILE].astype(jnp.int16)
    head = jnp.concatenate([exponent[:, band * TILE : (band + 1) * TILE] for band in range(bands)], axis=0)
    out[bands * pairs :, :] = head.astype(jnp.int16)


def decode(message, pairs, start, stop):
    bands = (message.shape[0] - HEAD) // pairs
    each = HEAD // bands
    head = message[bands * pairs :, :].astype(jnp.int32).astype(jnp.float32)
    parts = []
    for band in range(bands):
        scale = jnp.exp2(head[band * each : band * each + 1, :] * (-1.0 / STEPS))
        code = message[band * pairs + start : band * pairs + stop, :]
        parts.append(code.astype(jnp.int32).astype(jnp.float32) * scale)
    return jnp.concatenate(parts, axis=1)


def place():
    return lax.axis_index("rows") ^ lax.axis_index("cols")


def far_steps(col):
    return 3 - col // 2, 2 + col // 2


def early_kernel(product, gathered, pair, near_second, far_first, sums):
    mine = place()
    cut = far_first.shape[0]
    sums[mine] = product[...]
    sums[mine ^ 1] = jnp.dot(pair[...], gathered[mine ^ 1], preferred_element_type=jnp.float32)
    for step, start, block in ((2, cut, near_second), (3, 0, far_first)):
        sums[mine ^ step, start : start + block.shape[0], :] = jnp.dot(
            block[...], gathered[mine ^ step], preferred_element_type=jnp.float32
        )


def whole(n, early, near_sums, far_sums, out):
    cut = near_sums.shape[0]
    step = place() ^ n
    out[...] = early[n]

    @pl.when(step == 2)
    def _():
        out[:cut, :] = near_sums[...]

    @pl.when(step == 3)
    def _():
        out[cut:, :] = far_sums[...]


def late_kernel(early, gathered, near_first, far_second, near_sums, far_sums, one_far, held):
    mine = place()
    near_sums[...] = jnp.dot(near_first[...], gathered[mine ^ 2], preferred_element_type=jnp.float32)
    far_sums[...] = jnp.dot(far_second[...], gathered[mine ^ 3], preferred_element_type=jnp.float32)
    whole(far_steps(lax.axis_index("cols"))[0], early, near_sums, far_sums, held)
    encode(held[...], one_far)


def rest_kernel(early, near_sums, far_sums, one, other_far, kept_sums, held):
    for n, out in ((far_steps(lax.axis_index("cols"))[1], other_far), (1, one)):
        whole(n, early, near_sums, far_sums, held)
        encode(held[...], out)
    whole(0, early, near_sums, far_sums, kept_sums)


def first_kernel(residual, kept_sums, one_far, out):
    pairs = out.shape[0]
    out[...] = residual[...] + kept_sums[...] + decode(one_far, pairs, 0, pairs)


def last_kernel(base, other_far, one, out, total, sems):
    pairs = total.shape[0]
    size = pairs // PIECES
    started = copies(total, out, sems)
    for i, copy in enumerate(started):
        rows = (i * size, (i + 1) * size)
        total[rows[0] : rows[1], :] = base[rows[0] : rows[1], :] + decode(other_far, pairs, *rows) + decode(one, pairs, *rows)
        copy.start()
    for copy in started:
        copy.wait()


def swap(x, axis, step):
    return lax.ppermute(x, axis, [(i, i ^ step) for i in range(ROWS)])


def local_few(doubles, doubles_kept, integrals, integral_kept, residual):
    pairs, cd_local = doubles.shape
    width = integrals.shape[1]
    tiles = cd_local // TILE
    slots = tiles // GROUP * KEEP
    places = pltpu.SMEM((tiles + 1,), jnp.int32)
    sums_shape = jax.ShapeDtypeStruct((pairs, width), jnp.float32)
    parts = (DIRECT, pairs - DIRECT)
    blocks = [jax.ShapeDtypeStruct((rows, slots * TILE), doubles.dtype) for rows in parts]
    message = jax.ShapeDtypeStruct((pairs * width // TILE + HEAD, TILE), jnp.int16)
    doubles, doubles_kept, integrals, integral_kept = (
        pltpu.with_memory_space_constraint(x, pltpu.HBM) for x in (doubles, doubles_kept, integrals, integral_kept.T)
    )
    packed, first, second = pl.pallas_call(
        functools.partial(pack_kernel, tiles, slots),
        out_shape=[jax.ShapeDtypeStruct((pairs, slots * TILE), doubles.dtype)] + blocks,
        in_specs=[HBM, HBM],
        out_specs=[VMEM] * 3,
        scratch_shapes=[
            pltpu.SMEM(doubles_kept.shape, jnp.int32),
            pltpu.VMEM(doubles.shape, doubles.dtype),
            places,
            pltpu.SemaphoreType.DMA((PIECES + 1,)),
        ],
        compiler_params=PARAMS,
        name="pack",
    )(doubles_kept, doubles)
    near_second = swap(second, "rows", 2)
    pair = swap(packed, "rows", 1)
    far_first = swap(first, "rows", 3)
    near_first = swap(first, "rows", 2)
    far_second = swap(near_second, "rows", 1)
    gathered, product = pl.pallas_call(
        functools.partial(prepare_kernel, tiles, slots),
        out_shape=[jax.ShapeDtypeStruct((ROWS, slots * TILE, width), integrals.dtype), sums_shape],
        in_specs=[HBM, HBM, HBM, VMEM],
        out_specs=[VMEM] * 2,
        scratch_shapes=[
            pltpu.SMEM(doubles_kept.shape, jnp.int32),
            pltpu.SMEM(integral_kept.shape, jnp.int32),
            pltpu.VMEM(integrals.shape, integrals.dtype),
            places,
            pltpu.SemaphoreType.DMA((PIECES + 2,)),
        ],
        compiler_params=PARAMS,
        cost_estimate=cost(115 * 10**7),
        name="prepare",
    )(doubles_kept, integral_kept, integrals, packed)

    def on_vmem(kernel, name, flops, out_shape, *args, scratch=()):
        return pl.pallas_call(
            kernel,
            out_shape=out_shape,
            in_specs=[VMEM] * len(args),
            out_specs=jax.tree.map(lambda _: VMEM, out_shape),
            scratch_shapes=scratch,
            compiler_params=PARAMS,
            cost_estimate=cost(flops),
            name=name,
        )(*args)

    held = [pltpu.VMEM((pairs, width), jnp.float32)]
    part_sums = [jax.ShapeDtypeStruct((rows, width), jnp.float32) for rows in parts]
    all_sums = jax.ShapeDtypeStruct((ROWS, pairs, width), jnp.float32)
    early = on_vmem(early_kernel, "early", 0, all_sums, product, gathered, pair, near_second, far_first)
    near_sums, far_sums, one_far = on_vmem(
        late_kernel, "late", 10**11, part_sums + [message], early, gathered, near_first, far_second, scratch=held
    )
    one, other_far, kept_sums = on_vmem(
        rest_kernel, "rest", 0, [message] * 2 + [sums_shape], early, near_sums, far_sums, scratch=held
    )
    one_far, other_far = (
        lax.ppermute(x, "cols", [(col, col ^ far_steps(col)[i]) for col in range(ROWS)])
        for i, x in enumerate((one_far, other_far))
    )
    one = swap(one, "cols", 1)
    base = on_vmem(first_kernel, "first", 0, sums_shape, residual, kept_sums, one_far)
    return pl.pallas_call(
        last_kernel,
        out_shape=sums_shape,
        in_specs=[VMEM] * 3,
        out_specs=HBM,
        scratch_shapes=[pltpu.VMEM((pairs, width), jnp.float32), pltpu.SemaphoreType.DMA((PIECES,))],
        compiler_params=PARAMS,
        cost_estimate=cost(0),
        name="last",
    )(base, other_far, one)


def local_many(doubles, doubles_kept, integrals, integral_kept, residual):
    pairs, cd_local = doubles.shape
    tiles = cd_local // TILE
    blocks = lax.all_gather(doubles, "rows", axis=0).reshape(-1, pairs, tiles, TILE)
    blocks = blocks * doubles_kept.astype(doubles.dtype)[:, None, :, None]
    tiles_ab = integrals.shape[1] // TILE
    masked = integrals.reshape(tiles, TILE, tiles_ab, TILE) * integral_kept.astype(integrals.dtype)[:, None, :, None]
    sums = jnp.dot(
        blocks.reshape(-1, cd_local), masked.reshape(integrals.shape), preferred_element_type=jnp.float32
    )
    return residual + lax.psum_scatter(sums, "cols", scatter_dimension=0, tiled=True)


def solution(mesh):
    few = mesh.shape["rows"] == mesh.shape["cols"] == ROWS
    in_specs = (
        P(("groups", "rows"), "cols"),
        P("groups", "cols"),
        P(("groups", "cols"), "rows"),
        P(("groups", "cols"), "rows"),
        P(("groups", "cols"), "rows"),
    )
    out_specs = P(("groups", "cols"), "rows")
    return jax.shard_map(
        local_few if few else local_many, mesh=mesh, in_specs=in_specs, out_specs=out_specs, check_vma=False
    )
```

```python
import functools

import jax
import jax.numpy as jnp
from jax import lax
from jax.experimental import pallas as pl
from jax.experimental.pallas import tpu as pltpu
from jax.sharding import PartitionSpec as P

TILE = 128
GROUP = 8
KEEP = 4
HEAD = 16
STEPS = 8

VMEM = pl.BlockSpec(memory_space=pltpu.VMEM)
HBM = pl.BlockSpec(memory_space=pltpu.HBM)
PARAMS = pltpu.CompilerParams(vmem_limit_bytes=8 * 1024 * 1024)
NEAR_LATE = 48
DIRECT = 64
PIECES = 4
ROWS = 4


def cost(flops):
    return pl.CostEstimate(flops=flops, bytes_accessed=1024, transcendentals=0)


def list_kept(kept, row, tiles, places):
    at = jnp.int32(0)
    for tile in range(tiles):
        places[at] = jnp.int32(tile)
        at = at + kept[row, tile]


def copies(source, target, sems):
    size = source.shape[0] // PIECES
    rows = [pl.ds(i * size, size) for i in range(PIECES)]
    return [pltpu.make_async_copy(source.at[r], target.at[r], sems.at[i]) for i, r in enumerate(rows)]


def pack_kernel(tiles, slots, kept, doubles, packed, direct, first, second, table, block, places, sems):
    table_copy = pltpu.make_async_copy(kept, table, sems.at[PIECES])
    block_copies = copies(doubles, block, sems)
    table_copy.start()
    for copy in block_copies:
        copy.start()
    table_copy.wait()
    list_kept(table, lax.axis_index("rows"), tiles, places)
    for copy in block_copies:
        copy.wait()
    cut = first.shape[0]
    for slot in range(slots):
        tile = block[:, pl.ds(pl.multiple_of(places[slot] * TILE, TILE), TILE)]
        to = slice(slot * TILE, (slot + 1) * TILE)
        packed[:, to] = tile
        direct[:, to] = tile[: direct.shape[0]]
        first[:, to] = tile[:cut]
        second[:, to] = tile[cut:]


def prepare_kernel(tiles, slots, kept, int_kept, integrals, own, gathered, product, table, int_table, held, places, sems):
    started = copies(integrals, held, sems)
    for i, pair in enumerate(((kept, table), (int_kept, int_table)), PIECES):
        started.append(pltpu.make_async_copy(*pair, sems.at[i]))
    for copy in started:
        copy.start()
    for copy in started:
        copy.wait()
    row, col = lax.axis_index("rows"), lax.axis_index("cols")
    tiles_ab = integrals.shape[1] // TILE
    for n in range(ROWS):
        list_kept(table, col ^ n, tiles, places)
        for slot in range(slots):
            tile = places[slot]
            start = pl.multiple_of(tile * TILE, TILE)
            for ab in range(tiles_ab):
                part = held[pl.ds(start, TILE), ab * TILE : (ab + 1) * TILE]
                on = (int_table[ab, tile] != 0).astype(jnp.float32).astype(part.dtype)
                gathered[n, slot * TILE : (slot + 1) * TILE, ab * TILE : (ab + 1) * TILE] = part * on
    product[...] = jnp.dot(own[...], gathered[row ^ col], preferred_element_type=jnp.float32)


def tail_kernel(x, out):
    out[...] = x[x.shape[0] - out.shape[0] :, :]


def encode(x, out):
    pairs, width = x.shape
    largest = jnp.max(jnp.abs(x), axis=0, keepdims=True)
    exponent = jnp.floor((14.95 - jnp.log2(jnp.maximum(largest, 1e-30))) * STEPS)
    code = jnp.round(x * jnp.exp2(exponent * (1.0 / STEPS))).astype(jnp.int32)
    bands = width // TILE
    each = HEAD // bands
    exponent = jnp.broadcast_to(exponent.astype(jnp.int32), (each, width))
    for band in range(bands):
        out[band * pairs : (band + 1) * pairs, :] = code[:, band * TILE : (band + 1) * TILE].astype(jnp.int16)
    head = jnp.concatenate([exponent[:, band * TILE : (band + 1) * TILE] for band in range(bands)], axis=0)
    out[bands * pairs :, :] = head.astype(jnp.int16)


def decode(message, pairs, start, stop):
    bands = (message.shape[0] - HEAD) // pairs
    each = HEAD // bands
    head = message[bands * pairs :, :].astype(jnp.int32).astype(jnp.float32)
    parts = []
    for band in range(bands):
        scale = jnp.exp2(head[band * each : band * each + 1, :] * (-1.0 / STEPS))
        code = message[band * pairs + start : band * pairs + stop, :]
        parts.append(code.astype(jnp.int32).astype(jnp.float32) * scale)
    return jnp.concatenate(parts, axis=1)


def place():
    return lax.axis_index("rows") ^ lax.axis_index("cols")


def far_steps(col):
    return 3 - col // 2, 2 + col // 2


def early_kernel(product, gathered, pair, near_second, far_first, sums):
    mine = place()
    cut = product.shape[0] - near_second.shape[0]
    sums[mine] = product[...]
    sums[mine ^ 1] = jnp.dot(pair[...], gathered[mine ^ 1], preferred_element_type=jnp.float32)
    for step, start, block in ((2, cut, near_second), (3, 0, far_first)):
        sums[mine ^ step, start : start + block.shape[0], :] = jnp.dot(
            block[...], gathered[mine ^ step], preferred_element_type=jnp.float32
        )


def whole(n, early, near_sums, far_sums, out):
    step = place() ^ n
    out[...] = early[n]

    @pl.when(step == 2)
    def _():
        out[: near_sums.shape[0], :] = near_sums[...]

    @pl.when(step == 3)
    def _():
        out[out.shape[0] - far_sums.shape[0] :, :] = far_sums[...]


def late_kernel(early, gathered, near_first, far_second, near_sums, far_sums, one_far, held):
    mine = place()
    near_sums[...] = jnp.dot(near_first[...], gathered[mine ^ 2], preferred_element_type=jnp.float32)
    far_sums[...] = jnp.dot(far_second[...], gathered[mine ^ 3], preferred_element_type=jnp.float32)
    whole(far_steps(lax.axis_index("cols"))[0], early, near_sums, far_sums, held)
    encode(held[...], one_far)


def rest_kernel(early, near_sums, far_sums, one, other_far, kept_sums, held):
    for n, out in ((far_steps(lax.axis_index("cols"))[1], other_far), (1, one)):
        whole(n, early, near_sums, far_sums, held)
        encode(held[...], out)
    whole(0, early, near_sums, far_sums, kept_sums)


def first_kernel(residual, kept_sums, one_far, out):
    pairs = out.shape[0]
    out[...] = residual[...] + kept_sums[...] + decode(one_far, pairs, 0, pairs)


def last_kernel(base, other_far, one, out, total, sems):
    pairs = total.shape[0]
    size = pairs // PIECES
    started = copies(total, out, sems)
    for i, copy in enumerate(started):
        rows = (i * size, (i + 1) * size)
        total[rows[0] : rows[1], :] = base[rows[0] : rows[1], :] + decode(other_far, pairs, *rows) + decode(one, pairs, *rows)
        copy.start()
    for copy in started:
        copy.wait()


def swap(x, axis, step):
    return lax.ppermute(x, axis, [(i, i ^ step) for i in range(ROWS)])


def local_few(doubles, doubles_kept, integrals, integral_kept, residual):
    pairs, cd_local = doubles.shape
    width = integrals.shape[1]
    tiles = cd_local // TILE
    slots = tiles // GROUP * KEEP
    places = pltpu.SMEM((tiles + 1,), jnp.int32)
    sums_shape = jax.ShapeDtypeStruct((pairs, width), jnp.float32)
    blocks = [
        jax.ShapeDtypeStruct((rows, slots * TILE), doubles.dtype) for rows in (DIRECT, NEAR_LATE, pairs - NEAR_LATE)
    ]
    message = jax.ShapeDtypeStruct((pairs * width // TILE + HEAD, TILE), jnp.int16)
    doubles, doubles_kept, integrals, integral_kept = (
        pltpu.with_memory_space_constraint(x, pltpu.HBM) for x in (doubles, doubles_kept, integrals, integral_kept.T)
    )
    packed, direct, first, second = pl.pallas_call(
        functools.partial(pack_kernel, tiles, slots),
        out_shape=[jax.ShapeDtypeStruct((pairs, slots * TILE), doubles.dtype)] + blocks,
        in_specs=[HBM, HBM],
        out_specs=[VMEM] * 4,
        scratch_shapes=[
            pltpu.SMEM(doubles_kept.shape, jnp.int32),
            pltpu.VMEM(doubles.shape, doubles.dtype),
            places,
            pltpu.SemaphoreType.DMA((PIECES + 1,)),
        ],
        compiler_params=PARAMS,
        name="pack",
    )(doubles_kept, doubles)
    near_second = swap(second, "rows", 2)
    pair = swap(packed, "rows", 1)
    far_first = swap(direct, "rows", 3)
    near_first = swap(first, "rows", 2)
    handed_on = pl.pallas_call(
        tail_kernel,
        out_shape=jax.ShapeDtypeStruct((pairs - DIRECT, slots * TILE), doubles.dtype),
        in_specs=[VMEM],
        out_specs=VMEM,
        compiler_params=PARAMS,
        cost_estimate=cost(0),
        name="tail",
    )(near_second)
    far_second = swap(handed_on, "rows", 1)
    gathered, product = pl.pallas_call(
        functools.partial(prepare_kernel, tiles, slots),
        out_shape=[jax.ShapeDtypeStruct((ROWS, slots * TILE, width), integrals.dtype), sums_shape],
        in_specs=[HBM, HBM, HBM, VMEM],
        out_specs=[VMEM] * 2,
        scratch_shapes=[
            pltpu.SMEM(doubles_kept.shape, jnp.int32),
            pltpu.SMEM(integral_kept.shape, jnp.int32),
            pltpu.VMEM(integrals.shape, integrals.dtype),
            places,
            pltpu.SemaphoreType.DMA((PIECES + 2,)),
        ],
        compiler_params=PARAMS,
        cost_estimate=cost(115 * 10**7),
        name="prepare",
    )(doubles_kept, integral_kept, integrals, packed)

    def on_vmem(kernel, name, flops, out_shape, *args, scratch=()):
        return pl.pallas_call(
            kernel,
            out_shape=out_shape,
            in_specs=[VMEM] * len(args),
            out_specs=jax.tree.map(lambda _: VMEM, out_shape),
            scratch_shapes=scratch,
            compiler_params=PARAMS,
            cost_estimate=cost(flops),
            name=name,
        )(*args)

    held = [pltpu.VMEM((pairs, width), jnp.float32)]
    part_sums = [jax.ShapeDtypeStruct((rows, width), jnp.float32) for rows in (NEAR_LATE, pairs - DIRECT)]
    all_sums = jax.ShapeDtypeStruct((ROWS, pairs, width), jnp.float32)
    early = on_vmem(early_kernel, "early", 0, all_sums, product, gathered, pair, near_second, far_first)
    near_sums, far_sums, one_far = on_vmem(
        late_kernel, "late", 10**11, part_sums + [message], early, gathered, near_first, far_second, scratch=held
    )
    one, other_far, kept_sums = on_vmem(
        rest_kernel, "rest", 0, [message] * 2 + [sums_shape], early, near_sums, far_sums, scratch=held
    )
    one_far, other_far = (
        lax.ppermute(x, "cols", [(col, col ^ far_steps(col)[i]) for col in range(ROWS)])
        for i, x in enumerate((one_far, other_far))
    )
    one = swap(one, "cols", 1)
    base = on_vmem(first_kernel, "first", 0, sums_shape, residual, kept_sums, one_far)
    return pl.pallas_call(
        last_kernel,
        out_shape=sums_shape,
        in_specs=[VMEM] * 3,
        out_specs=HBM,
        scratch_shapes=[pltpu.VMEM((pairs, width), jnp.float32), pltpu.SemaphoreType.DMA((PIECES,))],
        compiler_params=PARAMS,
        cost_estimate=cost(0),
        name="last",
    )(base, other_far, one)


def local_many(doubles, doubles_kept, integrals, integral_kept, residual):
    pairs, cd_local = doubles.shape
    tiles = cd_local // TILE
    blocks = lax.all_gather(doubles, "rows", axis=0).reshape(-1, pairs, tiles, TILE)
    blocks = blocks * doubles_kept.astype(doubles.dtype)[:, None, :, None]
    tiles_ab = integrals.shape[1] // TILE
    masked = integrals.reshape(tiles, TILE, tiles_ab, TILE) * integral_kept.astype(integrals.dtype)[:, None, :, None]
    sums = jnp.dot(
        blocks.reshape(-1, cd_local), masked.reshape(integrals.shape), preferred_element_type=jnp.float32
    )
    return residual + lax.psum_scatter(sums, "cols", scatter_dimension=0, tiled=True)


def solution(mesh):
    few = mesh.shape["rows"] == mesh.shape["cols"] == ROWS
    in_specs = (
        P(("groups", "rows"), "cols"),
        P("groups", "cols"),
        P(("groups", "cols"), "rows"),
        P(("groups", "cols"), "rows"),
        P(("groups", "cols"), "rows"),
    )
    out_specs = P(("groups", "cols"), "rows")
    return jax.shard_map(
        local_few if few else local_many, mesh=mesh, in_specs=in_specs, out_specs=out_specs, check_vma=False
    )
```

```python
import functools

import jax
import jax.numpy as jnp
from jax import lax
from jax.experimental import pallas as pl
from jax.experimental.pallas import tpu as pltpu
from jax.sharding import PartitionSpec as P

TILE = 128
GROUP = 8
KEEP = 4
HEAD = 16
STEPS = 8

VMEM = pl.BlockSpec(memory_space=pltpu.VMEM)
HBM = pl.BlockSpec(memory_space=pltpu.HBM)
PARAMS = pltpu.CompilerParams(vmem_limit_bytes=8 * 1024 * 1024)
DIRECT = 48
PIECES = 4
ROWS = 4


def cost(flops):
    return pl.CostEstimate(flops=flops, bytes_accessed=1024, transcendentals=0)


def list_kept(kept, row, tiles, places):
    at = jnp.int32(0)
    for tile in range(tiles):
        places[at] = jnp.int32(tile)
        at = at + kept[row, tile]


def copies(source, target, sems):
    size = source.shape[0] // PIECES
    rows = [pl.ds(i * size, size) for i in range(PIECES)]
    return [pltpu.make_async_copy(source.at[r], target.at[r], sems.at[i]) for i, r in enumerate(rows)]


def pack_kernel(tiles, slots, kept, doubles, packed, first, second, table, block, places, sems):
    table_copy = pltpu.make_async_copy(kept, table, sems.at[PIECES])
    block_copies = copies(doubles, block, sems)
    table_copy.start()
    for copy in block_copies:
        copy.start()
    table_copy.wait()
    list_kept(table, lax.axis_index("rows"), tiles, places)
    for copy in block_copies:
        copy.wait()
    cut = first.shape[0]
    for slot in range(slots):
        tile = block[:, pl.ds(pl.multiple_of(places[slot] * TILE, TILE), TILE)]
        to = slice(slot * TILE, (slot + 1) * TILE)
        packed[:, to] = tile
        first[:, to] = tile[:cut]
        second[:, to] = tile[cut:]


def prepare_kernel(tiles, slots, kept, int_kept, integrals, own, gathered, product, table, int_table, held, places, sems):
    started = copies(integrals, held, sems)
    for i, pair in enumerate(((kept, table), (int_kept, int_table)), PIECES):
        started.append(pltpu.make_async_copy(*pair, sems.at[i]))
    for copy in started:
        copy.start()
    for copy in started:
        copy.wait()
    row, col = lax.axis_index("rows"), lax.axis_index("cols")
    tiles_ab = integrals.shape[1] // TILE
    for n in range(ROWS):
        list_kept(table, col ^ n, tiles, places)
        for slot in range(slots):
            tile = places[slot]
            start = pl.multiple_of(tile * TILE, TILE)
            for ab in range(tiles_ab):
                part = held[pl.ds(start, TILE), ab * TILE : (ab + 1) * TILE]
                on = (int_table[ab, tile] != 0).astype(jnp.float32).astype(part.dtype)
                gathered[n, slot * TILE : (slot + 1) * TILE, ab * TILE : (ab + 1) * TILE] = part * on
    product[...] = jnp.dot(own[...], gathered[row ^ col], preferred_element_type=jnp.float32)


def encode(x, out):
    pairs, width = x.shape
    largest = jnp.max(jnp.abs(x), axis=0, keepdims=True)
    exponent = jnp.floor((14.95 - jnp.log2(jnp.maximum(largest, 1e-30))) * STEPS)
    code = jnp.round(x * jnp.exp2(exponent * (1.0 / STEPS))).astype(jnp.int32)
    bands = width // TILE
    each = HEAD // bands
    exponent = jnp.broadcast_to(exponent.astype(jnp.int32), (each, width))
    for band in range(bands):
        out[band * pairs : (band + 1) * pairs, :] = code[:, band * TILE : (band + 1) * TILE].astype(jnp.int16)
    head = jnp.concatenate([exponent[:, band * TILE : (band + 1) * TILE] for band in range(bands)], axis=0)
    out[bands * pairs :, :] = head.astype(jnp.int16)


def decode(message, pairs, start, stop):
    bands = (message.shape[0] - HEAD) // pairs
    each = HEAD // bands
    head = message[bands * pairs :, :].astype(jnp.int32).astype(jnp.float32)
    parts = []
    for band in range(bands):
        scale = jnp.exp2(head[band * each : band * each + 1, :] * (-1.0 / STEPS))
        code = message[band * pairs + start : band * pairs + stop, :]
        parts.append(code.astype(jnp.int32).astype(jnp.float32) * scale)
    return jnp.concatenate(parts, axis=1)


def place():
    return lax.axis_index("rows") ^ lax.axis_index("cols")


def near_step(col):
    return 3 - col % 2


def chip_steps(row, col):
    odd = row % 2
    own = row // 2 == col // 2
    first = own * (3 - odd) + (1 - own) * (2 + odd)
    return first, 5 - first


def steps_here():
    row, col = lax.axis_index("rows"), lax.axis_index("cols")
    odd = row % 2
    first = jnp.where(row // 2 == col // 2, 3 - odd, 2 + odd)
    return first, 5 - first


def early_kernel(product, gathered, pair, near_second, far_first, near_first, sums, one_far):
    mine = place()
    near = near_step(lax.axis_index("cols"))
    cut = far_first.shape[0]
    sums[mine] = product[...]
    sums[mine ^ 1] = jnp.dot(pair[...], gathered[mine ^ 1], preferred_element_type=jnp.float32)
    for step, start, block in ((near, cut, near_second), (5 - near, 0, far_first), (near, 0, near_first)):
        sums[mine ^ step, start : start + block.shape[0], :] = jnp.dot(
            block[...], gathered[mine ^ step], preferred_element_type=jnp.float32
        )
    encode(sums[steps_here()[0]], one_far)


def whole(n, early, far_sums, out):
    out[...] = early[n]

    @pl.when((place() ^ n) == 5 - near_step(lax.axis_index("cols")))
    def _():
        out[out.shape[0] - far_sums.shape[0] :, :] = far_sums[...]


def late_kernel(early, gathered, far_second, far_sums, other_far, held):
    far = 5 - near_step(lax.axis_index("cols"))
    far_sums[...] = jnp.dot(far_second[...], gathered[place() ^ far], preferred_element_type=jnp.float32)
    whole(steps_here()[1], early, far_sums, held)
    encode(held[...], other_far)


def rest_kernel(early, far_sums, one, kept_sums, held):
    whole(1, early, far_sums, held)
    encode(held[...], one)
    whole(0, early, far_sums, kept_sums)


def first_kernel(residual, kept_sums, one_far, out):
    pairs = out.shape[0]
    out[...] = residual[...] + kept_sums[...] + decode(one_far, pairs, 0, pairs)


def last_kernel(base, other_far, one, out, total, sems):
    pairs = total.shape[0]
    size = pairs // PIECES
    started = copies(total, out, sems)
    for i, copy in enumerate(started):
        rows = (i * size, (i + 1) * size)
        total[rows[0] : rows[1], :] = base[rows[0] : rows[1], :] + decode(other_far, pairs, *rows) + decode(one, pairs, *rows)
        copy.start()
    for copy in started:
        copy.wait()


def swap(x, axis, step):
    return lax.ppermute(x, axis, [(i, i ^ step) for i in range(ROWS)])


def permute(x, target):
    pairs = [(r * ROWS + c, target(r, c)) for r in range(ROWS) for c in range(ROWS)]
    return lax.ppermute(x, ("rows", "cols"), [(i, r * ROWS + c) for i, (r, c) in pairs])


def step_rows(x, step):
    return permute(x, lambda row, col: (row ^ step(col), col))


def local_few(doubles, doubles_kept, integrals, integral_kept, residual):
    pairs, cd_local = doubles.shape
    width = integrals.shape[1]
    tiles = cd_local // TILE
    slots = tiles // GROUP * KEEP
    places = pltpu.SMEM((tiles + 1,), jnp.int32)
    sums_shape = jax.ShapeDtypeStruct((pairs, width), jnp.float32)
    parts = (DIRECT, pairs - DIRECT)
    blocks = [jax.ShapeDtypeStruct((rows, slots * TILE), doubles.dtype) for rows in parts]
    message = jax.ShapeDtypeStruct((pairs * width // TILE + HEAD, TILE), jnp.int16)
    doubles, doubles_kept, integrals, integral_kept = (
        pltpu.with_memory_space_constraint(x, pltpu.HBM) for x in (doubles, doubles_kept, integrals, integral_kept.T)
    )
    packed, first, second = pl.pallas_call(
        functools.partial(pack_kernel, tiles, slots),
        out_shape=[jax.ShapeDtypeStruct((pairs, slots * TILE), doubles.dtype)] + blocks,
        in_specs=[HBM, HBM],
        out_specs=[VMEM] * 3,
        scratch_shapes=[
            pltpu.SMEM(doubles_kept.shape, jnp.int32),
            pltpu.VMEM(doubles.shape, doubles.dtype),
            places,
            pltpu.SemaphoreType.DMA((PIECES + 1,)),
        ],
        compiler_params=PARAMS,
        name="pack",
    )(doubles_kept, doubles)
    near_second = step_rows(second, near_step)
    pair = swap(packed, "rows", 1)
    far_first = step_rows(first, lambda col: 5 - near_step(col))
    near_first = step_rows(first, near_step)
    far_second = swap(near_second, "rows", 1)
    gathered, product = pl.pallas_call(
        functools.partial(prepare_kernel, tiles, slots),
        out_shape=[jax.ShapeDtypeStruct((ROWS, slots * TILE, width), integrals.dtype), sums_shape],
        in_specs=[HBM, HBM, HBM, VMEM],
        out_specs=[VMEM] * 2,
        scratch_shapes=[
            pltpu.SMEM(doubles_kept.shape, jnp.int32),
            pltpu.SMEM(integral_kept.shape, jnp.int32),
            pltpu.VMEM(integrals.shape, integrals.dtype),
            places,
            pltpu.SemaphoreType.DMA((PIECES + 2,)),
        ],
        compiler_params=PARAMS,
        cost_estimate=cost(115 * 10**7),
        name="prepare",
    )(doubles_kept, integral_kept, integrals, packed)

    def on_vmem(kernel, name, flops, out_shape, *args, scratch=()):
        return pl.pallas_call(
            kernel,
            out_shape=out_shape,
            in_specs=[VMEM] * len(args),
            out_specs=jax.tree.map(lambda _: VMEM, out_shape),
            scratch_shapes=scratch,
            compiler_params=PARAMS,
            cost_estimate=cost(flops),
            name=name,
        )(*args)

    held = [pltpu.VMEM((pairs, width), jnp.float32)]
    late_sums = jax.ShapeDtypeStruct((parts[1], width), jnp.float32)
    all_sums = jax.ShapeDtypeStruct((ROWS, pairs, width), jnp.float32)
    early, one_far = on_vmem(
        early_kernel,
        "early",
        0,
        [all_sums, message],
        product,
        gathered,
        pair,
        near_second,
        far_first,
        near_first,
    )
    one_far = permute(one_far, lambda row, col: (row, col ^ chip_steps(row, col)[0]))
    far_sums, other_far = on_vmem(
        late_kernel, "late", 10**11, [late_sums, message], early, gathered, far_second, scratch=held
    )
    other_far = permute(other_far, lambda row, col: (row, col ^ chip_steps(row, col)[1]))
    one, kept_sums = on_vmem(rest_kernel, "rest", 0, [message, sums_shape], early, far_sums, scratch=held)
    one = swap(one, "cols", 1)
    base = on_vmem(first_kernel, "first", 0, sums_shape, residual, kept_sums, one_far)
    return pl.pallas_call(
        last_kernel,
        out_shape=sums_shape,
        in_specs=[VMEM] * 3,
        out_specs=HBM,
        scratch_shapes=[pltpu.VMEM((pairs, width), jnp.float32), pltpu.SemaphoreType.DMA((PIECES,))],
        compiler_params=PARAMS,
        cost_estimate=cost(0),
        name="last",
    )(base, other_far, one)


def local_many(doubles, doubles_kept, integrals, integral_kept, residual):
    pairs, cd_local = doubles.shape
    tiles = cd_local // TILE
    blocks = lax.all_gather(doubles, "rows", axis=0).reshape(-1, pairs, tiles, TILE)
    blocks = blocks * doubles_kept.astype(doubles.dtype)[:, None, :, None]
    tiles_ab = integrals.shape[1] // TILE
    masked = integrals.reshape(tiles, TILE, tiles_ab, TILE) * integral_kept.astype(integrals.dtype)[:, None, :, None]
    sums = jnp.dot(
        blocks.reshape(-1, cd_local), masked.reshape(integrals.shape), preferred_element_type=jnp.float32
    )
    return residual + lax.psum_scatter(sums, "cols", scatter_dimension=0, tiled=True)


def solution(mesh):
    few = mesh.shape["rows"] == mesh.shape["cols"] == ROWS
    in_specs = (
        P(("groups", "rows"), "cols"),
        P("groups", "cols"),
        P(("groups", "cols"), "rows"),
        P(("groups", "cols"), "rows"),
        P(("groups", "cols"), "rows"),
    )
    out_specs = P(("groups", "cols"), "rows")
    return jax.shard_map(
        local_few if few else local_many, mesh=mesh, in_specs=in_specs, out_specs=out_specs, check_vma=False
    )
```

```python
import functools

import jax
import jax.numpy as jnp
from jax import lax
from jax.experimental import pallas as pl
from jax.experimental.pallas import tpu as pltpu
from jax.sharding import PartitionSpec as P

TILE = 128
GROUP = 8
KEEP = 4
HEAD = 16
STEPS = 8

VMEM = pl.BlockSpec(memory_space=pltpu.VMEM)
HBM = pl.BlockSpec(memory_space=pltpu.HBM)
PARAMS = pltpu.CompilerParams(vmem_limit_bytes=8 * 1024 * 1024)
DIRECT = 48
PIECES = 4
ROWS = 4


def cost(flops):
    return pl.CostEstimate(flops=flops, bytes_accessed=1024, transcendentals=0)


def list_kept(kept, row, tiles, places):
    at = jnp.int32(0)
    for tile in range(tiles):
        places[at] = jnp.int32(tile)
        at = at + kept[row, tile]


def copies(source, target, sems):
    size = source.shape[0] // PIECES
    rows = [pl.ds(i * size, size) for i in range(PIECES)]
    return [pltpu.make_async_copy(source.at[r], target.at[r], sems.at[i]) for i, r in enumerate(rows)]


def pack_kernel(tiles, slots, kept, doubles, packed, first, second, table, block, places, sems):
    table_copy = pltpu.make_async_copy(kept, table, sems.at[PIECES])
    block_copies = copies(doubles, block, sems)
    table_copy.start()
    for copy in block_copies:
        copy.start()
    table_copy.wait()
    list_kept(table, lax.axis_index("rows"), tiles, places)
    for copy in block_copies:
        copy.wait()
    cut = first.shape[0]
    for slot in range(slots):
        tile = block[:, pl.ds(pl.multiple_of(places[slot] * TILE, TILE), TILE)]
        to = slice(slot * TILE, (slot + 1) * TILE)
        packed[:, to] = tile
        first[:, to] = tile[:cut]
        second[:, to] = tile[cut:]


def prepare_kernel(tiles, slots, kept, int_kept, integrals, own, gathered, product, table, int_table, held, places, sems):
    started = copies(integrals, held, sems)
    for i, pair in enumerate(((kept, table), (int_kept, int_table)), PIECES):
        started.append(pltpu.make_async_copy(*pair, sems.at[i]))
    for copy in started:
        copy.start()
    for copy in started:
        copy.wait()
    row, col = lax.axis_index("rows"), lax.axis_index("cols")
    tiles_ab = integrals.shape[1] // TILE
    for n in range(ROWS):
        list_kept(table, col ^ n, tiles, places)
        for slot in range(slots):
            tile = places[slot]
            start = pl.multiple_of(tile * TILE, TILE)
            for ab in range(tiles_ab):
                part = held[pl.ds(start, TILE), ab * TILE : (ab + 1) * TILE]
                on = (int_table[ab, tile] != 0).astype(jnp.float32).astype(part.dtype)
                gathered[n, slot * TILE : (slot + 1) * TILE, ab * TILE : (ab + 1) * TILE] = part * on
    product[...] = jnp.dot(own[...], gathered[row ^ col], preferred_element_type=jnp.float32)


def encode(x, out):
    pairs, width = x.shape
    largest = jnp.max(jnp.abs(x), axis=0, keepdims=True)
    exponent = jnp.floor((14.95 - jnp.log2(jnp.maximum(largest, 1e-30))) * STEPS)
    code = jnp.round(x * jnp.exp2(exponent * (1.0 / STEPS))).astype(jnp.int32)
    bands = width // TILE
    each = HEAD // bands
    exponent = jnp.broadcast_to(exponent.astype(jnp.int32), (each, width))
    for band in range(bands):
        out[band * pairs : (band + 1) * pairs, :] = code[:, band * TILE : (band + 1) * TILE].astype(jnp.int16)
    head = jnp.concatenate([exponent[:, band * TILE : (band + 1) * TILE] for band in range(bands)], axis=0)
    out[bands * pairs :, :] = head.astype(jnp.int16)


def decode(message, pairs, start, stop):
    bands = (message.shape[0] - HEAD) // pairs
    each = HEAD // bands
    head = message[bands * pairs :, :].astype(jnp.int32).astype(jnp.float32)
    parts = []
    for band in range(bands):
        scale = jnp.exp2(head[band * each : band * each + 1, :] * (-1.0 / STEPS))
        code = message[band * pairs + start : band * pairs + stop, :]
        parts.append(code.astype(jnp.int32).astype(jnp.float32) * scale)
    return jnp.concatenate(parts, axis=1)


def place():
    return lax.axis_index("rows") ^ lax.axis_index("cols")


def near_step(col):
    return 3 - col % 2


def chip_steps(row, col):
    odd = row % 2
    own = row // 2 == col // 2
    first = own * (3 - odd) + (1 - own) * (2 + odd)
    return first, 5 - first


def steps_here():
    row, col = lax.axis_index("rows"), lax.axis_index("cols")
    odd = row % 2
    first = jnp.where(row // 2 == col // 2, 3 - odd, 2 + odd)
    return first, 5 - first


def early_kernel(product, gathered, pair, near_second, far_first, near_first, sums, one_far):
    mine = place()
    near = near_step(lax.axis_index("cols"))
    cut = far_first.shape[0]
    sums[mine] = product[...]
    sums[mine ^ 1] = jnp.dot(pair[...], gathered[mine ^ 1], preferred_element_type=jnp.float32)
    for step, start, block in ((near, cut, near_second), (5 - near, 0, far_first), (near, 0, near_first)):
        sums[mine ^ step, start : start + block.shape[0], :] = jnp.dot(
            block[...], gathered[mine ^ step], preferred_element_type=jnp.float32
        )
    encode(sums[steps_here()[0]], one_far)


def whole(n, early, far_sums, out):
    out[...] = early[n]

    @pl.when((place() ^ n) == 5 - near_step(lax.axis_index("cols")))
    def _():
        out[out.shape[0] - far_sums.shape[0] :, :] = far_sums[...]


def late_kernel(early, gathered, far_second, far_sums):
    far = 5 - near_step(lax.axis_index("cols"))
    far_sums[...] = jnp.dot(far_second[...], gathered[place() ^ far], preferred_element_type=jnp.float32)


def rest_kernel(early, far_sums, other_far, one, kept_sums, held):
    whole(steps_here()[1], early, far_sums, held)
    encode(held[...], other_far)
    whole(1, early, far_sums, held)
    encode(held[...], one)
    whole(0, early, far_sums, kept_sums)


def first_kernel(residual, kept_sums, one_far, out):
    pairs = out.shape[0]
    out[...] = residual[...] + kept_sums[...] + decode(one_far, pairs, 0, pairs)


def last_kernel(base, other_far, one, out, total, sems):
    pairs = total.shape[0]
    size = pairs // PIECES
    started = copies(total, out, sems)
    for i, copy in enumerate(started):
        rows = (i * size, (i + 1) * size)
        total[rows[0] : rows[1], :] = base[rows[0] : rows[1], :] + decode(other_far, pairs, *rows) + decode(one, pairs, *rows)
        copy.start()
    for copy in started:
        copy.wait()


def swap(x, axis, step):
    return lax.ppermute(x, axis, [(i, i ^ step) for i in range(ROWS)])


def permute(x, target):
    pairs = [(r * ROWS + c, target(r, c)) for r in range(ROWS) for c in range(ROWS)]
    return lax.ppermute(x, ("rows", "cols"), [(i, r * ROWS + c) for i, (r, c) in pairs])


def step_rows(x, step):
    return permute(x, lambda row, col: (row ^ step(col), col))


def local_few(doubles, doubles_kept, integrals, integral_kept, residual):
    pairs, cd_local = doubles.shape
    width = integrals.shape[1]
    tiles = cd_local // TILE
    slots = tiles // GROUP * KEEP
    places = pltpu.SMEM((tiles + 1,), jnp.int32)
    sums_shape = jax.ShapeDtypeStruct((pairs, width), jnp.float32)
    parts = (DIRECT, pairs - DIRECT)
    blocks = [jax.ShapeDtypeStruct((rows, slots * TILE), doubles.dtype) for rows in parts]
    message = jax.ShapeDtypeStruct((pairs * width // TILE + HEAD, TILE), jnp.int16)
    doubles, doubles_kept, integrals, integral_kept = (
        pltpu.with_memory_space_constraint(x, pltpu.HBM) for x in (doubles, doubles_kept, integrals, integral_kept.T)
    )
    packed, first, second = pl.pallas_call(
        functools.partial(pack_kernel, tiles, slots),
        out_shape=[jax.ShapeDtypeStruct((pairs, slots * TILE), doubles.dtype)] + blocks,
        in_specs=[HBM, HBM],
        out_specs=[VMEM] * 3,
        scratch_shapes=[
            pltpu.SMEM(doubles_kept.shape, jnp.int32),
            pltpu.VMEM(doubles.shape, doubles.dtype),
            places,
            pltpu.SemaphoreType.DMA((PIECES + 1,)),
        ],
        compiler_params=PARAMS,
        name="pack",
    )(doubles_kept, doubles)
    near_second = step_rows(second, near_step)
    pair = swap(packed, "rows", 1)
    far_first = step_rows(first, lambda col: 5 - near_step(col))
    near_first = step_rows(first, near_step)
    far_second = swap(near_second, "rows", 1)
    gathered, product = pl.pallas_call(
        functools.partial(prepare_kernel, tiles, slots),
        out_shape=[jax.ShapeDtypeStruct((ROWS, slots * TILE, width), integrals.dtype), sums_shape],
        in_specs=[HBM, HBM, HBM, VMEM],
        out_specs=[VMEM] * 2,
        scratch_shapes=[
            pltpu.SMEM(doubles_kept.shape, jnp.int32),
            pltpu.SMEM(integral_kept.shape, jnp.int32),
            pltpu.VMEM(integrals.shape, integrals.dtype),
            places,
            pltpu.SemaphoreType.DMA((PIECES + 2,)),
        ],
        compiler_params=PARAMS,
        cost_estimate=cost(115 * 10**7),
        name="prepare",
    )(doubles_kept, integral_kept, integrals, packed)

    def on_vmem(kernel, name, flops, out_shape, *args, scratch=()):
        return pl.pallas_call(
            kernel,
            out_shape=out_shape,
            in_specs=[VMEM] * len(args),
            out_specs=jax.tree.map(lambda _: VMEM, out_shape),
            scratch_shapes=scratch,
            compiler_params=PARAMS,
            cost_estimate=cost(flops),
            name=name,
        )(*args)

    held = [pltpu.VMEM((pairs, width), jnp.float32)]
    late_sums = jax.ShapeDtypeStruct((parts[1], width), jnp.float32)
    all_sums = jax.ShapeDtypeStruct((ROWS, pairs, width), jnp.float32)
    early, one_far = on_vmem(
        early_kernel,
        "early",
        0,
        [all_sums, message],
        product,
        gathered,
        pair,
        near_second,
        far_first,
        near_first,
    )
    one_far = permute(one_far, lambda row, col: (row, col ^ chip_steps(row, col)[0]))
    far_sums = on_vmem(late_kernel, "late", 10**11, late_sums, early, gathered, far_second)
    other_far, one, kept_sums = on_vmem(
        rest_kernel, "rest", 0, [message] * 2 + [sums_shape], early, far_sums, scratch=held
    )
    other_far = permute(other_far, lambda row, col: (row, col ^ chip_steps(row, col)[1]))
    one = swap(one, "cols", 1)
    base = on_vmem(first_kernel, "first", 0, sums_shape, residual, kept_sums, one_far)
    return pl.pallas_call(
        last_kernel,
        out_shape=sums_shape,
        in_specs=[VMEM] * 3,
        out_specs=HBM,
        scratch_shapes=[pltpu.VMEM((pairs, width), jnp.float32), pltpu.SemaphoreType.DMA((PIECES,))],
        compiler_params=PARAMS,
        cost_estimate=cost(0),
        name="last",
    )(base, other_far, one)


def local_many(doubles, doubles_kept, integrals, integral_kept, residual):
    pairs, cd_local = doubles.shape
    tiles = cd_local // TILE
    blocks = lax.all_gather(doubles, "rows", axis=0).reshape(-1, pairs, tiles, TILE)
    blocks = blocks * doubles_kept.astype(doubles.dtype)[:, None, :, None]
    tiles_ab = integrals.shape[1] // TILE
    masked = integrals.reshape(tiles, TILE, tiles_ab, TILE) * integral_kept.astype(integrals.dtype)[:, None, :, None]
    sums = jnp.dot(
        blocks.reshape(-1, cd_local), masked.reshape(integrals.shape), preferred_element_type=jnp.float32
    )
    return residual + lax.psum_scatter(sums, "cols", scatter_dimension=0, tiled=True)


def solution(mesh):
    few = mesh.shape["rows"] == mesh.shape["cols"] == ROWS
    in_specs = (
        P(("groups", "rows"), "cols"),
        P("groups", "cols"),
        P(("groups", "cols"), "rows"),
        P(("groups", "cols"), "rows"),
        P(("groups", "cols"), "rows"),
    )
    out_specs = P(("groups", "cols"), "rows")
    return jax.shard_map(
        local_few if few else local_many, mesh=mesh, in_specs=in_specs, out_specs=out_specs, check_vma=False
    )
```

```python
import functools

import jax
import jax.numpy as jnp
from jax import lax
from jax.experimental import pallas as pl
from jax.experimental.pallas import tpu as pltpu
from jax.sharding import PartitionSpec as P

TILE = 128
GROUP = 8
KEEP = 4
HEAD = 16
STEPS = 8

VMEM = pl.BlockSpec(memory_space=pltpu.VMEM)
HBM = pl.BlockSpec(memory_space=pltpu.HBM)
PARAMS = pltpu.CompilerParams(vmem_limit_bytes=8 * 1024 * 1024)
DIRECT = 48
PIECES = 4
ROWS = 4


def cost(flops):
    return pl.CostEstimate(flops=flops, bytes_accessed=1024, transcendentals=0)


def list_kept(kept, row, tiles, places):
    at = jnp.int32(0)
    for tile in range(tiles):
        places[at] = jnp.int32(tile)
        at = at + kept[row, tile]


def copies(source, target, sems):
    size = source.shape[0] // PIECES
    rows = [pl.ds(i * size, size) for i in range(PIECES)]
    return [pltpu.make_async_copy(source.at[r], target.at[r], sems.at[i]) for i, r in enumerate(rows)]


def pack_kernel(tiles, slots, kept, doubles, packed, first, second, table, block, places, sems):
    table_copy = pltpu.make_async_copy(kept, table, sems.at[PIECES])
    block_copies = copies(doubles, block, sems)
    table_copy.start()
    for copy in block_copies:
        copy.start()
    table_copy.wait()
    list_kept(table, lax.axis_index("rows"), tiles, places)
    for copy in block_copies:
        copy.wait()
    cut = first.shape[0]
    for slot in range(slots):
        tile = block[:, pl.ds(pl.multiple_of(places[slot] * TILE, TILE), TILE)]
        to = slice(slot * TILE, (slot + 1) * TILE)
        packed[:, to] = tile
        first[:, to] = tile[:cut]
        second[:, to] = tile[cut:]


def prepare_kernel(tiles, slots, kept, int_kept, integrals, own, gathered, product, table, int_table, held, places, sems):
    started = copies(integrals, held, sems)
    for i, pair in enumerate(((kept, table), (int_kept, int_table)), PIECES):
        started.append(pltpu.make_async_copy(*pair, sems.at[i]))
    for copy in started:
        copy.start()
    for copy in started:
        copy.wait()
    row, col = lax.axis_index("rows"), lax.axis_index("cols")
    tiles_ab = integrals.shape[1] // TILE
    for n in range(ROWS):
        list_kept(table, col ^ n, tiles, places)
        for slot in range(slots):
            tile = places[slot]
            start = pl.multiple_of(tile * TILE, TILE)
            for ab in range(tiles_ab):
                part = held[pl.ds(start, TILE), ab * TILE : (ab + 1) * TILE]
                on = (int_table[ab, tile] != 0).astype(jnp.float32).astype(part.dtype)
                gathered[n, slot * TILE : (slot + 1) * TILE, ab * TILE : (ab + 1) * TILE] = part * on
    product[...] = jnp.dot(own[...], gathered[row ^ col], preferred_element_type=jnp.float32)


def encode(x, out):
    pairs, width = x.shape
    largest = jnp.max(jnp.abs(x), axis=0, keepdims=True)
    exponent = jnp.floor((14.95 - jnp.log2(jnp.maximum(largest, 1e-30))) * STEPS)
    code = jnp.round(x * jnp.exp2(exponent * (1.0 / STEPS))).astype(jnp.int32)
    bands = width // TILE
    each = HEAD // bands
    exponent = jnp.broadcast_to(exponent.astype(jnp.int32), (each, width))
    for band in range(bands):
        out[band * pairs : (band + 1) * pairs, :] = code[:, band * TILE : (band + 1) * TILE].astype(jnp.int16)
    head = jnp.concatenate([exponent[:, band * TILE : (band + 1) * TILE] for band in range(bands)], axis=0)
    out[bands * pairs :, :] = head.astype(jnp.int16)


def decode(message, pairs, start, stop):
    bands = (message.shape[0] - HEAD) // pairs
    each = HEAD // bands
    head = message[bands * pairs :, :].astype(jnp.int32).astype(jnp.float32)
    parts = []
    for band in range(bands):
        scale = jnp.exp2(head[band * each : band * each + 1, :] * (-1.0 / STEPS))
        code = message[band * pairs + start : band * pairs + stop, :]
        parts.append(code.astype(jnp.int32).astype(jnp.float32) * scale)
    return jnp.concatenate(parts, axis=1)


def place():
    return lax.axis_index("rows") ^ lax.axis_index("cols")


def near_step(col):
    return 3 - col % 2


def chip_steps(row, col):
    odd = row % 2
    first = 3 - odd
    return first, 5 - first


def steps_here():
    row, col = lax.axis_index("rows"), lax.axis_index("cols")
    odd = row % 2
    first = 3 - odd
    return first, 5 - first


def early_kernel(product, gathered, pair, near_second, far_first, near_first, sums, one_far):
    mine = place()
    near = near_step(lax.axis_index("cols"))
    cut = far_first.shape[0]
    sums[mine] = product[...]
    sums[mine ^ 1] = jnp.dot(pair[...], gathered[mine ^ 1], preferred_element_type=jnp.float32)
    for step, start, block in ((near, cut, near_second), (5 - near, 0, far_first), (near, 0, near_first)):
        sums[mine ^ step, start : start + block.shape[0], :] = jnp.dot(
            block[...], gathered[mine ^ step], preferred_element_type=jnp.float32
        )
    encode(sums[steps_here()[0]], one_far)


def whole(n, early, far_sums, out):
    out[...] = early[n]

    @pl.when((place() ^ n) == 5 - near_step(lax.axis_index("cols")))
    def _():
        out[out.shape[0] - far_sums.shape[0] :, :] = far_sums[...]


def late_kernel(early, gathered, far_second, far_sums):
    far = 5 - near_step(lax.axis_index("cols"))
    far_sums[...] = jnp.dot(far_second[...], gathered[place() ^ far], preferred_element_type=jnp.float32)


def rest_kernel(early, far_sums, other_far, one, kept_sums, held):
    whole(steps_here()[1], early, far_sums, held)
    encode(held[...], other_far)
    whole(1, early, far_sums, held)
    encode(held[...], one)
    whole(0, early, far_sums, kept_sums)


def first_kernel(residual, kept_sums, one_far, out):
    pairs = out.shape[0]
    out[...] = residual[...] + kept_sums[...] + decode(one_far, pairs, 0, pairs)


def last_kernel(base, other_far, one, out, total, sems):
    pairs = total.shape[0]
    size = pairs // PIECES
    started = copies(total, out, sems)
    for i, copy in enumerate(started):
        rows = (i * size, (i + 1) * size)
        total[rows[0] : rows[1], :] = base[rows[0] : rows[1], :] + decode(other_far, pairs, *rows) + decode(one, pairs, *rows)
        copy.start()
    for copy in started:
        copy.wait()


def swap(x, axis, step):
    return lax.ppermute(x, axis, [(i, i ^ step) for i in range(ROWS)])


def permute(x, target):
    pairs = [(r * ROWS + c, target(r, c)) for r in range(ROWS) for c in range(ROWS)]
    return lax.ppermute(x, ("rows", "cols"), [(i, r * ROWS + c) for i, (r, c) in pairs])


def step_rows(x, step):
    return permute(x, lambda row, col: (row ^ step(col), col))


def local_few(doubles, doubles_kept, integrals, integral_kept, residual):
    pairs, cd_local = doubles.shape
    width = integrals.shape[1]
    tiles = cd_local // TILE
    slots = tiles // GROUP * KEEP
    places = pltpu.SMEM((tiles + 1,), jnp.int32)
    sums_shape = jax.ShapeDtypeStruct((pairs, width), jnp.float32)
    parts = (DIRECT, pairs - DIRECT)
    blocks = [jax.ShapeDtypeStruct((rows, slots * TILE), doubles.dtype) for rows in parts]
    message = jax.ShapeDtypeStruct((pairs * width // TILE + HEAD, TILE), jnp.int16)
    doubles, doubles_kept, integrals, integral_kept = (
        pltpu.with_memory_space_constraint(x, pltpu.HBM) for x in (doubles, doubles_kept, integrals, integral_kept.T)
    )
    packed, first, second = pl.pallas_call(
        functools.partial(pack_kernel, tiles, slots),
        out_shape=[jax.ShapeDtypeStruct((pairs, slots * TILE), doubles.dtype)] + blocks,
        in_specs=[HBM, HBM],
        out_specs=[VMEM] * 3,
        scratch_shapes=[
            pltpu.SMEM(doubles_kept.shape, jnp.int32),
            pltpu.VMEM(doubles.shape, doubles.dtype),
            places,
            pltpu.SemaphoreType.DMA((PIECES + 1,)),
        ],
        compiler_params=PARAMS,
        name="pack",
    )(doubles_kept, doubles)
    near_second = step_rows(second, near_step)
    pair = swap(packed, "rows", 1)
    far_first = step_rows(first, lambda col: 5 - near_step(col))
    near_first = step_rows(first, near_step)
    far_second = swap(near_second, "rows", 1)
    gathered, product = pl.pallas_call(
        functools.partial(prepare_kernel, tiles, slots),
        out_shape=[jax.ShapeDtypeStruct((ROWS, slots * TILE, width), integrals.dtype), sums_shape],
        in_specs=[HBM, HBM, HBM, VMEM],
        out_specs=[VMEM] * 2,
        scratch_shapes=[
            pltpu.SMEM(doubles_kept.shape, jnp.int32),
            pltpu.SMEM(integral_kept.shape, jnp.int32),
            pltpu.VMEM(integrals.shape, integrals.dtype),
            places,
            pltpu.SemaphoreType.DMA((PIECES + 2,)),
        ],
        compiler_params=PARAMS,
        cost_estimate=cost(115 * 10**7),
        name="prepare",
    )(doubles_kept, integral_kept, integrals, packed)

    def on_vmem(kernel, name, flops, out_shape, *args, scratch=()):
        return pl.pallas_call(
            kernel,
            out_shape=out_shape,
            in_specs=[VMEM] * len(args),
            out_specs=jax.tree.map(lambda _: VMEM, out_shape),
            scratch_shapes=scratch,
            compiler_params=PARAMS,
            cost_estimate=cost(flops),
            name=name,
        )(*args)

    held = [pltpu.VMEM((pairs, width), jnp.float32)]
    late_sums = jax.ShapeDtypeStruct((parts[1], width), jnp.float32)
    all_sums = jax.ShapeDtypeStruct((ROWS, pairs, width), jnp.float32)
    early, one_far = on_vmem(
        early_kernel,
        "early",
        0,
        [all_sums, message],
        product,
        gathered,
        pair,
        near_second,
        far_first,
        near_first,
    )
    one_far = permute(one_far, lambda row, col: (row, col ^ chip_steps(row, col)[0]))
    far_sums = on_vmem(late_kernel, "late", 10**11, late_sums, early, gathered, far_second)
    other_far, one, kept_sums = on_vmem(
        rest_kernel, "rest", 0, [message] * 2 + [sums_shape], early, far_sums, scratch=held
    )
    other_far = permute(other_far, lambda row, col: (row, col ^ chip_steps(row, col)[1]))
    one = swap(one, "cols", 1)
    base = on_vmem(first_kernel, "first", 0, sums_shape, residual, kept_sums, one_far)
    return pl.pallas_call(
        last_kernel,
        out_shape=sums_shape,
        in_specs=[VMEM] * 3,
        out_specs=HBM,
        scratch_shapes=[pltpu.VMEM((pairs, width), jnp.float32), pltpu.SemaphoreType.DMA((PIECES,))],
        compiler_params=PARAMS,
        cost_estimate=cost(0),
        name="last",
    )(base, other_far, one)


def local_many(doubles, doubles_kept, integrals, integral_kept, residual):
    pairs, cd_local = doubles.shape
    tiles = cd_local // TILE
    blocks = lax.all_gather(doubles, "rows", axis=0).reshape(-1, pairs, tiles, TILE)
    blocks = blocks * doubles_kept.astype(doubles.dtype)[:, None, :, None]
    tiles_ab = integrals.shape[1] // TILE
    masked = integrals.reshape(tiles, TILE, tiles_ab, TILE) * integral_kept.astype(integrals.dtype)[:, None, :, None]
    sums = jnp.dot(
        blocks.reshape(-1, cd_local), masked.reshape(integrals.shape), preferred_element_type=jnp.float32
    )
    return residual + lax.psum_scatter(sums, "cols", scatter_dimension=0, tiled=True)


def solution(mesh):
    few = mesh.shape["rows"] == mesh.shape["cols"] == ROWS
    in_specs = (
        P(("groups", "rows"), "cols"),
        P("groups", "cols"),
        P(("groups", "cols"), "rows"),
        P(("groups", "cols"), "rows"),
        P(("groups", "cols"), "rows"),
    )
    out_specs = P(("groups", "cols"), "rows")
    return jax.shard_map(
        local_few if few else local_many, mesh=mesh, in_specs=in_specs, out_specs=out_specs, check_vma=False
    )
```

```python
import functools

import jax
import jax.numpy as jnp
from jax import lax
from jax.experimental import pallas as pl
from jax.experimental.pallas import tpu as pltpu
from jax.sharding import PartitionSpec as P

TILE = 128
GROUP = 8
KEEP = 4
HEAD = 16
STEPS = 8

VMEM = pl.BlockSpec(memory_space=pltpu.VMEM)
HBM = pl.BlockSpec(memory_space=pltpu.HBM)
PARAMS = pltpu.CompilerParams(vmem_limit_bytes=8 * 1024 * 1024)
DIRECT = 32
PIECES = 4
ROWS = 4


def cost(flops):
    return pl.CostEstimate(flops=flops, bytes_accessed=1024, transcendentals=0)


def list_kept(kept, row, tiles, places):
    at = jnp.int32(0)
    for tile in range(tiles):
        places[at] = jnp.int32(tile)
        at = at + kept[row, tile]


def copies(source, target, sems):
    size = source.shape[0] // PIECES
    rows = [pl.ds(i * size, size) for i in range(PIECES)]
    return [pltpu.make_async_copy(source.at[r], target.at[r], sems.at[i]) for i, r in enumerate(rows)]


def pack_kernel(tiles, slots, kept, doubles, packed, first, second, table, block, places, sems):
    table_copy = pltpu.make_async_copy(kept, table, sems.at[PIECES])
    block_copies = copies(doubles, block, sems)
    table_copy.start()
    for copy in block_copies:
        copy.start()
    table_copy.wait()
    list_kept(table, lax.axis_index("rows"), tiles, places)
    for copy in block_copies:
        copy.wait()
    cut = first.shape[0]
    for slot in range(slots):
        tile = block[:, pl.ds(pl.multiple_of(places[slot] * TILE, TILE), TILE)]
        to = slice(slot * TILE, (slot + 1) * TILE)
        packed[:, to] = tile
        first[:, to] = tile[:cut]
        second[:, to] = tile[cut:]


def prepare_kernel(tiles, slots, kept, int_kept, integrals, own, gathered, product, table, int_table, held, places, sems):
    started = copies(integrals, held, sems)
    for i, pair in enumerate(((kept, table), (int_kept, int_table)), PIECES):
        started.append(pltpu.make_async_copy(*pair, sems.at[i]))
    for copy in started:
        copy.start()
    for copy in started:
        copy.wait()
    row, col = lax.axis_index("rows"), lax.axis_index("cols")
    tiles_ab = integrals.shape[1] // TILE
    for n in range(ROWS):
        list_kept(table, col ^ n, tiles, places)
        for slot in range(slots):
            tile = places[slot]
            start = pl.multiple_of(tile * TILE, TILE)
            for ab in range(tiles_ab):
                part = held[pl.ds(start, TILE), ab * TILE : (ab + 1) * TILE]
                on = (int_table[ab, tile] != 0).astype(jnp.float32).astype(part.dtype)
                gathered[n, slot * TILE : (slot + 1) * TILE, ab * TILE : (ab + 1) * TILE] = part * on
    product[...] = jnp.dot(own[...], gathered[row ^ col], preferred_element_type=jnp.float32)


def encode(x, out):
    pairs, width = x.shape
    largest = jnp.max(jnp.abs(x), axis=0, keepdims=True)
    exponent = jnp.floor((14.95 - jnp.log2(jnp.maximum(largest, 1e-30))) * STEPS)
    code = jnp.round(x * jnp.exp2(exponent * (1.0 / STEPS))).astype(jnp.int32)
    bands = width // TILE
    each = HEAD // bands
    exponent = jnp.broadcast_to(exponent.astype(jnp.int32), (each, width))
    for band in range(bands):
        out[band * pairs : (band + 1) * pairs, :] = code[:, band * TILE : (band + 1) * TILE].astype(jnp.int16)
    head = jnp.concatenate([exponent[:, band * TILE : (band + 1) * TILE] for band in range(bands)], axis=0)
    out[bands * pairs :, :] = head.astype(jnp.int16)


def decode(message, pairs, start, stop):
    bands = (message.shape[0] - HEAD) // pairs
    each = HEAD // bands
    head = message[bands * pairs :, :].astype(jnp.int32).astype(jnp.float32)
    parts = []
    for band in range(bands):
        scale = jnp.exp2(head[band * each : band * each + 1, :] * (-1.0 / STEPS))
        code = message[band * pairs + start : band * pairs + stop, :]
        parts.append(code.astype(jnp.int32).astype(jnp.float32) * scale)
    return jnp.concatenate(parts, axis=1)


def place():
    return lax.axis_index("rows") ^ lax.axis_index("cols")


def near_step(col):
    return 3 - col % 2


def chip_steps(row, col):
    odd = row % 2
    own = row // 2 == col // 2
    first = own * (3 - odd) + (1 - own) * (2 + odd)
    return first, 5 - first


def steps_here():
    row, col = lax.axis_index("rows"), lax.axis_index("cols")
    odd = row % 2
    first = jnp.where(row // 2 == col // 2, 3 - odd, 2 + odd)
    return first, 5 - first


def early_kernel(product, gathered, pair, near_second, far_first, near_first, sums, one_far):
    mine = place()
    near = near_step(lax.axis_index("cols"))
    cut = far_first.shape[0]
    sums[mine] = product[...]
    sums[mine ^ 1] = jnp.dot(pair[...], gathered[mine ^ 1], preferred_element_type=jnp.float32)
    for step, start, block in ((near, cut, near_second), (5 - near, 0, far_first), (near, 0, near_first)):
        sums[mine ^ step, start : start + block.shape[0], :] = jnp.dot(
            block[...], gathered[mine ^ step], preferred_element_type=jnp.float32
        )
    encode(sums[steps_here()[0]], one_far)


def whole(n, early, far_sums, out):
    out[...] = early[n]

    @pl.when((place() ^ n) == 5 - near_step(lax.axis_index("cols")))
    def _():
        out[out.shape[0] - far_sums.shape[0] :, :] = far_sums[...]


def late_kernel(early, gathered, far_second, far_sums):
    far = 5 - near_step(lax.axis_index("cols"))
    far_sums[...] = jnp.dot(far_second[...], gathered[place() ^ far], preferred_element_type=jnp.float32)


def rest_kernel(early, far_sums, other_far, one, kept_sums, held):
    whole(steps_here()[1], early, far_sums, held)
    encode(held[...], other_far)
    whole(1, early, far_sums, held)
    encode(held[...], one)
    whole(0, early, far_sums, kept_sums)


def first_kernel(residual, kept_sums, one_far, out):
    pairs = out.shape[0]
    out[...] = residual[...] + kept_sums[...] + decode(one_far, pairs, 0, pairs)


def last_kernel(base, other_far, one, out, total, sems):
    pairs = total.shape[0]
    size = pairs // PIECES
    started = copies(total, out, sems)
    for i, copy in enumerate(started):
        rows = (i * size, (i + 1) * size)
        total[rows[0] : rows[1], :] = base[rows[0] : rows[1], :] + decode(other_far, pairs, *rows) + decode(one, pairs, *rows)
        copy.start()
    for copy in started:
        copy.wait()


def swap(x, axis, step):
    return lax.ppermute(x, axis, [(i, i ^ step) for i in range(ROWS)])


def permute(x, target):
    pairs = [(r * ROWS + c, target(r, c)) for r in range(ROWS) for c in range(ROWS)]
    return lax.ppermute(x, ("rows", "cols"), [(i, r * ROWS + c) for i, (r, c) in pairs])


def step_rows(x, step):
    return permute(x, lambda row, col: (row ^ step(col), col))


def local_few(doubles, doubles_kept, integrals, integral_kept, residual):
    pairs, cd_local = doubles.shape
    width = integrals.shape[1]
    tiles = cd_local // TILE
    slots = tiles // GROUP * KEEP
    places = pltpu.SMEM((tiles + 1,), jnp.int32)
    sums_shape = jax.ShapeDtypeStruct((pairs, width), jnp.float32)
    parts = (DIRECT, pairs - DIRECT)
    blocks = [jax.ShapeDtypeStruct((rows, slots * TILE), doubles.dtype) for rows in parts]
    message = jax.ShapeDtypeStruct((pairs * width // TILE + HEAD, TILE), jnp.int16)
    doubles, doubles_kept, integrals, integral_kept = (
        pltpu.with_memory_space_constraint(x, pltpu.HBM) for x in (doubles, doubles_kept, integrals, integral_kept.T)
    )
    packed, first, second = pl.pallas_call(
        functools.partial(pack_kernel, tiles, slots),
        out_shape=[jax.ShapeDtypeStruct((pairs, slots * TILE), doubles.dtype)] + blocks,
        in_specs=[HBM, HBM],
        out_specs=[VMEM] * 3,
        scratch_shapes=[
            pltpu.SMEM(doubles_kept.shape, jnp.int32),
            pltpu.VMEM(doubles.shape, doubles.dtype),
            places,
            pltpu.SemaphoreType.DMA((PIECES + 1,)),
        ],
        compiler_params=PARAMS,
        name="pack",
    )(doubles_kept, doubles)
    near_second = step_rows(second, near_step)
    pair = swap(packed, "rows", 1)
    far_first = step_rows(first, lambda col: 5 - near_step(col))
    near_first = step_rows(first, near_step)
    far_second = swap(near_second, "rows", 1)
    gathered, product = pl.pallas_call(
        functools.partial(prepare_kernel, tiles, slots),
        out_shape=[jax.ShapeDtypeStruct((ROWS, slots * TILE, width), integrals.dtype), sums_shape],
        in_specs=[HBM, HBM, HBM, VMEM],
        out_specs=[VMEM] * 2,
        scratch_shapes=[
            pltpu.SMEM(doubles_kept.shape, jnp.int32),
            pltpu.SMEM(integral_kept.shape, jnp.int32),
            pltpu.VMEM(integrals.shape, integrals.dtype),
            places,
            pltpu.SemaphoreType.DMA((PIECES + 2,)),
        ],
        compiler_params=PARAMS,
        cost_estimate=cost(115 * 10**7),
        name="prepare",
    )(doubles_kept, integral_kept, integrals, packed)

    def on_vmem(kernel, name, flops, out_shape, *args, scratch=()):
        return pl.pallas_call(
            kernel,
            out_shape=out_shape,
            in_specs=[VMEM] * len(args),
            out_specs=jax.tree.map(lambda _: VMEM, out_shape),
            scratch_shapes=scratch,
            compiler_params=PARAMS,
            cost_estimate=cost(flops),
            name=name,
        )(*args)

    held = [pltpu.VMEM((pairs, width), jnp.float32)]
    late_sums = jax.ShapeDtypeStruct((parts[1], width), jnp.float32)
    all_sums = jax.ShapeDtypeStruct((ROWS, pairs, width), jnp.float32)
    early, one_far = on_vmem(
        early_kernel,
        "early",
        0,
        [all_sums, message],
        product,
        gathered,
        pair,
        near_second,
        far_first,
        near_first,
    )
    one_far = permute(one_far, lambda row, col: (row, col ^ chip_steps(row, col)[0]))
    far_sums = on_vmem(late_kernel, "late", 10**11, late_sums, early, gathered, far_second)
    other_far, one, kept_sums = on_vmem(
        rest_kernel, "rest", 0, [message] * 2 + [sums_shape], early, far_sums, scratch=held
    )
    other_far = permute(other_far, lambda row, col: (row, col ^ chip_steps(row, col)[1]))
    one = swap(one, "cols", 1)
    base = on_vmem(first_kernel, "first", 0, sums_shape, residual, kept_sums, one_far)
    return pl.pallas_call(
        last_kernel,
        out_shape=sums_shape,
        in_specs=[VMEM] * 3,
        out_specs=HBM,
        scratch_shapes=[pltpu.VMEM((pairs, width), jnp.float32), pltpu.SemaphoreType.DMA((PIECES,))],
        compiler_params=PARAMS,
        cost_estimate=cost(0),
        name="last",
    )(base, other_far, one)


def local_many(doubles, doubles_kept, integrals, integral_kept, residual):
    pairs, cd_local = doubles.shape
    tiles = cd_local // TILE
    blocks = lax.all_gather(doubles, "rows", axis=0).reshape(-1, pairs, tiles, TILE)
    blocks = blocks * doubles_kept.astype(doubles.dtype)[:, None, :, None]
    tiles_ab = integrals.shape[1] // TILE
    masked = integrals.reshape(tiles, TILE, tiles_ab, TILE) * integral_kept.astype(integrals.dtype)[:, None, :, None]
    sums = jnp.dot(
        blocks.reshape(-1, cd_local), masked.reshape(integrals.shape), preferred_element_type=jnp.float32
    )
    return residual + lax.psum_scatter(sums, "cols", scatter_dimension=0, tiled=True)


def solution(mesh):
    few = mesh.shape["rows"] == mesh.shape["cols"] == ROWS
    in_specs = (
        P(("groups", "rows"), "cols"),
        P("groups", "cols"),
        P(("groups", "cols"), "rows"),
        P(("groups", "cols"), "rows"),
        P(("groups", "cols"), "rows"),
    )
    out_specs = P(("groups", "cols"), "rows")
    return jax.shard_map(
        local_few if few else local_many, mesh=mesh, in_specs=in_specs, out_specs=out_specs, check_vma=False
    )
```
